256 devices in a mesh: grp: 4 (over z_hi), ta: 16 (over y, x), gz: 4 (over z_lo, core).
Axes of the slice: x: 4, y: 4, z: 8 (z_hi: 4, z_lo: 2; z = z_hi * 2 + z_lo), core: 2. Of those that a mesh axis runs over, the one named last changes fastest.
Arguments:
- source_field: float32 [2, 4, 3, 16, 32, 8, 128], P(None, None, None, 'grp', 'ta', 'gz'), may hold values from -6 to 6
- gauge_links: float32 [4, 2, 3, 3, 16, 32, 8, 8], P(None, None, None, None, 'grp', 'ta', 'gz'), may hold values from -2.5 to 2.5
- null_vectors: float32 [2, 4, 3, 16, 32, 8, 192], P(None, None, None, 'grp', 'ta', 'gz'), may hold values from -0.625 to 0.625
- coarse_links: float32 [5, 2, 24, 24, 4, 16, 4, 2], P(None, None, None, None, 'grp', 'ta', 'gz'), may hold values from -1 to 1
Outputs:
- solution_field: float32 [2, 4, 3, 16, 32, 8, 128], P(None, None, None, 'grp', 'ta', 'gz')
- coarse_solution: float32 [2, 24, 4, 4, 16, 4, 2], P(None, None, None, 'grp', 'ta', 'gz')
The draws below stay inside these ranges and needn't reach their ends.
All inputs are finite; a program needn't handle non-finite values.
Results may differ from the reference program's by a relative error of at most 0.0003.
Values sent between devices are 32-bit elements; how exact they have to be, the bound alone decides.
A program may use at most 192 MiB of HBM per device.

```python
import math
import jax
import jax.numpy as jnp
from jax import lax

CY = 8
LS = 16
LSC = 4
NVEC = 24
BX = 4
BY = 4
BT = 2
BZ = 2
DEG = 4
CITERS = 4
NX = 16
NT = 32
NZ = 8
NXB = 4
NTB = 16
NZB = 4
NYB = 2


def draw_coarse_links(key, part):
    key = jax.random.fold_in(key, 7)
    slice_key = jax.random.fold_in(key, 1)
    entry_key = jax.random.fold_in(key, 2)
    spread = 2.0 / math.sqrt(4.0 * NVEC)
    slice_scale = jnp.exp(jax.random.uniform(slice_key, (NTB,), jnp.float32, math.log(0.25), math.log(2.0)))
    full_shape = (5, 2, NVEC, NVEC, NXB, NTB, NZB, NYB)
    base = jax.random.normal(entry_key, full_shape, jnp.float32)
    values = base * spread * slice_scale[None, None, None, None, None, :, None, None]
    return jnp.clip(values, -1.0, 1.0)


def shard_levels(own_key, shape, split, smallest, top_value):
    def one(dim, parts):
        heights = jax.random.uniform(jax.random.fold_in(jax.random.fold_in(own_key, 6), dim), (parts,), jnp.float32, smallest / len(split), top_value / len(split))
        return jnp.repeat(jnp.exp(heights), shape[dim] // parts).reshape((-1,) + (1,) * (len(shape) - dim - 1))

    gain = one(*split[0])
    for cut in split[1:]:
        gain = gain * one(*cut)
    return gain


def centred(stream_key, dims, width, bound, shards=(), held_as=jnp.bfloat16):
    level = shard_levels(stream_key, dims, shards, -0.22, 0.18) if shards else 1.0
    values = jax.random.normal(stream_key, dims, jnp.float32) * width * level
    return jnp.minimum(jnp.maximum(values, -bound), bound).astype(held_as)


def setup_inputs(seed: int = 0) -> dict:
    seeds = jax.random.split(jax.random.key(seed), 5)
    return {
        "source_field": centred(seeds[0], (2, 4, 3, NX, NT, NZ, LS * CY), 1.0, 6.0, ((3, 4), (4, 16), (5, 4)), jnp.float32),
        "gauge_links": centred(seeds[1], (4, 2, 3, 3, NX, NT, NZ, CY), 6 ** -0.5, 2.5, ((4, 4), (5, 16), (6, 4)), jnp.float32),
        "null_vectors": centred(seeds[2], (2, 4, 3, NX, NT, NZ, NVEC * CY), (12 * BX * BY * BT * BZ // 8) ** -0.5, 0.625, ((3, 4), (4, 16), (5, 4)), jnp.float32),
        "coarse_links": draw_coarse_links(jax.random.fold_in(seeds[4], 71), 0),
    }


site_mass = 2.0
hop_kappa = 0.1
fifth_hop = 0.4
wall_mass = 0.1
cheb_lower = 0.6
cheb_upper = 3.4
coarse_mass = 3.0
coarse_fifth = 0.3

gamma_table = (
    ((3, 0.0, 1.0), (2, 0.0, 1.0), (1, 0.0, -1.0), (0, 0.0, -1.0)),
    ((3, -1.0, 0.0), (2, 1.0, 0.0), (1, 1.0, 0.0), (0, -1.0, 0.0)),
    ((2, 0.0, 1.0), (3, 0.0, -1.0), (0, 0.0, -1.0), (1, 0.0, 1.0)),
    ((2, 1.0, 0.0), (3, 1.0, 0.0), (0, 1.0, 0.0), (1, 1.0, 0.0)),
)


def contract(pattern, left, right):
    return jnp.einsum(pattern, left, right, precision=lax.Precision.HIGHEST)


def tile_layers(array, layers):
    return jnp.tile(array, (1,) * (array.ndim - 1) + (layers,))


def spin_project(values, direction, factor):
    real_rows = []
    imag_rows = []
    for row in range(4):
        column, gamma_real, gamma_imag = gamma_table[direction][row]
        other_real = gamma_real * values[0, column] - gamma_imag * values[1, column]
        other_imag = gamma_real * values[1, column] + gamma_imag * values[0, column]
        real_rows.append(values[0, row] + factor * other_real)
        imag_rows.append(values[1, row] + factor * other_imag)
    return jnp.stack([jnp.stack(real_rows), jnp.stack(imag_rows)])


def shifted_inner(values, offset, period):
    last_width = values.shape[-1]
    position = lax.broadcasted_iota(jnp.int32, (last_width,), 0) % period
    if offset == 1:
        return jnp.where(position == period - 1, jnp.roll(values, period - 1, -1), jnp.roll(values, -1, -1))
    return jnp.where(position == 0, jnp.roll(values, 1 - period, -1), jnp.roll(values, 1, -1))


def link_times(matrix, values, dagger):
    real_link, imag_link = matrix[0], matrix[1]
    if dagger:
        real_link = jnp.swapaxes(real_link, 0, 1)
        imag_link = -jnp.swapaxes(imag_link, 0, 1)
    out_real = jnp.zeros(values[0].shape, values.dtype)
    out_imag = jnp.zeros(values[0].shape, values.dtype)
    for column in range(3):
        left_real = real_link[:, column][None]
        left_imag = imag_link[:, column][None]
        right_real = values[0][:, column][:, None]
        right_imag = values[1][:, column][:, None]
        out_real = out_real + left_real * right_real - left_imag * right_imag
        out_imag = out_imag + left_real * right_imag + left_imag * right_real
    return jnp.stack([out_real, out_imag])


def fifth_term(values, period):
    last_width = values.shape[-1]
    layer_count = last_width // period
    layer_index = lax.broadcasted_iota(jnp.int32, (last_width,), 0) // period
    from_below = jnp.roll(values, period, -1) * jnp.where(layer_index == 0, -wall_mass, 1.0)
    from_above = jnp.roll(values, -period, -1) * jnp.where(layer_index == layer_count - 1, -wall_mass, 1.0)
    return jnp.concatenate([from_below[:, :2], from_above[:, 2:]], axis=1)


def fine_apply(values, present, lowered, forward, backward, period):
    hopping = link_times(present[1], spin_project(shifted_inner(values, 1, period), 1, -1.0), False)
    hopping = hopping + link_times(shifted_inner(present[1], -1, period),
                                   spin_project(shifted_inner(values, -1, period), 1, 1.0), True)
    for position, direction in enumerate((0, 2, 3)):
        hopping = hopping + link_times(present[direction], spin_project(forward[position], direction, -1.0), False)
        hopping = hopping + link_times(lowered[position], spin_project(backward[position], direction, 1.0), True)
    return site_mass * values - hop_kappa * hopping - fifth_hop * fifth_term(values, period)


def chebyshev(operator, initial, source, from_zero):
    centre = 0.5 * (cheb_upper + cheb_lower)
    half_width = 0.5 * (cheb_upper - cheb_lower)
    spread_ratio = centre / half_width
    ratio_now = 1.0 / spread_ratio
    remain = source if from_zero else source - operator(initial)
    update = remain / centre
    result = initial + update
    for sweep_index in range(DEG - 1):
        remain = remain - operator(update)
        ratio_next = 1.0 / (2.0 * spread_ratio - ratio_now)
        update = (ratio_next * ratio_now) * update + (2.0 * ratio_next / half_width) * remain
        result = result + update
        ratio_now = ratio_next
    return result


def block_shape(array_shape, blocks):
    block_x, block_t, block_z = blocks
    return (4, 3, array_shape[3] // block_x, block_x, array_shape[4] // block_t, block_t, array_shape[5] // block_z, block_z)


def restrict(residual, vectors, blocks, block_y, coarse_layers, period):
    layers = residual.shape[-1] // period
    vector_count = vectors.shape[-1] // period
    summed = residual.reshape(residual.shape[:-1] + (coarse_layers, layers // coarse_layers, period)).sum(axis=7)
    lead_shape = block_shape(residual.shape, blocks)
    res_blocks = summed.reshape((2,) + lead_shape + (coarse_layers, period // block_y, block_y))
    vec_blocks = vectors.reshape((2,) + lead_shape + (vector_count, period // block_y, block_y))
    pattern = "abxitjzlsym,abxitjzlkym->ksxtzy"
    real_part = contract(pattern, res_blocks[0], vec_blocks[0]) + contract(pattern, res_blocks[1], vec_blocks[1])
    imag_part = contract(pattern, res_blocks[1], vec_blocks[0]) - contract(pattern, res_blocks[0], vec_blocks[1])
    return jnp.stack([real_part, imag_part])


def prolong(coarse, vectors, blocks, block_y, layers, period):
    vector_count = vectors.shape[-1] // period
    coarse_layers = coarse.shape[2]
    lead_shape = block_shape(vectors.shape, blocks)
    vec_blocks = vectors.reshape((2,) + lead_shape + (vector_count, period // block_y, block_y))
    pattern = "abxitjzlkym,ksxtzy->abxitjzlsym"
    real_part = contract(pattern, vec_blocks[0], coarse[0]) - contract(pattern, vec_blocks[1], coarse[1])
    imag_part = contract(pattern, vec_blocks[0], coarse[1]) + contract(pattern, vec_blocks[1], coarse[0])
    joined = jnp.stack([real_part, imag_part]).reshape(vectors.shape[:-1] + (coarse_layers, 1, period))
    spread = jnp.broadcast_to(joined, vectors.shape[:-1] + (coarse_layers, layers // coarse_layers, period))
    return spread.reshape(vectors.shape[:-1] + (layers * period,))


def coarse_times(matrix, values, dagger):
    pattern = "qkxtzy,qsxtzy->ksxtzy" if dagger else "kqxtzy,qsxtzy->ksxtzy"
    flip_sign = -1.0 if dagger else 1.0
    real_part = contract(pattern, matrix[0], values[0]) - flip_sign * contract(pattern, matrix[1], values[1])
    imag_part = contract(pattern, matrix[0], values[1]) + flip_sign * contract(pattern, matrix[1], values[0])
    return jnp.stack([real_part, imag_part])


def coarse_apply(values, stencil, shifter):
    backs = tuple(coarse_times(stencil[direction], values, True) for direction in (1, 3, 4))
    shifted_up, shifted_down = shifter((values,) + backs)
    combined = coarse_mass * values + coarse_times(stencil[0], values, False)
    combined = combined + coarse_times(stencil[2], jnp.roll(values, -1, 6), False)
    combined = combined + jnp.roll(coarse_times(stencil[2], values, True), 1, 6)
    for position, direction in enumerate((1, 3, 4)):
        combined = combined + coarse_times(stencil[direction], shifted_up[0][position], False)
        combined = combined + shifted_down[position + 1][position]
    layers = values.shape[2]
    layer_index = lax.broadcasted_iota(jnp.int32, (1, 1, layers, 1, 1, 1, 1), 2)
    from_below = jnp.roll(values, 1, 2) * jnp.where(layer_index == 0, -wall_mass, 1.0)
    from_above = jnp.roll(values, -1, 2) * jnp.where(layer_index == layers - 1, -wall_mass, 1.0)
    return combined - coarse_fifth * (from_below + from_above)


def minimal_residual(operator, source, summer):
    solution = jnp.zeros_like(source)
    remain = source
    for sweep_index in range(CITERS):
        image = operator(remain)
        totals = summer((jnp.sum(image[0] * remain[0] + image[1] * remain[1]),
                         jnp.sum(image[0] * remain[1] - image[1] * remain[0]),
                         jnp.sum(image * image)))
        alpha_real = totals[0] / totals[2]
        alpha_imag = totals[1] / totals[2]
        solution = solution + jnp.stack([alpha_real * remain[0] - alpha_imag * remain[1],
                                         alpha_real * remain[1] + alpha_imag * remain[0]])
        remain = remain - jnp.stack([alpha_real * image[0] - alpha_imag * image[1],
                                     alpha_real * image[1] + alpha_imag * image[0]])
    return solution


def roll_shifter(arrays):
    shifted_up = tuple(tuple(jnp.roll(member, -1, axis_pos) for axis_pos in (3, 5, 4)) for member in arrays)
    shifted_down = tuple(tuple(jnp.roll(member, 1, axis_pos) for axis_pos in (3, 5, 4)) for member in arrays)
    return shifted_up, shifted_down


def keep_terms(terms):
    return terms


def reference(source_field, gauge_links, null_vectors, coarse_links):
    period = gauge_links.shape[-1]
    present = [tile_layers(gauge_links[direction], LS) for direction in range(4)]
    lowered = (jnp.roll(present[0], 1, 3), jnp.roll(present[2], 1, 5), jnp.roll(present[3], 1, 4))

    def operator(values):
        shifted_up, shifted_down = roll_shifter((values,))
        return fine_apply(values, present, lowered, shifted_up[0], shifted_down[0], period)

    def coarse_operator(values):
        return coarse_apply(values, coarse_links, roll_shifter)

    first = chebyshev(operator, jnp.zeros_like(source_field), source_field, True)
    remain = source_field - operator(first)
    coarse_source = restrict(remain, null_vectors, (BX, BT, BZ), BY, LSC, period)
    coarse_solution = minimal_residual(coarse_operator, coarse_source, keep_terms)
    corrected = first + prolong(coarse_solution, null_vectors, (BX, BT, BZ), BY, LS, period)
    return chebyshev(operator, corrected, source_field, False), coarse_solution
```

```python
import functools

import jax
import jax.numpy as jnp
from jax import lax
from jax.experimental import pallas as pl
from jax.experimental.pallas import tpu as pltpu
from jax.sharding import PartitionSpec as P

MESH = pl.DeviceIdType.MESH
F32 = jnp.float32

site_mass = 2.0
hop_kappa = 0.1
fifth_hop = 0.4
wall_mass = 0.1
cheb_lower = 0.6
cheb_upper = 3.4
coarse_mass = 3.0
coarse_fifth = 0.3
basis_scale = 0.125
DEG = 4
CITERS = 4
gamma_table = (
    ((3, 0.0, 1.0), (2, 0.0, 1.0)),
    ((3, -1.0, 0.0), (2, 1.0, 0.0)),
    ((2, 0.0, 1.0), (3, 0.0, -1.0)),
    ((2, 1.0, 0.0), (3, 1.0, 0.0)),
)
AXES = ((0, "grp"), (2, "gz"), (3, "ta"))
COARSE_DIRS = (1, 3, 4)


def cheb_coefficients():
    centre = 0.5 * (cheb_upper + cheb_lower)
    half_width = 0.5 * (cheb_upper - cheb_lower)
    spread_ratio = centre / half_width
    ratio_now = 1.0 / spread_ratio
    pairs = []
    for _ in range(DEG - 1):
        ratio_next = 1.0 / (2.0 * spread_ratio - ratio_now)
        pairs.append((ratio_next * ratio_now, 2.0 * ratio_next / half_width))
        ratio_now = ratio_next
    return 1.0 / centre, pairs


START, PAIRS = cheb_coefficients()
ALPHA = [pair[0] for pair in PAIRS] + [0.0, 0.0] + [pair[0] for pair in PAIRS]
BETA = [pair[1] for pair in PAIRS] + [0.0, START] + [pair[1] for pair in PAIRS]


def plus(a, b, sign):
    return a + b if sign > 0 else a - b


def project(v, mu, f):
    real, imag = [], []
    for a in range(2):
        b, gr, gi = gamma_table[mu][a]
        if gr != 0.0:
            real.append(plus(v[0][a], v[0][b], f * gr))
            imag.append(plus(v[1][a], v[1][b], f * gr))
        else:
            real.append(plus(v[0][a], v[1][b], -f * gi))
            imag.append(plus(v[1][a], v[0][b], f * gi))
    return [real, imag]


def rebuild(acc, h, mu, f):
    for a in range(2):
        b, gr, gi = gamma_table[mu][a]
        acc[0][a] = acc[0][a] + h[0][a]
        acc[1][a] = acc[1][a] + h[1][a]
        if gr != 0.0:
            acc[0][b] = plus(acc[0][b], h[0][a], f * gr)
            acc[1][b] = plus(acc[1][b], h[1][a], f * gr)
        else:
            acc[0][b] = plus(acc[0][b], h[1][a], f * gi)
            acc[1][b] = plus(acc[1][b], h[0][a], -f * gi)


def link_mul(links, mu, t, h, dagger):
    out = [[None, None], [None, None]]
    for col in range(3):
        if dagger:
            lr, li = links[mu, 0, col, :, t], links[mu, 1, col, :, t]
        else:
            lr, li = links[mu, 0, :, col, t], links[mu, 1, :, col, t]
        for a in range(2):
            hr, hi = h[0][a][col][None], h[1][a][col][None]
            if dagger:
                re, im = lr * hr + li * hi, lr * hi - li * hr
            else:
                re, im = lr * hr - li * hi, lr * hi + li * hr
            out[0][a] = re if col == 0 else out[0][a] + re
            out[1][a] = im if col == 0 else out[1][a] + im
    return out


def each(fn, h):
    return [[fn(h[ri][a]) for a in range(2)] for ri in range(2)]


def dot(a, b, dims=((1,), (0,))):
    return lax.dot_general(
        a, b, (dims, ((), ())), precision=lax.Precision.HIGHEST, preferred_element_type=F32
    )


def iota(shape, dim):
    return lax.broadcasted_iota(jnp.int32, shape, dim)


def phases_of(sizes):
    phases = []
    for axis in ("gz", "ta", "grp"):
        size = sizes[axis]
        if size > 4 and size % 4 == 0:
            phases.append((axis, 1, 4))
            phases.append((axis, 4, size // 4))
        elif size > 1:
            phases.append((axis, 1, size))
    return phases


def kernel(sizes, src, gauge, null, coarse, u_out, e_out, p, r, u, acc, links, g8, hx, qx, hz, qz, ht, qt,
           sendx, sendz, sendt, recvx, recvz, recvt, nv, nvt, low, ff, fb, basis, crecv, ar_send, ar_recv,
           fsend, frecv, lsend, lrecv, csend, crsem, asend, arsem):
    me = {axis: lax.axis_index(axis) for axis in ("grp", "ta", "gz")}
    phases = phases_of(sizes)

    def moved(axis, by):
        return lax.rem(me[axis] + (by + sizes[axis]), sizes[axis])

    def in_group(axis, stride, count, by):
        own = lax.rem(lax.div(me[axis], stride), count)
        return me[axis] + (lax.rem(own + by, count) - own) * stride

    barrier = pltpu.get_barrier_semaphore()
    partners = []
    for _, axis in AXES:
        partners += [{axis: moved(axis, 1)}, {axis: moved(axis, -1)}]
    for axis, stride, count in phases:
        partners += [{axis: in_group(axis, stride, count, by)} for by in range(1, count)]
    for partner in partners:
        pl.semaphore_signal(barrier, inc=1, device_id=partner, device_id_type=MESH)

    for t in range(2):
        for x in range(4):
            rows = src[:, 4 * x + 2 * t:4 * x + 2 * t + 2, :].reshape(2, 4, 3, 2, 128)
            r[:, :, :, t, 2 * x:2 * x + 2, :] = rows
            p[:, :, :, t, 2 * x:2 * x + 2, :] = rows * START
            u[:, :, :, t, 2 * x:2 * x + 2, :] = rows * START
            g8[:, t, 2 * x:2 * x + 2, :] = gauge[:, 4 * x + 2 * t:4 * x + 2 * t + 2, :]
    spread_y = jnp.where((iota((8, 128), 1) & 7) == iota((8, 128), 0), 1.0, 0.0).astype(F32)
    tiled = dot(g8[...].reshape(72 * 16, 8), spread_y) * (-hop_kappa)
    links[...] = tiled.reshape(4, 2, 3, 3, 2, 8, 128)

    pl.semaphore_wait(barrier, len(partners))

    def low_copy(d):
        return pltpu.make_async_remote_copy(
            src_ref=coarse.at[pl.ds(COARSE_DIRS[d] * 96, 96)], dst_ref=low.at[d], send_sem=lsend.at[d],
            recv_sem=lrecv.at[d], device_id={AXES[d][1]: moved(AXES[d][1], 1)}, device_id_type=MESH)

    for d in range(3):
        low_copy(d).start()

    row8 = iota((8, 128), 0)
    lane8 = iota((8, 128), 1)

    def face_copy(d, side, slot):
        out, into = ((sendx, recvx), (sendz, recvz), (sendt, recvt))[d]
        axis = AXES[d][1]
        return pltpu.make_async_remote_copy(
            src_ref=out.at[side], dst_ref=into.at[slot, side], send_sem=fsend.at[2 * d + side],
            recv_sem=frecv.at[slot, 2 * d + side], device_id={axis: moved(axis, 2 * side - 1)},
            device_id_type=MESH)

    def field(ref, t):
        return [[ref[ri, s, :, t] for s in range(4)] for ri in range(2)]

    def build_null():
        for t in range(2):
            for x in range(4):
                nv[:, t, 2 * x:2 * x + 2, :] = null[:, x, t]

    def build_null_transposed():
        for ri in range(2):
            half = nv[12 * ri:12 * ri + 12].reshape(192, 192)
            nvt[192 * ri:192 * ri + 192, :] = half.T

    def build_coarse():
        for d in range(3):
            low_copy(d).wait()
        ff[...] = jnp.zeros_like(ff)
        fb[...] = jnp.zeros_like(fb)
        zero = jnp.zeros((24, 104), F32)

        def piece(ref, base, y):
            return jnp.concatenate([ref[pl.ds(base + y, 24, stride=2), :] * basis_scale, zero], axis=1)

        def placed(value, at):
            return value if at == 0 else pltpu.roll(value, at, 1)

        for y in range(2):
            blocks = []
            for direction in (0, 1, 3, 4, 2):
                blocks.append([piece(coarse, direction * 96 + ri * 48, y) for ri in range(2)])
            for ro in range(2):
                for tile in range(3):
                    total = None
                    for j in range(2):
                        if 2 * tile + j > 4:
                            continue
                        mr, mi = blocks[2 * tile + j]
                        first, second = (mr, -mi) if ro == 0 else (mi, mr)
                        part = placed(first, 64 * j) + placed(second, 64 * j + 32)
                        total = part if total is None else total + part
                    ff[64 * y + 32 * ro:64 * y + 32 * ro + 24, 128 * tile:128 * tile + 128] = total
        for block in range(4):
            parts = []
            for y in range(2):
                if block == 0:
                    parts.append([piece(coarse, 2 * 96 + ri * 48, 1 - y) for ri in range(2)])
                else:
                    parts.append([piece(low.at[block - 1], ri * 48, y) for ri in range(2)])
            for ri in range(2):
                total = None
                for y in range(2):
                    mr, mi = parts[y]
                    first, second = (mr, -mi) if ri == 0 else (mi, mr)
                    part = placed(first, 64 * y) + placed(second, 64 * y + 32)
                    total = part if total is None else total + part
                fb[64 * block + 32 * ri:64 * block + 32 * ri + 24, :] = total

    def apply_fine(k, hooks):
        slot = lax.rem(k, 2)
        even = (iota((3, 8, 128), 1) & 1) == 0
        for t in range(2):
            v = field(p, t)
            down = project(v, 0, -1.0)
            up = link_mul(links, 0, t, project(v, 0, 1.0), True)
            for ri in range(2):
                for a in range(2):
                    j = 2 * (2 * a + t)
                    sendx[0, 3 * ri:3 * ri + 3, j:j + 2, :] = down[ri][a][:, 0:2]
                    sendx[1, 3 * ri:3 * ri + 3, j:j + 2, :] = up[ri][a][:, 6:8]
                    hx[ri, a, :, t] = pltpu.roll(down[ri][a], 6, 1)
                    qx[ri, a, :, t] = pltpu.roll(up[ri][a], 2, 1)
        face_copy(0, 0, slot).start()
        face_copy(0, 1, slot).start()
        downs, ups = [], []
        for t in range(2):
            v = field(p, t)
            downs.append(project(v, 2, -1.0))
            ups.append(link_mul(links, 2, t, project(v, 2, 1.0), True))
        for ri in range(2):
            for a in range(2):
                for t in range(2):
                    hz[ri, a, :, t] = pltpu.roll(downs[t][ri][a], 7, 1)
                    qz[ri, a, :, t] = pltpu.roll(ups[t][ri][a], 1, 1)
                sendz[0, ri, a] = jnp.where(even, downs[0][ri][a], pltpu.roll(downs[1][ri][a], 1, 1))
                sendz[1, ri, a] = jnp.where(even, pltpu.roll(ups[0][ri][a], 7, 1), ups[1][ri][a])
        face_copy(1, 0, slot).start()
        face_copy(1, 1, slot).start()
        v = field(p, 0)
        down = project(v, 3, -1.0)
        own_up = link_mul(links, 3, 0, project(v, 3, 1.0), True)
        v = field(p, 1)
        own_down = project(v, 3, -1.0)
        up = link_mul(links, 3, 1, project(v, 3, 1.0), True)
        for ri in range(2):
            for a in range(2):
                sendt[0, ri, a] = down[ri][a]
                sendt[1, ri, a] = up[ri][a]
                ht[ri, a] = own_down[ri][a]
                qt[ri, a] = own_up[ri][a]
        face_copy(2, 0, slot).start()
        face_copy(2, 1, slot).start()

        lane = iota((3, 8, 128), 2)
        ypos = lane & 7
        below = jnp.where(lane < 8, fifth_hop * wall_mass, -fifth_hop).astype(F32)
        above = jnp.where(lane >= 120, fifth_hop * wall_mass, -fifth_hop).astype(F32)
        for t in range(2):
            v = field(p, t)
            total = [[None] * 4, [None] * 4]
            for ri in range(2):
                for s in range(4):
                    if s < 2:
                        side = below * pltpu.roll(v[ri][s], 8, 2)
                    else:
                        side = above * pltpu.roll(v[ri][s], 120, 2)
                    total[ri][s] = site_mass * v[ri][s] + side
            h = each(lambda w: jnp.where(ypos == 7, pltpu.roll(w, 7, 2), pltpu.roll(w, 127, 2)), project(v, 1, -1.0))
            rebuild(total, link_mul(links, 1, t, h, False), 1, -1.0)
            h = link_mul(links, 1, t, project(v, 1, 1.0), True)
            h = each(lambda w: jnp.where(ypos == 0, pltpu.roll(w, 121, 2), pltpu.roll(w, 1, 2)), h)
            rebuild(total, h, 1, 1.0)
            if t == 0:
                h = [[ht[ri, a] for a in range(2)] for ri in range(2)]
                rebuild(total, link_mul(links, 3, 0, h, False), 3, -1.0)
            else:
                rebuild(total, [[qt[ri, a] for a in range(2)] for ri in range(2)], 3, 1.0)
            for ri in range(2):
                for s in range(4):
                    acc[ri, s, :, t] = total[ri][s]
        for at, hook in hooks:
            pl.when(k == at)(hook)

        for d in (2, 0):
            face_copy(d, 0, slot).wait()
            face_copy(d, 1, slot).wait()
        for ri in range(2):
            for a in range(2):
                for t in range(2):
                    j = 2 * (2 * a + t)
                    hx[ri, a, :, t, 6:8, :] = recvx[slot, 0, 3 * ri:3 * ri + 3, j:j + 2, :]
                    qx[ri, a, :, t, 0:2, :] = recvx[slot, 1, 3 * ri:3 * ri + 3, j:j + 2, :]
        for t in range(2):
            total = field(acc, t)
            if t == 0:
                rebuild(total, [[recvt[slot, 1, ri, a] for a in range(2)] for ri in range(2)], 3, 1.0)
            else:
                h = [[recvt[slot, 0, ri, a] for a in range(2)] for ri in range(2)]
                rebuild(total, link_mul(links, 3, 1, h, False), 3, -1.0)
            h = [[hx[ri, a, :, t] for a in range(2)] for ri in range(2)]
            rebuild(total, link_mul(links, 0, t, h, False), 0, -1.0)
            rebuild(total, [[qx[ri, a, :, t] for a in range(2)] for ri in range(2)], 0, 1.0)
            for ri in range(2):
                for s in range(4):
                    acc[ri, s, :, t] = total[ri][s]
        face_copy(1, 0, slot).wait()
        face_copy(1, 1, slot).wait()
        alpha = jnp.float32(ALPHA[0])
        beta = jnp.float32(BETA[0])
        for at in range(1, 8):
            alpha = jnp.where(k == at, jnp.float32(ALPHA[at]), alpha)
            beta = jnp.where(k == at, jnp.float32(BETA[at]), beta)
        for t in range(2):
            total = field(acc, t)
            h = [[None, None], [None, None]]
            q = [[None, None], [None, None]]
            for ri in range(2):
                for a in range(2):
                    came, back = recvz[slot, 0, ri, a], recvz[slot, 1, ri, a]
                    if t == 0:
                        came = pltpu.roll(came, 1, 1)
                    else:
                        back = pltpu.roll(back, 7, 1)
                    h[ri][a] = jnp.where(even, hz[ri, a, :, t], came)
                    q[ri][a] = jnp.where(even, back, qz[ri, a, :, t])
            rebuild(total, link_mul(links, 2, t, h, False), 2, -1.0)
            rebuild(total, q, 2, 1.0)
            for ri in range(2):
                for s in range(4):
                    left = r[ri, s, :, t] - total[ri][s]
                    step = alpha * p[ri, s, :, t] + beta * left
                    r[ri, s, :, t] = left
                    p[ri, s, :, t] = step
                    u[ri, s, :, t] = u[ri, s, :, t] + step

    def first_half(k, carry):
        apply_fine(k, ((0, build_null), (1, build_null_transposed), (2, build_coarse)))
        return carry

    def second_half(k, carry):
        apply_fine(k, ())
        return carry

    lax.fori_loop(0, DEG, first_half, 0)

    diagonal = (iota((192, 256), 0) & 7) == (iota((192, 256), 1) & 7)
    selector = jnp.where(
        ((lane8 >> 5) == (row8 & 3)) & (((lane8 & 7) >> 2) == (row8 >> 2)), 1.0, 0.0).astype(F32)
    fold = jnp.where((iota((32, 192), 1) >> 3) == iota((32, 192), 0), 1.0, 0.0).astype(F32)
    both = jnp.concatenate([r[0].reshape(192, 128), r[1].reshape(192, 128)], axis=1)
    prod = dot(nvt[...], both)
    real = prod[0:192, 0:128] + prod[192:384, 128:256]
    imag = prod[0:192, 128:256] - prod[192:384, 0:128]
    kept = jnp.where(diagonal, jnp.concatenate([real, imag], axis=1), 0.0)
    summed = dot(fold, kept)
    stacked = jnp.concatenate([summed[:, 0:128], summed[:, 128:256]] * 2, axis=0)
    basis[0] = dot(selector, stacked, ((1,), (1,)))

    def coarse_copy(step, d, side):
        axis = AXES[d][1]
        return pltpu.make_async_remote_copy(
            src_ref=basis.at[step], dst_ref=crecv.at[step, 2 * d + side], send_sem=csend.at[step, 2 * d + side],
            recv_sem=crsem.at[step, 2 * d + side], device_id={axis: moved(axis, 2 * side - 1)},
            device_id_type=MESH)

    low_half = lane8 < 64
    for step in range(CITERS):
        for d in range(3):
            for side in range(2):
                coarse_copy(step, d, side).start()
        own = basis[step]
        other = pltpu.roll(own, 4, 0)
        layer = row8 & 3
        from_below = jnp.where(layer == 0, -wall_mass * pltpu.roll(own, 5, 0), pltpu.roll(own, 1, 0))
        from_above = jnp.where(layer == 3, -wall_mass * pltpu.roll(own, 3, 0), pltpu.roll(own, 7, 0))
        local = (-coarse_fifth * basis_scale) * (from_below + from_above)
        for d in range(3):
            for side in range(2):
                coarse_copy(step, d, side).wait()
        got = [crecv[step, j] for j in range(6)]
        ahead = jnp.concatenate(
            [jnp.where(low_half, own, got[0]), jnp.where(low_half, got[2], got[4]), other], axis=1)
        behind = jnp.concatenate(
            [jnp.where(low_half, other, got[1]), jnp.where(low_half, got[3], got[5])], axis=1)
        out = dot(ahead, ff[...], ((1,), (1,))) + dot(behind, fb[...])
        out = jnp.where((row8 < 4) == low_half, out, pltpu.roll(out, 64, 1))
        basis[step + 1] = out + local

    vectors = [basis[i] for i in range(CITERS + 1)]
    sign = jnp.where((lane8 & 32) == 0, 1.0, -1.0).astype(F32)
    turned = [sign * pltpu.roll(v, 32, 1) for v in vectors]
    entries = []
    for i in range(CITERS + 1):
        for j in range(i, CITERS + 1):
            entries.append((i, j, 0))
    for i in range(CITERS + 1):
        for j in range(i + 1, CITERS + 1):
            entries.append((i, j, 1))
    count = len(entries)
    products = jnp.concatenate(
        [jnp.where(low_half, vectors[i] * (vectors[j] if part == 0 else turned[j]), 0.0) for i, j, part in entries],
        axis=0)
    rowsum = dot(products, jnp.ones((128, 128), F32))
    mine = (iota((8 * count, 128), 0) >> 3) == iota((8 * count, 128), 1)
    sums = dot(jnp.ones((8, 8 * count), F32), jnp.where(mine, rowsum, 0.0))
    for number, (axis, stride, width) in enumerate(phases):
        ar_send[number] = sums
        copies = []
        for by in range(1, width):
            copies.append(pltpu.make_async_remote_copy(
                src_ref=ar_send.at[number], dst_ref=ar_recv.at[number, by - 1], send_sem=asend.at[number, by - 1],
                recv_sem=arsem.at[number, by - 1], device_id={axis: in_group(axis, stride, width, by)},
                device_id_type=MESH))
        for copy in copies:
            copy.start()
        for by, copy in enumerate(copies):
            copy.wait()
            sums = sums + ar_recv[number, by]

    size = CITERS + 1
    gram = [[None] * size for _ in range(size)]
    for number, (i, j, part) in enumerate(entries):
        value = jnp.broadcast_to(sums[:, number:number + 1], (8, 128))
        if part == 0:
            gram[i][j] = (value, None)
            if i != j:
                gram[j][i] = (value, None)
        else:
            gram[i][j] = (gram[i][j][0], value)
            gram[j][i] = (gram[j][i][0], -value)

    def gram_times(vector):
        result = []
        for i in range(size):
            tr, ti = None, None
            for j, (vr, vi) in enumerate(vector):
                gr, gi = gram[i][j]
                re, im = gr * vr, gr * vi
                if gi is not None:
                    re, im = re - gi * vi, im + gi * vr
                tr = re if tr is None else tr + re
                ti = im if ti is None else ti + im
            result.append((tr, ti))
        return result

    one, none = jnp.ones((8, 128), F32), jnp.zeros((8, 128), F32)
    coef = [(one, none)]
    seen = gram_times(coef)
    answer = [(none, none)] * CITERS
    grow = 1.0 / basis_scale
    for step in range(CITERS):
        image = []
        for i in range(step + 2):
            re = im = none
            if i <= step:
                re, im = coarse_mass * coef[i][0], coarse_mass * coef[i][1]
            if i >= 1:
                re, im = re + grow * coef[i - 1][0], im + grow * coef[i - 1][1]
            image.append((re, im))
        through = gram_times(image)
        top_r = top_i = bottom = none
        for i, (dr, di) in enumerate(image):
            top_r = top_r + (dr * seen[i][0] + di * seen[i][1])
            top_i = top_i + (dr * seen[i][1] - di * seen[i][0])
            bottom = bottom + (dr * through[i][0] + di * through[i][1])
        ar, ai = top_r / bottom, top_i / bottom
        for i, (cr, ci) in enumerate(coef):
            answer[i] = (answer[i][0] + (ar * cr - ai * ci), answer[i][1] + (ar * ci + ai * cr))
        padded = coef + [(none, none)]
        coef = [(cr - (ar * dr - ai * di), ci - (ar * di + ai * dr))
                for (cr, ci), (dr, di) in zip(padded, image)]
        seen = [(sr - (ar * zr - ai * zi), si - (ar * zi + ai * zr))
                for (sr, si), (zr, zi) in zip(seen, through)]
    found = none
    for i in range(CITERS):
        found = found + (answer[i][0] * vectors[i] - answer[i][1] * turned[i])
    e_out[...] = found

    spread = dot(found, selector, ((0,), (0,)))
    paired = jnp.concatenate([spread[0:32], spread[32:64]], axis=1)
    unfold = jnp.where((iota((192, 32), 0) >> 3) == iota((192, 32), 1), 1.0, 0.0).astype(F32)
    weights = jnp.where(diagonal, dot(unfold, paired), 0.0)
    prod = dot(nv[...].reshape(384, 192), weights)
    real = (prod[0:192, 0:128] - prod[192:384, 128:256]).reshape(4, 3, 2, 8, 128)
    imag = (prod[0:192, 128:256] + prod[192:384, 0:128]).reshape(4, 3, 2, 8, 128)
    p[0] = real
    p[1] = imag
    u[0] = u[0] + real
    u[1] = u[1] + imag

    lax.fori_loop(DEG, 2 * DEG, second_half, 0)
    for t in range(2):
        for x in range(4):
            u_out[:, 4 * x + 2 * t:4 * x + 2 * t + 2, :] = u[:, :, :, t, 2 * x:2 * x + 2, :].reshape(24, 2, 128)


def body(sizes, source_field, gauge_links, null_vectors, coarse_links):
    count = len(phases_of(sizes))
    vmem = pl.BlockSpec(memory_space=pltpu.VMEM)
    half = (2, 2, 3, 2, 8, 128)
    full = (2, 4, 3, 2, 8, 128)
    shapes = [full, full, full, full, (4, 2, 3, 3, 2, 8, 128), (72, 2, 8, 8), half, half, half, half,
              (2, 2, 3, 8, 128), (2, 2, 3, 8, 128),
              (2, 6, 8, 128), (2, 2, 2, 3, 8, 128), (2, 2, 2, 3, 8, 128),
              (2, 2, 6, 8, 128), (2, 2, 2, 2, 3, 8, 128), (2, 2, 2, 2, 3, 8, 128),
              (24, 2, 8, 192), (384, 192), (3, 96, 24), (128, 384), (256, 128), (CITERS + 1, 8, 128),
              (CITERS, 6, 8, 128), (count, 8, 128), (count, 3, 8, 128)]
    sems = [(6,), (2, 6), (3,), (3,), (CITERS, 6), (CITERS, 6), (count, 3), (count, 3)]
    out, found = pl.pallas_call(
        functools.partial(kernel, sizes),
        out_shape=(jax.ShapeDtypeStruct((24, 16, 128), F32), jax.ShapeDtypeStruct((8, 128), F32)),
        in_specs=[vmem] * 4,
        out_specs=(vmem, vmem),
        scratch_shapes=[pltpu.VMEM(shape, F32) for shape in shapes]
        + [pltpu.SemaphoreType.DMA(shape) for shape in sems],
        compiler_params=pltpu.CompilerParams(
            collective_id=0, has_side_effects=True, vmem_limit_bytes=40 * 1024 * 1024),
    )(
        source_field.reshape(24, 16, 128),
        gauge_links.reshape(72, 16, 8),
        null_vectors.reshape(24, 4, 2, 2, 192),
        coarse_links.transpose(0, 1, 2, 4, 5, 6, 7, 3).reshape(480, 24),
    )
    found = found[:, 0:64].reshape(2, 4, 2, 32)[:, :, :, 0:24].transpose(2, 3, 1, 0)
    return out.reshape(source_field.shape), found.reshape(2, 24, 4, 1, 1, 1, 2)


def solution(mesh):
    sizes = {axis: mesh.shape[axis] for axis in ("grp", "ta", "gz")}
    placed = (
        P(None, None, None, "grp", "ta", "gz", None),
        P(None, None, None, None, "grp", "ta", "gz", None),
        P(None, None, None, "grp", "ta", "gz", None),
        P(None, None, None, None, "grp", "ta", "gz", None),
    )
    return jax.shard_map(
        functools.partial(body, sizes),
        mesh=mesh,
        in_specs=placed,
        out_specs=(
            P(None, None, None, "grp", "ta", "gz", None),
            P(None, None, None, "grp", "ta", "gz", None),
        ),
        check_vma=False,
    )
```

```python
import functools

import jax
import jax.numpy as jnp
from jax import lax
from jax.experimental import pallas as pl
from jax.experimental.pallas import tpu as pltpu
from jax.sharding import PartitionSpec as P

MESH = pl.DeviceIdType.MESH
F32 = jnp.float32

site_mass = 2.0
hop_kappa = 0.1
fifth_hop = 0.4
wall_mass = 0.1
cheb_lower = 0.6
cheb_upper = 3.4
coarse_mass = 3.0
coarse_fifth = 0.3
basis_scale = 0.125
DEG = 4
CITERS = 4
gamma_table = (
    ((3, 0.0, 1.0), (2, 0.0, 1.0)),
    ((3, -1.0, 0.0), (2, 1.0, 0.0)),
    ((2, 0.0, 1.0), (3, 0.0, -1.0)),
    ((2, 1.0, 0.0), (3, 1.0, 0.0)),
)
AXES = ((0, "grp"), (2, "gz"), (3, "ta"))
COARSE_DIRS = (1, 3, 4)


def cheb_coefficients():
    centre = 0.5 * (cheb_upper + cheb_lower)
    half_width = 0.5 * (cheb_upper - cheb_lower)
    spread_ratio = centre / half_width
    ratio_now = 1.0 / spread_ratio
    pairs = []
    for _ in range(DEG - 1):
        ratio_next = 1.0 / (2.0 * spread_ratio - ratio_now)
        pairs.append((ratio_next * ratio_now, 2.0 * ratio_next / half_width))
        ratio_now = ratio_next
    return 1.0 / centre, pairs


START, PAIRS = cheb_coefficients()
ALPHA = [pair[0] for pair in PAIRS] + [0.0, 0.0] + [pair[0] for pair in PAIRS]
BETA = [pair[1] for pair in PAIRS] + [0.0, START] + [pair[1] for pair in PAIRS]


def plus(a, b, sign):
    return a + b if sign > 0 else a - b


def project(v, mu, f):
    real, imag = [], []
    for a in range(2):
        b, gr, gi = gamma_table[mu][a]
        if gr != 0.0:
            real.append(plus(v[0][a], v[0][b], f * gr))
            imag.append(plus(v[1][a], v[1][b], f * gr))
        else:
            real.append(plus(v[0][a], v[1][b], -f * gi))
            imag.append(plus(v[1][a], v[0][b], f * gi))
    return [real, imag]


def rebuild(acc, h, mu, f):
    for a in range(2):
        b, gr, gi = gamma_table[mu][a]
        acc[0][a] = acc[0][a] + h[0][a]
        acc[1][a] = acc[1][a] + h[1][a]
        if gr != 0.0:
            acc[0][b] = plus(acc[0][b], h[0][a], f * gr)
            acc[1][b] = plus(acc[1][b], h[1][a], f * gr)
        else:
            acc[0][b] = plus(acc[0][b], h[1][a], f * gi)
            acc[1][b] = plus(acc[1][b], h[0][a], -f * gi)


def link_mul(links, mu, t, h, dagger):
    out = [[None, None], [None, None]]
    for col in range(3):
        if dagger:
            lr, li = links[mu, 0, col, :, t], links[mu, 1, col, :, t]
        else:
            lr, li = links[mu, 0, :, col, t], links[mu, 1, :, col, t]
        for a in range(2):
            hr, hi = h[0][a][col][None], h[1][a][col][None]
            if dagger:
                re, im = lr * hr + li * hi, lr * hi - li * hr
            else:
                re, im = lr * hr - li * hi, lr * hi + li * hr
            out[0][a] = re if col == 0 else out[0][a] + re
            out[1][a] = im if col == 0 else out[1][a] + im
    return out


def each(fn, h):
    return [[fn(h[ri][a]) for a in range(2)] for ri in range(2)]


def dot(a, b, dims=((1,), (0,))):
    return lax.dot_general(
        a, b, (dims, ((), ())), precision=lax.Precision.HIGHEST, preferred_element_type=F32
    )


def iota(shape, dim):
    return lax.broadcasted_iota(jnp.int32, shape, dim)


def kernel(sizes, src_in, gauge_in, null_in, coarse_in, u_out, e_out, src, gauge, null, coarse, p, u, fields, acc, links, g8,
           hx, qx, hz, qz, ht, qt, sendx, sendz, sendt, recvx, recvz, recvt, nv, nvt, low, ff, fb, basis, crecv, ar_send,
           ar_recv, isem, fsend, frecv, lsend, lrecv, csend, crsem, asend, arsem):
    me = {axis: lax.axis_index(axis) for axis in ("grp", "ta", "gz")}
    plane = sizes["grp"] * sizes["gz"]
    spot = me["grp"] * sizes["gz"] + me["gz"]

    def moved(axis, by):
        return lax.rem(me[axis] + (by + sizes[axis]), sizes[axis])

    def in_plane(by):
        other = lax.rem(spot + by, plane)
        return {"grp": lax.div(other, sizes["gz"]), "gz": lax.rem(other, sizes["gz"])}

    groups = ([{"ta": moved("ta", by)} for by in range(1, sizes["ta"])], [in_plane(by) for by in range(1, plane)])

    barrier = pltpu.get_barrier_semaphore()
    for partner in groups[0] + groups[1]:
        pl.semaphore_signal(barrier, inc=1, device_id=partner, device_id_type=MESH)

    loads = [pltpu.make_async_copy(a, b, isem.at[i]) for i, (a, b) in enumerate(
        ((gauge_in, gauge), (src_in, src), (coarse_in, coarse), (null_in, null)))]
    for load in loads:
        load.start()

    r = fields.at[4]

    loads[0].wait()
    for t in range(2):
        for x in range(4):
            g8[:, t, 2 * x:2 * x + 2, :] = gauge[:, 4 * x + 2 * t:4 * x + 2 * t + 2, :]
    spread_y = jnp.where((iota((8, 128), 1) & 7) == iota((8, 128), 0), 1.0, 0.0).astype(F32)
    tiled = dot(g8[...].reshape(72 * 16, 8), spread_y) * (-hop_kappa)
    links[...] = tiled.reshape(4, 2, 3, 3, 2, 8, 128)
    loads[1].wait()
    for t in range(2):
        for x in range(4):
            rows = src[:, 4 * x + 2 * t:4 * x + 2 * t + 2, :].reshape(2, 4, 3, 2, 128)
            r[:, :, :, t, 2 * x:2 * x + 2, :] = rows
            p[:, :, :, t, 2 * x:2 * x + 2, :] = rows * START
            u[:, :, :, t, 2 * x:2 * x + 2, :] = rows * START
    loads[2].wait()

    pl.semaphore_wait(barrier, len(groups[0]) + len(groups[1]))

    def low_copy(d):
        return pltpu.make_async_remote_copy(
            src_ref=coarse.at[pl.ds(COARSE_DIRS[d] * 96, 96)], dst_ref=low.at[d], send_sem=lsend.at[d],
            recv_sem=lrecv.at[d], device_id={AXES[d][1]: moved(AXES[d][1], 1)}, device_id_type=MESH)

    row8 = iota((8, 128), 0)
    lane8 = iota((8, 128), 1)

    def face_copy(d, side, ls, rs):
        out, into = ((sendx, recvx), (sendz, recvz), (sendt, recvt))[d]
        axis = AXES[d][1]
        return pltpu.make_async_remote_copy(
            src_ref=out.at[ls, side], dst_ref=into.at[rs, side], send_sem=fsend.at[ls, 2 * d + side],
            recv_sem=frecv.at[rs, 2 * d + side], device_id={axis: moved(axis, 2 * side - 1)},
            device_id_type=MESH)

    def field(ref, t):
        return [[ref[ri, s, :, t] for s in range(4)] for ri in range(2)]

    def keep(ref, t, total):
        for ri in range(2):
            for s in range(4):
                ref[ri, s, :, t] = total[ri][s]

    def build_null():
        loads[3].wait()
        for t in range(2):
            for x in range(4):
                nv[:, t, 2 * x:2 * x + 2, :] = null[:, x, t]

    def build_null_transposed():
        for ri in range(2):
            half = nv[12 * ri:12 * ri + 12].reshape(192, 192)
            nvt[192 * ri:192 * ri + 192, :] = half.T

    def build_coarse():
        for d in range(3):
            low_copy(d).wait()
        ff[...] = jnp.zeros_like(ff)
        fb[...] = jnp.zeros_like(fb)
        zero = jnp.zeros((24, 104), F32)

        def piece(ref, base, y):
            return jnp.concatenate([ref[pl.ds(base + y, 24, stride=2), :] * basis_scale, zero], axis=1)

        def placed(value, at):
            return value if at == 0 else pltpu.roll(value, at, 1)

        for y in range(2):
            blocks = []
            for direction in (0, 1, 3, 4, 2):
                blocks.append([piece(coarse, direction * 96 + ri * 48, y) for ri in range(2)])
            for ro in range(2):
                for tile in range(3):
                    total = None
                    for j in range(2):
                        if 2 * tile + j > 4:
                            continue
                        mr, mi = blocks[2 * tile + j]
                        first, second = (mr, -mi) if ro == 0 else (mi, mr)
                        part = placed(first, 64 * j) + placed(second, 64 * j + 32)
                        total = part if total is None else total + part
                    ff[64 * y + 32 * ro:64 * y + 32 * ro + 24, 128 * tile:128 * tile + 128] = total
        for block in range(4):
            parts = []
            for y in range(2):
                if block == 0:
                    parts.append([piece(coarse, 2 * 96 + ri * 48, 1 - y) for ri in range(2)])
                else:
                    parts.append([piece(low.at[block - 1], ri * 48, y) for ri in range(2)])
            for ri in range(2):
                total = None
                for y in range(2):
                    mr, mi = parts[y]
                    first, second = (mr, -mi) if ri == 0 else (mi, mr)
                    part = placed(first, 64 * y) + placed(second, 64 * y + 32)
                    total = part if total is None else total + part
                fb[64 * block + 32 * ri:64 * block + 32 * ri + 24, :] = total

    even = (iota((3, 8, 128), 1) & 1) == 0

    def start(f, ls, rs):
        v = field(f, 0)
        down = project(v, 3, -1.0)
        own_up = link_mul(links, 3, 0, project(v, 3, 1.0), True)
        v = field(f, 1)
        own_down = project(v, 3, -1.0)
        up = link_mul(links, 3, 1, project(v, 3, 1.0), True)
        for ri in range(2):
            for a in range(2):
                sendt[ls, 0, ri, a] = down[ri][a]
                sendt[ls, 1, ri, a] = up[ri][a]
                ht[ls, ri, a] = own_down[ri][a]
                qt[ls, ri, a] = own_up[ri][a]
        face_copy(2, 0, ls, rs).start()
        face_copy(2, 1, ls, rs).start()
        for t in range(2):
            v = field(f, t)
            down = project(v, 0, -1.0)
            up = link_mul(links, 0, t, project(v, 0, 1.0), True)
            for ri in range(2):
                for a in range(2):
                    j = 2 * (2 * a + t)
                    sendx[ls, 0, 3 * ri:3 * ri + 3, j:j + 2, :] = down[ri][a][:, 0:2]
                    sendx[ls, 1, 3 * ri:3 * ri + 3, j:j + 2, :] = up[ri][a][:, 6:8]
                    hx[ls, ri, a, :, t] = pltpu.roll(down[ri][a], 6, 1)
                    qx[ls, ri, a, :, t] = pltpu.roll(up[ri][a], 2, 1)
        face_copy(0, 0, ls, rs).start()
        face_copy(0, 1, ls, rs).start()
        downs, ups = [], []
        for t in range(2):
            v = field(f, t)
            downs.append(project(v, 2, -1.0))
            ups.append(link_mul(links, 2, t, project(v, 2, 1.0), True))
        for ri in range(2):
            for a in range(2):
                for t in range(2):
                    hz[ls, ri, a, :, t] = pltpu.roll(downs[t][ri][a], 7, 1)
                    qz[ls, ri, a, :, t] = pltpu.roll(ups[t][ri][a], 1, 1)
                sendz[ls, 0, ri, a] = jnp.where(even, downs[0][ri][a], pltpu.roll(downs[1][ri][a], 1, 1))
                sendz[ls, 1, ri, a] = jnp.where(even, pltpu.roll(ups[0][ri][a], 7, 1), ups[1][ri][a])
        face_copy(1, 0, ls, rs).start()
        face_copy(1, 1, ls, rs).start()

        lane = iota((3, 8, 128), 2)
        ypos = lane & 7
        below = jnp.where(lane < 8, fifth_hop * wall_mass, -fifth_hop).astype(F32)
        above = jnp.where(lane >= 120, fifth_hop * wall_mass, -fifth_hop).astype(F32)
        for t in range(2):
            v = field(f, t)
            total = [[None] * 4, [None] * 4]
            for ri in range(2):
                for s in range(4):
                    if s < 2:
                        side = below * pltpu.roll(v[ri][s], 8, 2)
                    else:
                        side = above * pltpu.roll(v[ri][s], 120, 2)
                    total[ri][s] = site_mass * v[ri][s] + side
            h = each(lambda w: jnp.where(ypos == 7, pltpu.roll(w, 7, 2), pltpu.roll(w, 127, 2)), project(v, 1, -1.0))
            rebuild(total, link_mul(links, 1, t, h, False), 1, -1.0)
            h = link_mul(links, 1, t, project(v, 1, 1.0), True)
            h = each(lambda w: jnp.where(ypos == 0, pltpu.roll(w, 121, 2), pltpu.roll(w, 1, 2)), h)
            rebuild(total, h, 1, 1.0)
            if t == 0:
                h = [[ht[ls, ri, a] for a in range(2)] for ri in range(2)]
                rebuild(total, link_mul(links, 3, 0, h, False), 3, -1.0)
            else:
                rebuild(total, [[qt[ls, ri, a] for a in range(2)] for ri in range(2)], 3, 1.0)
            keep(acc.at[ls], t, total)

    def finish(ls, rs, emit):
        face_copy(1, 0, ls, rs).wait()
        face_copy(1, 1, ls, rs).wait()
        for t in range(2):
            total = field(acc.at[ls], t)
            h = [[None, None], [None, None]]
            q = [[None, None], [None, None]]
            for ri in range(2):
                for a in range(2):
                    came, back = recvz[rs, 0, ri, a], recvz[rs, 1, ri, a]
                    if t == 0:
                        came = pltpu.roll(came, 1, 1)
                    else:
                        back = pltpu.roll(back, 7, 1)
                    h[ri][a] = jnp.where(even, hz[ls, ri, a, :, t], came)
                    q[ri][a] = jnp.where(even, back, qz[ls, ri, a, :, t])
            rebuild(total, link_mul(links, 2, t, h, False), 2, -1.0)
            rebuild(total, q, 2, 1.0)
            keep(acc.at[ls], t, total)
        face_copy(0, 0, ls, rs).wait()
        face_copy(0, 1, ls, rs).wait()
        for ri in range(2):
            for a in range(2):
                for t in range(2):
                    j = 2 * (2 * a + t)
                    hx[ls, ri, a, :, t, 6:8, :] = recvx[rs, 0, 3 * ri:3 * ri + 3, j:j + 2, :]
                    qx[ls, ri, a, :, t, 0:2, :] = recvx[rs, 1, 3 * ri:3 * ri + 3, j:j + 2, :]
        for t in range(2):
            total = field(acc.at[ls], t)
            h = [[hx[ls, ri, a, :, t] for a in range(2)] for ri in range(2)]
            rebuild(total, link_mul(links, 0, t, h, False), 0, -1.0)
            rebuild(total, [[qx[ls, ri, a, :, t] for a in range(2)] for ri in range(2)], 0, 1.0)
            keep(acc.at[ls], t, total)
        face_copy(2, 0, ls, rs).wait()
        face_copy(2, 1, ls, rs).wait()
        for t in range(2):
            total = field(acc.at[ls], t)
            if t == 0:
                rebuild(total, [[recvt[rs, 1, ri, a] for a in range(2)] for ri in range(2)], 3, 1.0)
            else:
                h = [[recvt[rs, 0, ri, a] for a in range(2)] for ri in range(2)]
                rebuild(total, link_mul(links, 3, 1, h, False), 3, -1.0)
            emit(t, total)

    def advance(k):
        alpha = jnp.float32(ALPHA[0])
        beta = jnp.float32(BETA[0])
        for at in range(1, 2 * DEG):
            alpha = jnp.where(k == at, jnp.float32(ALPHA[at]), alpha)
            beta = jnp.where(k == at, jnp.float32(BETA[at]), beta)

        def emit(t, total):
            for ri in range(2):
                for s in range(4):
                    left = r[ri, s, :, t] - total[ri][s]
                    step = alpha * p[ri, s, :, t] + beta * left
                    r[ri, s, :, t] = left
                    p[ri, s, :, t] = step
                    u[ri, s, :, t] = u[ri, s, :, t] + step

        return emit

    def round_of(k, hooks):
        slot = lax.rem(k, 2)
        start(p, 0, slot)
        for at, hook in hooks:
            pl.when(k == at)(hook)
        finish(0, slot, advance(k))

    def first_half(k, carry):
        round_of(k, ((0, build_null), (1, build_null_transposed), (2, build_coarse)))
        return carry

    def second_half(k, carry):
        round_of(k, ())
        return carry

    for d in range(3):
        low_copy(d).start()
    lax.fori_loop(0, DEG, first_half, 0)

    diagonal = (iota((192, 256), 0) & 7) == (iota((192, 256), 1) & 7)
    selector = jnp.where(
        ((lane8 >> 5) == (row8 & 3)) & (((lane8 & 7) >> 2) == (row8 >> 2)), 1.0, 0.0).astype(F32)
    fold = jnp.where((iota((32, 192), 1) >> 3) == iota((32, 192), 0), 1.0, 0.0).astype(F32)
    unfold = jnp.where((iota((192, 32), 0) >> 3) == iota((192, 32), 1), 1.0, 0.0).astype(F32)
    both = jnp.concatenate([r[0].reshape(192, 128), r[1].reshape(192, 128)], axis=1)
    prod = dot(nvt[...], both)
    real = prod[0:192, 0:128] + prod[192:384, 128:256]
    imag = prod[0:192, 128:256] - prod[192:384, 0:128]
    kept = jnp.where(diagonal, jnp.concatenate([real, imag], axis=1), 0.0)
    summed = dot(fold, kept)
    stacked = jnp.concatenate([summed[:, 0:128], summed[:, 128:256]] * 2, axis=0)
    basis[0] = dot(selector, stacked, ((1,), (1,)))

    def coarse_copy(step, d, side):
        axis = AXES[d][1]
        return pltpu.make_async_remote_copy(
            src_ref=basis.at[step], dst_ref=crecv.at[step, 2 * d + side], send_sem=csend.at[step, 2 * d + side],
            recv_sem=crsem.at[step, 2 * d + side], device_id={axis: moved(axis, 2 * side - 1)},
            device_id_type=MESH)

    low_half = lane8 < 64

    def prolong(step):
        spread = dot(basis[step], selector, ((0,), (0,)))
        paired = jnp.concatenate([spread[0:32], spread[32:64]], axis=1)
        weights = jnp.where(diagonal, dot(unfold, paired), 0.0)
        prod = dot(nv[...].reshape(384, 192), weights)
        fields[step, 0] = (prod[0:192, 0:128] - prod[192:384, 128:256]).reshape(4, 3, 2, 8, 128)
        fields[step, 1] = (prod[0:192, 128:256] + prod[192:384, 0:128]).reshape(4, 3, 2, 8, 128)

    def into(index):
        return lambda t, total: keep(fields.at[index], t, total)

    def finish_first(step):
        finish(lax.rem(step, 2), 2 + step, into(5 + step))

    def finish_second(step):
        finish(2 + lax.rem(step, 2), 6 + step, into(9 + step))

    def start_second(step):
        start(fields.at[4 + step], 2 + lax.rem(step, 2), 6 + step)

    def coarse_step(step, carry):
        for d in (2, 0, 1):
            for side in range(2):
                coarse_copy(step, d, side).start()
        prolong(step)
        start(fields.at[step], lax.rem(step, 2), 2 + step)

        @pl.when(step >= 1)
        def _():
            finish_first(step - 1)
            finish_second(step - 1)

        start_second(step)

        own = basis[step]
        other = pltpu.roll(own, 4, 0)
        layer = row8 & 3
        from_below = jnp.where(layer == 0, -wall_mass * pltpu.roll(own, 5, 0), pltpu.roll(own, 1, 0))
        from_above = jnp.where(layer == 3, -wall_mass * pltpu.roll(own, 3, 0), pltpu.roll(own, 7, 0))
        local = (-coarse_fifth * basis_scale) * (from_below + from_above)
        for d in range(3):
            for side in range(2):
                coarse_copy(step, d, side).wait()
        got = [crecv[step, j] for j in range(6)]
        ahead = jnp.concatenate(
            [jnp.where(low_half, own, got[0]), jnp.where(low_half, got[2], got[4]), other], axis=1)
        behind = jnp.concatenate(
            [jnp.where(low_half, other, got[1]), jnp.where(low_half, got[3], got[5])], axis=1)
        out = dot(ahead, ff[...], ((1,), (1,))) + dot(behind, fb[...])
        out = jnp.where((row8 < 4) == low_half, out, pltpu.roll(out, 64, 1))
        basis[step + 1] = out + local
        return carry

    lax.fori_loop(0, CITERS, coarse_step, 0)

    size = CITERS + 1
    vectors = [basis[i] for i in range(size)]
    sign = jnp.where((lane8 & 32) == 0, 1.0, -1.0).astype(F32)
    turned = [sign * pltpu.roll(v, 32, 1) for v in vectors]
    entries = [(i, j, 0) for i in range(size) for j in range(i, size)]
    entries += [(i, j, 1) for i in range(size) for j in range(i + 1, size)]
    none = jnp.zeros((8, 128), F32)
    products = [vectors[i] * (vectors[j] if part == 0 else turned[j]) for i, j, part in entries]
    products = jnp.stack(products + [none] * (32 - len(products)))
    rows = jnp.sum(jnp.where(low_half[None], products, 0.0), axis=1)
    padded = jnp.concatenate([rows, jnp.zeros((96, 128), F32)], axis=0)
    sums = dot(jnp.ones((8, 128), F32), padded, ((1,), (1,)))

    def sum_copies(phase):
        return [pltpu.make_async_remote_copy(
            src_ref=ar_send.at[phase], dst_ref=ar_recv.at[phase, by], send_sem=asend.at[phase, by],
            recv_sem=arsem.at[phase, by], device_id=partner, device_id_type=MESH)
            for by, partner in enumerate(groups[phase])]

    def send_sums(phase, value):
        ar_send[phase] = value
        for copy in sum_copies(phase):
            copy.start()

    def take_sums(phase):
        parts = [ar_send[phase]]
        for by, copy in enumerate(sum_copies(phase)):
            copy.wait()
            parts.append(ar_recv[phase, by])
        while len(parts) > 1:
            parts = [parts[i] + parts[i + 1] if i + 1 < len(parts) else parts[i] for i in range(0, len(parts), 2)]
        return parts[0]

    send_sums(0, sums)
    finish_first(CITERS - 1)
    start_second(CITERS)
    finish_second(CITERS - 1)
    send_sums(1, take_sums(0))
    finish_second(CITERS)
    sums = take_sums(1)

    moments = [[None] * size for _ in range(size)]
    for number, (i, j, part) in enumerate(entries):
        value = jnp.broadcast_to(sums[:, number:number + 1], (8, 128))
        moments[i][j] = (value, none) if part == 0 else (moments[i][j][0], value)
    one = jnp.ones((8, 128), F32)
    coef = [(one, none)]
    answer = [(none, none)] * CITERS
    grow = 1.0 / basis_scale
    for step in range(CITERS):
        m00, m11 = moments[0][0][0], moments[1][1][0]
        m01r, m01i = moments[0][1]
        bottom = 1.0 / ((coarse_mass * coarse_mass) * m00 + (2.0 * coarse_mass * grow) * m01r + (grow * grow) * m11)
        ar = (coarse_mass * m00 + grow * m01r) * bottom
        ai = (-grow * m01i) * bottom
        for i, (cr, ci) in enumerate(coef):
            answer[i] = (answer[i][0] + (ar * cr - ai * ci), answer[i][1] + (ar * ci + ai * cr))
        kr, ki = 1.0 - coarse_mass * ar, -coarse_mass * ai
        dr, di = -grow * ar, -grow * ai
        kk, dd = kr * kr + ki * ki, dr * dr + di * di
        wr, wi = kr * dr + ki * di, kr * di - ki * dr
        fresh = [[None] * size for _ in range(size)]
        for m in range(size - 1 - step):
            for n in range(m, size - 1 - step):
                hr, hi = moments[m][n]
                nr, ni = moments[m][n + 1]
                fr, fi = moments[m + 1][n + 1]
                if m == n:
                    fresh[m][n] = ((kk * hr + dd * fr) + 2.0 * (wr * nr - wi * ni), none)
                else:
                    lr, li = moments[m + 1][n]
                    fresh[m][n] = ((kk * hr + dd * fr) + (wr * nr - wi * ni) + (wr * lr + wi * li),
                                   (kk * hi + dd * fi) + (wr * ni + wi * nr) + (wr * li - wi * lr))
        moments = fresh
        grown = [(kr * cr - ki * ci, kr * ci + ki * cr) for cr, ci in coef] + [(none, none)]
        for i, (cr, ci) in enumerate(coef):
            gr, gi = grown[i + 1]
            grown[i + 1] = (gr + (dr * cr - di * ci), gi + (dr * ci + di * cr))
        coef = grown

    alpha, beta = PAIRS[0]
    for t in range(2):
        for s in range(4):
            parts = [[fields[4, ri, s, :, t], fields[9, ri, s, :, t], u[ri, s, :, t]] for ri in range(2)]
            for i in range(CITERS):
                cr, ci = answer[i][0][None], answer[i][1][None]
                for part, at in ((0, 5 + i), (1, 10 + i), (2, i)):
                    fr, fi = fields[at, 0, s, :, t], fields[at, 1, s, :, t]
                    re, im = cr * fr - ci * fi, cr * fi + ci * fr
                    parts[0][part] = plus(parts[0][part], re, 1.0 if part == 2 else -1.0)
                    parts[1][part] = plus(parts[1][part], im, 1.0 if part == 2 else -1.0)
            for ri in range(2):
                left, through, result = parts[ri]
                step = START * left
                left = left - START * through
                after = alpha * step + beta * left
                r[ri, s, :, t] = left
                p[ri, s, :, t] = after
                u[ri, s, :, t] = result + step + after

    found = none
    for i in range(CITERS):
        found = found + (answer[i][0] * vectors[i] - answer[i][1] * turned[i])
    for ri in range(2):
        part = found if ri == 0 else pltpu.roll(found, 96, 1)
        for c in range(4):
            for y in range(2):
                at = 8 * ri + 2 * c + y
                e_out[at:at + 1, :] = part[4 * y + c:4 * y + c + 1, 0:24]

    lax.fori_loop(DEG + 2, 2 * DEG, second_half, 0)
    for t in range(2):
        for x in range(4):
            u_out[:, 4 * x + 2 * t:4 * x + 2 * t + 2, :] = u[:, :, :, t, 2 * x:2 * x + 2, :].reshape(24, 2, 128)


def body(sizes, source_field, gauge_links, null_vectors, coarse_links):
    hbm = pl.BlockSpec(memory_space=pl.ANY)
    vmem = pl.BlockSpec(memory_space=pltpu.VMEM)
    half = (4, 2, 2, 3, 2, 8, 128)
    full = (2, 4, 3, 2, 8, 128)
    most = max(sizes["ta"], sizes["grp"] * sizes["gz"]) - 1
    arguments = [(24, 16, 128), (72, 16, 8), (24, 4, 2, 2, 192), (480, 24)]
    shapes = arguments + [full, full, (14,) + full, (4,) + full, (4, 2, 3, 3, 2, 8, 128), (72, 2, 8, 8),
                          half, half, half, half, (4, 2, 2, 3, 8, 128), (4, 2, 2, 3, 8, 128),
                          (4, 2, 6, 8, 128), (4, 2, 2, 2, 3, 8, 128), (4, 2, 2, 2, 3, 8, 128),
                          (11, 2, 6, 8, 128), (11, 2, 2, 2, 3, 8, 128), (11, 2, 2, 2, 3, 8, 128),
                          (24, 2, 8, 192), (384, 192), (3, 96, 24), (128, 384), (256, 128), (CITERS + 1, 8, 128),
                          (CITERS, 6, 8, 128), (2, 8, 128), (2, most, 8, 128)]
    sems = [(4,), (4, 6), (11, 6), (3,), (3,), (CITERS, 6), (CITERS, 6), (2, most), (2, most)]
    out, found = pl.pallas_call(
        functools.partial(kernel, sizes),
        out_shape=(jax.ShapeDtypeStruct((24, 16, 128), F32), jax.ShapeDtypeStruct((16, 24), F32)),
        in_specs=[hbm] * 4,
        out_specs=(vmem, vmem),
        scratch_shapes=[pltpu.VMEM(shape, F32) for shape in shapes]
        + [pltpu.SemaphoreType.DMA(shape) for shape in sems],
        compiler_params=pltpu.CompilerParams(
            collective_id=0, has_side_effects=True, vmem_limit_bytes=56 * 1024 * 1024),
    )(
        source_field.reshape(arguments[0]),
        gauge_links.reshape(arguments[1]),
        null_vectors.reshape(arguments[2]),
        coarse_links.transpose(0, 1, 2, 4, 5, 6, 7, 3).reshape(arguments[3]),
    )
    found = found.reshape(2, 4, 2, 24).transpose(0, 3, 1, 2)
    return out.reshape(source_field.shape), found.reshape(2, 24, 4, 1, 1, 1, 2)


def solution(mesh):
    sizes = {axis: mesh.shape[axis] for axis in ("grp", "ta", "gz")}
    placed = (
        P(None, None, None, "grp", "ta", "gz", None),
        P(None, None, None, None, "grp", "ta", "gz", None),
        P(None, None, None, "grp", "ta", "gz", None),
        P(None, None, None, None, "grp", "ta", "gz", None),
    )
    return jax.shard_map(
        functools.partial(body, sizes),
        mesh=mesh,
        in_specs=placed,
        out_specs=(
            P(None, None, None, "grp", "ta", "gz", None),
            P(None, None, None, "grp", "ta", "gz", None),
        ),
        check_vma=False,
    )
```

```python
import functools

import jax
import jax.numpy as jnp
from jax import lax
from jax.experimental import pallas as pl
from jax.experimental.pallas import tpu as pltpu
from jax.sharding import PartitionSpec as P

MESH = pl.DeviceIdType.MESH
F32 = jnp.float32

site_mass = 2.0
hop_kappa = 0.1
fifth_hop = 0.4
wall_mass = 0.1
cheb_lower = 0.6
cheb_upper = 3.4
coarse_mass = 3.0
coarse_fifth = 0.3
basis_scale = 0.125
DEG = 4
CITERS = 4
gamma_table = (
    ((3, 0.0, 1.0), (2, 0.0, 1.0)),
    ((3, -1.0, 0.0), (2, 1.0, 0.0)),
    ((2, 0.0, 1.0), (3, 0.0, -1.0)),
    ((2, 1.0, 0.0), (3, 1.0, 0.0)),
)
AXES = ((0, "grp"), (2, "gz"), (3, "ta"))
COARSE_DIRS = (1, 3, 4)


def cheb_coefficients():
    centre = 0.5 * (cheb_upper + cheb_lower)
    half_width = 0.5 * (cheb_upper - cheb_lower)
    spread_ratio = centre / half_width
    ratio_now = 1.0 / spread_ratio
    pairs = []
    for _ in range(DEG - 1):
        ratio_next = 1.0 / (2.0 * spread_ratio - ratio_now)
        pairs.append((ratio_next * ratio_now, 2.0 * ratio_next / half_width))
        ratio_now = ratio_next
    return 1.0 / centre, pairs


START, PAIRS = cheb_coefficients()
ALPHA = [pair[0] for pair in PAIRS] + [0.0, 0.0] + [pair[0] for pair in PAIRS]
BETA = [pair[1] for pair in PAIRS] + [0.0, START] + [pair[1] for pair in PAIRS]


def plus(a, b, sign):
    return a + b if sign > 0 else a - b


def project(v, mu, f):
    real, imag = [], []
    for a in range(2):
        b, gr, gi = gamma_table[mu][a]
        if gr != 0.0:
            real.append(plus(v[0][a], v[0][b], f * gr))
            imag.append(plus(v[1][a], v[1][b], f * gr))
        else:
            real.append(plus(v[0][a], v[1][b], -f * gi))
            imag.append(plus(v[1][a], v[0][b], f * gi))
    return [real, imag]


def rebuild(acc, h, mu, f):
    for a in range(2):
        b, gr, gi = gamma_table[mu][a]
        acc[0][a] = acc[0][a] + h[0][a]
        acc[1][a] = acc[1][a] + h[1][a]
        if gr != 0.0:
            acc[0][b] = plus(acc[0][b], h[0][a], f * gr)
            acc[1][b] = plus(acc[1][b], h[1][a], f * gr)
        else:
            acc[0][b] = plus(acc[0][b], h[1][a], f * gi)
            acc[1][b] = plus(acc[1][b], h[0][a], -f * gi)


def link_mul(links, mu, t, h, dagger):
    out = [[None, None], [None, None]]
    for col in range(3):
        if dagger:
            lr, li = links[mu, 0, col, :, t], links[mu, 1, col, :, t]
        else:
            lr, li = links[mu, 0, :, col, t], links[mu, 1, :, col, t]
        for a in range(2):
            hr, hi = h[0][a][col][None], h[1][a][col][None]
            if dagger:
                re, im = lr * hr + li * hi, lr * hi - li * hr
            else:
                re, im = lr * hr - li * hi, lr * hi + li * hr
            out[0][a] = re if col == 0 else out[0][a] + re
            out[1][a] = im if col == 0 else out[1][a] + im
    return out


def each(fn, h):
    return [[fn(h[ri][a]) for a in range(2)] for ri in range(2)]


def dot(a, b, dims=((1,), (0,))):
    return lax.dot_general(
        a, b, (dims, ((), ())), precision=lax.Precision.HIGHEST, preferred_element_type=F32
    )


def halves(a):
    high = a.astype(jnp.bfloat16)
    return high, (a - high.astype(F32)).astype(jnp.bfloat16)


def dot_halves(a, b):
    return sum(jnp.dot(a[i], b[j], preferred_element_type=F32) for i, j in ((1, 0), (0, 1), (0, 0)))


def pick(ones, b):
    ones = ones.astype(jnp.bfloat16)
    high, low = halves(b)
    return jnp.dot(ones, low, preferred_element_type=F32) + jnp.dot(ones, high, preferred_element_type=F32)


def iota(shape, dim):
    return lax.broadcasted_iota(jnp.int32, shape, dim)


def wrap(sizes, disp):
    return tuple(by % sizes[axis] for by, (_, axis) in zip(disp, AXES))


STENCIL = (((0, 0, 0), 0), ((0, 0, 0), 1), ((1, 0, 0), 0), ((-1, 0, 0), 0),
           ((0, 1, 0), 0), ((0, -1, 0), 0), ((0, 0, 1), 0), ((0, 0, -1), 0))
CHUNKS = ((0, 4), (4, 8))


def reach(sizes):
    keys = []
    for first, flip in STENCIL:
        for second, again in STENCIL:
            key = (wrap(sizes, [i + j for i, j in zip(first, second)]), flip ^ again)
            if key not in keys:
                keys.append(key)
    far = []
    for disp, _ in keys:
        if any(disp) and disp not in far:
            far.append(disp)
    return keys, far


def kernel(sizes, src_in, gauge_in, null_in, coarse_in, u_out, e_out, src, gauge, null, coarse, p, u, fields, acc, links, g8,
           hx, qx, hz, qz, ht, qt, sendx, sendz, sendt, recvx, recvz, recvt, nv, nvs, nvt, low, ff, fb, wide, rows24, wrecv,
           twice, basis, crecv, ar_send, ar_recv, isem, fsend, frecv, lsend, lrecv, wsend, wrsem, csend, crsem, asend, arsem):
    keys, far = reach(sizes)
    me = {axis: lax.axis_index(axis) for axis in ("grp", "ta", "gz")}
    plane = sizes["grp"] * sizes["gz"]
    spot = me["grp"] * sizes["gz"] + me["gz"]

    def moved(axis, by):
        return lax.rem(me[axis] + (by + sizes[axis]), sizes[axis])

    def in_plane(by):
        other = lax.rem(spot + by, plane)
        return {"grp": lax.div(other, sizes["gz"]), "gz": lax.rem(other, sizes["gz"])}

    groups = ([{"ta": moved("ta", by)} for by in range(1, sizes["ta"])], [in_plane(by) for by in range(1, plane)])

    def at(disp):
        return {axis: moved(axis, by) for by, (_, axis) in zip(disp, AXES)}

    def back(disp):
        return at(wrap(sizes, [-by for by in disp]))

    barrier = pltpu.get_barrier_semaphore()
    partners = [at(disp) for disp, _ in STENCIL if any(disp)]
    for partner in partners:
        pl.semaphore_signal(barrier, inc=1, device_id=partner, device_id_type=MESH)

    loads = [pltpu.make_async_copy(a, b, isem.at[i]) for i, (a, b) in enumerate(
        ((gauge_in, gauge), (src_in, src), (coarse_in, coarse), (null_in, null)))]
    for load in loads:
        load.start()

    r = fields.at[4]

    loads[0].wait()
    for t in range(2):
        for x in range(4):
            g8[:, t, 2 * x:2 * x + 2, :] = gauge[:, 4 * x + 2 * t:4 * x + 2 * t + 2, :]
    spread_y = jnp.where((iota((8, 128), 1) & 7) == iota((8, 128), 0), 1.0, 0.0).astype(F32)
    tiled = dot(g8[...].reshape(72 * 16, 8), spread_y) * (-hop_kappa)
    links[...] = tiled.reshape(4, 2, 3, 3, 2, 8, 128)
    loads[1].wait()
    for t in range(2):
        for x in range(4):
            rows = src[:, 4 * x + 2 * t:4 * x + 2 * t + 2, :].reshape(2, 4, 3, 2, 128)
            r[:, :, :, t, 2 * x:2 * x + 2, :] = rows
            p[:, :, :, t, 2 * x:2 * x + 2, :] = rows * START
            u[:, :, :, t, 2 * x:2 * x + 2, :] = rows * START
    loads[2].wait()

    pl.semaphore_wait(barrier, len(partners))

    def low_copy(d):
        return pltpu.make_async_remote_copy(
            src_ref=coarse.at[pl.ds(COARSE_DIRS[d] * 96, 96)], dst_ref=low.at[d], send_sem=lsend.at[d],
            recv_sem=lrecv.at[d], device_id={AXES[d][1]: moved(AXES[d][1], 1)}, device_id_type=MESH)

    row8 = iota((8, 128), 0)
    lane8 = iota((8, 128), 1)

    def face_copy(d, side, ls, rs):
        out, into = ((sendx, recvx), (sendz, recvz), (sendt, recvt))[d]
        axis = AXES[d][1]
        return pltpu.make_async_remote_copy(
            src_ref=out.at[ls, side], dst_ref=into.at[rs, side], send_sem=fsend.at[ls, 2 * d + side],
            recv_sem=frecv.at[rs, 2 * d + side], device_id={axis: moved(axis, 2 * side - 1)},
            device_id_type=MESH)

    def field(ref, t):
        return [[ref[ri, s, :, t] for s in range(4)] for ri in range(2)]

    def keep(ref, t, total):
        for ri in range(2):
            for s in range(4):
                ref[ri, s, :, t] = total[ri][s]

    def build_null():
        loads[3].wait()
        for t in range(2):
            for x in range(4):
                nv[:, t, 2 * x:2 * x + 2, :] = null[:, x, t]

    def build_null_transposed():
        for ri in range(2):
            half = nv[12 * ri:12 * ri + 12].reshape(192, 192)
            for part, value in enumerate(halves(half)):
                nvs[part, 192 * ri:192 * ri + 192, :] = value
            for part, value in enumerate(halves(half.T)):
                nvt[part, 192 * ri:192 * ri + 192, :] = value

    def build_coarse():
        for d in range(3):
            low_copy(d).wait()
        ff[...] = jnp.zeros_like(ff)
        fb[...] = jnp.zeros_like(fb)
        zero = jnp.zeros((24, 104), F32)

        def piece(ref, base, y):
            return jnp.concatenate([ref[pl.ds(base + y, 24, stride=2), :] * basis_scale, zero], axis=1)

        def placed(value, at):
            return value if at == 0 else pltpu.roll(value, at, 1)

        for y in range(2):
            blocks = []
            for direction in (0, 1, 3, 4, 2):
                blocks.append([piece(coarse, direction * 96 + ri * 48, y) for ri in range(2)])
            for ro in range(2):
                for tile in range(3):
                    total = None
                    for j in range(2):
                        if 2 * tile + j > 4:
                            continue
                        mr, mi = blocks[2 * tile + j]
                        first, second = (mr, -mi) if ro == 0 else (mi, mr)
                        part = placed(first, 64 * j) + placed(second, 64 * j + 32)
                        total = part if total is None else total + part
                    ff[64 * y + 32 * ro:64 * y + 32 * ro + 24, 128 * tile:128 * tile + 128] = total
        for block in range(4):
            parts = []
            for y in range(2):
                if block == 0:
                    parts.append([piece(coarse, 2 * 96 + ri * 48, 1 - y) for ri in range(2)])
                else:
                    parts.append([piece(low.at[block - 1], ri * 48, y) for ri in range(2)])
            for ri in range(2):
                total = None
                for y in range(2):
                    mr, mi = parts[y]
                    first, second = (mr, -mi) if ri == 0 else (mi, mr)
                    part = placed(first, 64 * y) + placed(second, 64 * y + 32)
                    total = part if total is None else total + part
                fb[64 * block + 32 * ri:64 * block + 32 * ri + 24, :] = total
        flat = ff[...].T
        order = (flat[0:64], flat[256:320] + fb[0:64], flat[64:128], fb[64:128], flat[128:192], fb[128:192],
                 flat[192:256], fb[192:256])
        for block, rows in enumerate(order):
            wide[64 * block:64 * block + 64, :] = rows
            rows24[block] = rows[0:24]

    def row_copy(block, chunk):
        first, last = CHUNKS[chunk]
        return pltpu.make_async_remote_copy(
            src_ref=rows24.at[first:last], dst_ref=wrecv.at[block - 2, first:last], send_sem=wsend.at[block - 2, chunk],
            recv_sem=wrsem.at[block - 2, chunk], device_id=back(STENCIL[block][0]), device_id_type=MESH)

    def send_rows(chunk):
        def send():
            for block in range(2, 8):
                row_copy(block, chunk).start()

        return send

    def build_null_and_send():
        send_rows(0)()
        build_null_transposed()

    def build_twice():
        twice[...] = jnp.zeros_like(twice)
        for block, (disp, flip) in enumerate(STENCIL):
            if block >= 2:
                for chunk in range(len(CHUNKS)):
                    row_copy(block, chunk).wait()
            mine = wide[64 * block:64 * block + 64, :]
            left = iota((64, 128), 1) < 64
            upper, lower = jnp.where(left, mine, 0.0), jnp.where(left, 0.0, mine)
            weights = jnp.concatenate([lower, upper] if flip else [upper, lower], axis=0)
            theirs = rows24[...] if block < 2 else wrecv[block - 2]
            product = dot(theirs.reshape(8 * 24, 128), weights)
            real_lane = (iota((8 * 24, 128), 1) & 32) == 0
            turned = jnp.where(real_lane, -pltpu.roll(product, 96, 1), pltpu.roll(product, 32, 1))
            for other, (further, again) in enumerate(STENCIL):
                key = (wrap(sizes, [i + j for i, j in zip(disp, further)]), flip ^ again)
                base = 64 * keys.index(key)
                for ri, part in ((0, product), (1, turned)):
                    twice[base + 32 * ri:base + 32 * ri + 24, :] += part[24 * other:24 * other + 24]

    even = (iota((3, 8, 128), 1) & 1) == 0

    def start(f, ls, rs):
        v = field(f, 0)
        down = project(v, 3, -1.0)
        own_up = link_mul(links, 3, 0, project(v, 3, 1.0), True)
        v = field(f, 1)
        own_down = project(v, 3, -1.0)
        up = link_mul(links, 3, 1, project(v, 3, 1.0), True)
        for ri in range(2):
            for a in range(2):
                sendt[ls, 0, ri, a] = down[ri][a]
                sendt[ls, 1, ri, a] = up[ri][a]
                ht[ls, ri, a] = own_down[ri][a]
                qt[ls, ri, a] = own_up[ri][a]
        face_copy(2, 0, ls, rs).start()
        face_copy(2, 1, ls, rs).start()
        for t in range(2):
            v = field(f, t)
            down = project(v, 0, -1.0)
            up = link_mul(links, 0, t, project(v, 0, 1.0), True)
            for ri in range(2):
                for a in range(2):
                    j = 2 * (2 * a + t)
                    sendx[ls, 0, 3 * ri:3 * ri + 3, j:j + 2, :] = down[ri][a][:, 0:2]
                    sendx[ls, 1, 3 * ri:3 * ri + 3, j:j + 2, :] = up[ri][a][:, 6:8]
                    hx[ls, ri, a, :, t] = pltpu.roll(down[ri][a], 6, 1)
                    qx[ls, ri, a, :, t] = pltpu.roll(up[ri][a], 2, 1)
        face_copy(0, 0, ls, rs).start()
        face_copy(0, 1, ls, rs).start()
        downs, ups = [], []
        for t in range(2):
            v = field(f, t)
            downs.append(project(v, 2, -1.0))
            ups.append(link_mul(links, 2, t, project(v, 2, 1.0), True))
        for ri in range(2):
            for a in range(2):
                for t in range(2):
                    hz[ls, ri, a, :, t] = pltpu.roll(downs[t][ri][a], 7, 1)
                    qz[ls, ri, a, :, t] = pltpu.roll(ups[t][ri][a], 1, 1)
                sendz[ls, 0, ri, a] = jnp.where(even, downs[0][ri][a], pltpu.roll(downs[1][ri][a], 1, 1))
                sendz[ls, 1, ri, a] = jnp.where(even, pltpu.roll(ups[0][ri][a], 7, 1), ups[1][ri][a])
        face_copy(1, 0, ls, rs).start()
        face_copy(1, 1, ls, rs).start()

        lane = iota((3, 8, 128), 2)
        ypos = lane & 7
        below = jnp.where(lane < 8, fifth_hop * wall_mass, -fifth_hop).astype(F32)
        above = jnp.where(lane >= 120, fifth_hop * wall_mass, -fifth_hop).astype(F32)
        for t in range(2):
            v = field(f, t)
            total = [[None] * 4, [None] * 4]
            for ri in range(2):
                for s in range(4):
                    if s < 2:
                        side = below * pltpu.roll(v[ri][s], 8, 2)
                    else:
                        side = above * pltpu.roll(v[ri][s], 120, 2)
                    total[ri][s] = site_mass * v[ri][s] + side
            h = each(lambda w: jnp.where(ypos == 7, pltpu.roll(w, 7, 2), pltpu.roll(w, 127, 2)), project(v, 1, -1.0))
            rebuild(total, link_mul(links, 1, t, h, False), 1, -1.0)
            h = link_mul(links, 1, t, project(v, 1, 1.0), True)
            h = each(lambda w: jnp.where(ypos == 0, pltpu.roll(w, 121, 2), pltpu.roll(w, 1, 2)), h)
            rebuild(total, h, 1, 1.0)
            if t == 0:
                h = [[ht[ls, ri, a] for a in range(2)] for ri in range(2)]
                rebuild(total, link_mul(links, 3, 0, h, False), 3, -1.0)
            else:
                rebuild(total, [[qt[ls, ri, a] for a in range(2)] for ri in range(2)], 3, 1.0)
            keep(acc.at[ls], t, total)

    def finish(ls, rs, emit):
        face_copy(1, 0, ls, rs).wait()
        face_copy(1, 1, ls, rs).wait()
        for t in range(2):
            total = field(acc.at[ls], t)
            h = [[None, None], [None, None]]
            q = [[None, None], [None, None]]
            for ri in range(2):
                for a in range(2):
                    came, back = recvz[rs, 0, ri, a], recvz[rs, 1, ri, a]
                    if t == 0:
                        came = pltpu.roll(came, 1, 1)
                    else:
                        back = pltpu.roll(back, 7, 1)
                    h[ri][a] = jnp.where(even, hz[ls, ri, a, :, t], came)
                    q[ri][a] = jnp.where(even, back, qz[ls, ri, a, :, t])
            rebuild(total, link_mul(links, 2, t, h, False), 2, -1.0)
            rebuild(total, q, 2, 1.0)
            keep(acc.at[ls], t, total)
        face_copy(0, 0, ls, rs).wait()
        face_copy(0, 1, ls, rs).wait()
        for ri in range(2):
            for a in range(2):
                for t in range(2):
                    j = 2 * (2 * a + t)
                    hx[ls, ri, a, :, t, 6:8, :] = recvx[rs, 0, 3 * ri:3 * ri + 3, j:j + 2, :]
                    qx[ls, ri, a, :, t, 0:2, :] = recvx[rs, 1, 3 * ri:3 * ri + 3, j:j + 2, :]
        for t in range(2):
            total = field(acc.at[ls], t)
            h = [[hx[ls, ri, a, :, t] for a in range(2)] for ri in range(2)]
            rebuild(total, link_mul(links, 0, t, h, False), 0, -1.0)
            rebuild(total, [[qx[ls, ri, a, :, t] for a in range(2)] for ri in range(2)], 0, 1.0)
            keep(acc.at[ls], t, total)
        face_copy(2, 0, ls, rs).wait()
        face_copy(2, 1, ls, rs).wait()
        for t in range(2):
            total = field(acc.at[ls], t)
            if t == 0:
                rebuild(total, [[recvt[rs, 1, ri, a] for a in range(2)] for ri in range(2)], 3, 1.0)
            else:
                h = [[recvt[rs, 0, ri, a] for a in range(2)] for ri in range(2)]
                rebuild(total, link_mul(links, 3, 1, h, False), 3, -1.0)
            emit(t, total)

    def advance(k):
        alpha = jnp.float32(ALPHA[0])
        beta = jnp.float32(BETA[0])
        for at in range(1, 2 * DEG):
            alpha = jnp.where(k == at, jnp.float32(ALPHA[at]), alpha)
            beta = jnp.where(k == at, jnp.float32(BETA[at]), beta)

        def emit(t, total):
            for ri in range(2):
                for s in range(4):
                    left = r[ri, s, :, t] - total[ri][s]
                    step = alpha * p[ri, s, :, t] + beta * left
                    r[ri, s, :, t] = left
                    p[ri, s, :, t] = step
                    u[ri, s, :, t] = u[ri, s, :, t] + step

        return emit

    def round_of(k, hooks):
        slot = lax.rem(k, 2)
        start(p, 0, slot)
        for at, hook in hooks:
            pl.when(k == at)(hook)
        finish(0, slot, advance(k))

    def first_half(k, carry):
        round_of(k, ((0, build_null), (1, build_coarse), (2, build_null_and_send), (3, send_rows(1))))
        return carry

    def second_half(k, carry):
        round_of(k, ())
        return carry

    for d in range(3):
        low_copy(d).start()
    lax.fori_loop(0, DEG, first_half, 0)

    diagonal = (iota((192, 256), 0) & 7) == (iota((192, 256), 1) & 7)
    selector = jnp.where(
        ((lane8 >> 5) == (row8 & 3)) & (((lane8 & 7) >> 2) == (row8 >> 2)), 1.0, 0.0).astype(F32)
    fold = jnp.where((iota((32, 192), 1) >> 3) == iota((32, 192), 0), 1.0, 0.0).astype(F32)
    unfold = jnp.where((iota((192, 32), 0) >> 3) == iota((192, 32), 1), 1.0, 0.0).astype(F32)
    both = jnp.concatenate([r[0].reshape(192, 128), r[1].reshape(192, 128)], axis=1)
    prod = dot_halves((nvt[0], nvt[1]), halves(both))
    real = prod[0:192, 0:128] + prod[192:384, 128:256]
    imag = prod[0:192, 128:256] - prod[192:384, 0:128]
    kept = jnp.where(diagonal, jnp.concatenate([real, imag], axis=1), 0.0)
    summed = pick(fold, kept)
    stacked = jnp.concatenate([summed[:, 0:128], summed[:, 128:256]] * 2, axis=0)
    basis[0] = dot(selector, stacked, ((1,), (1,)))

    def coarse_copies(step):
        return [pltpu.make_async_remote_copy(
            src_ref=basis.at[2 * step], dst_ref=crecv.at[step, i], send_sem=csend.at[step, i],
            recv_sem=crsem.at[step, i], device_id=back(disp), device_id_type=MESH)
            for i, disp in enumerate(far)]

    low_half = lane8 < 64

    def prolong(step):
        spread = dot(basis[step], selector, ((0,), (0,)))
        paired = jnp.concatenate([spread[0:32], spread[32:64]], axis=1)
        weights = jnp.where(diagonal, pick(unfold, paired), 0.0)
        prod = dot_halves((nvs[0], nvs[1]), halves(weights))
        fields[step, 0] = (prod[0:192, 0:128] - prod[192:384, 128:256]).reshape(4, 3, 2, 8, 128)
        fields[step, 1] = (prod[0:192, 128:256] + prod[192:384, 0:128]).reshape(4, 3, 2, 8, 128)

    def begin(f):
        start(fields.at[f], 1 + f, 2 + f)

    def end(f):
        finish(1 + f, 2 + f, lambda t, total: keep(fields.at[5 + f], t, total))

    def across(own):
        layer = row8 & 3
        from_below = jnp.where(layer == 0, -wall_mass * pltpu.roll(own, 5, 0), pltpu.roll(own, 1, 0))
        from_above = jnp.where(layer == 3, -wall_mass * pltpu.roll(own, 3, 0), pltpu.roll(own, 7, 0))
        return (-coarse_fifth * basis_scale) * (from_below + from_above)

    def gathered(step, wanted):
        own = basis[2 * step]
        parts = []
        for disp, flip in wanted:
            disp = wrap(sizes, disp)
            part = crecv[step, far.index(disp)] if any(disp) else own
            parts.append(pltpu.roll(part, 4, 0) if flip else part)
        if len(parts) % 2:
            parts.append(own)
        return jnp.concatenate(
            [jnp.where(low_half, parts[i], parts[i + 1]) for i in range(0, len(parts), 2)], axis=1)

    def own_y(out):
        return jnp.where((row8 < 4) == low_half, out, pltpu.roll(out, 64, 1))

    def send_basis(step):
        for copy in coarse_copies(step):
            copy.start()

    def take_basis(step):
        for copy in coarse_copies(step):
            copy.wait()
        once = own_y(dot(gathered(step, STENCIL), wide[...]))
        shifted = across(basis[2 * step])
        basis[2 * step + 1] = once + shifted
        return 2.0 * once + shifted

    def take_second(step, first):
        again = own_y(dot(gathered(step, keys), twice[...]))
        basis[2 * step + 2] = again + across(first)

    send_basis(0)
    prolong(0)
    begin(0)
    begin(4)
    build_twice()
    take_second(0, take_basis(0))
    send_basis(1)

    def lift(f, carry):
        prolong(f)
        begin(f)
        return carry

    lax.fori_loop(1, 3, lift, 0)
    end(0)
    begin(5)
    end(4)
    first = take_basis(1)
    prolong(3)
    begin(3)
    take_second(1, first)

    size = CITERS + 1
    vectors = [basis[i] for i in range(size)]
    sign = jnp.where((lane8 & 32) == 0, 1.0, -1.0).astype(F32)
    turned = [sign * pltpu.roll(v, 32, 1) for v in vectors]
    entries = [(i, j, 0) for i in range(size) for j in range(i, size)]
    entries += [(i, j, 1) for i in range(size) for j in range(i + 1, size)]
    none = jnp.zeros((8, 128), F32)
    products = [vectors[i] * (vectors[j] if part == 0 else turned[j]) for i, j, part in entries]
    products = jnp.stack(products + [none] * (32 - len(products)))
    rows = jnp.sum(jnp.where(low_half[None], products, 0.0), axis=1)
    padded = jnp.concatenate([rows, jnp.zeros((96, 128), F32)], axis=0)
    sums = dot(jnp.ones((8, 128), F32), padded, ((1,), (1,)))

    def sum_copies(phase):
        return [pltpu.make_async_remote_copy(
            src_ref=ar_send.at[phase], dst_ref=ar_recv.at[phase, by], send_sem=asend.at[phase, by],
            recv_sem=arsem.at[phase, by], device_id=partner, device_id_type=MESH)
            for by, partner in enumerate(groups[phase])]

    def send_sums(phase, value):
        ar_send[phase] = value
        for copy in sum_copies(phase):
            copy.start()

    def take_sums(phase):
        parts = [ar_send[phase]]
        for by, copy in enumerate(sum_copies(phase)):
            copy.wait()
            parts.append(ar_recv[phase, by])
        while len(parts) > 1:
            parts = [parts[i] + parts[i + 1] if i + 1 < len(parts) else parts[i] for i in range(0, len(parts), 2)]
        return parts[0]

    send_sums(0, sums)

    def turn(f, carry):
        end(f)
        begin(5 + f)
        return carry

    def settle(f, carry):
        end(f)
        return carry

    lax.fori_loop(1, 3, turn, 0)
    end(5)
    send_sums(1, take_sums(0))
    end(3)
    begin(8)
    lax.fori_loop(6, 8, settle, 0)
    end(8)
    sums = take_sums(1)

    moments = [[None] * size for _ in range(size)]
    for number, (i, j, part) in enumerate(entries):
        value = jnp.broadcast_to(sums[:, number:number + 1], (8, 128))
        moments[i][j] = (value, none) if part == 0 else (moments[i][j][0], value)
    one = jnp.ones((8, 128), F32)
    coef = [(one, none)]
    answer = [(none, none)] * CITERS
    grow = 1.0 / basis_scale
    for step in range(CITERS):
        m00, m11 = moments[0][0][0], moments[1][1][0]
        m01r, m01i = moments[0][1]
        bottom = 1.0 / ((coarse_mass * coarse_mass) * m00 + (2.0 * coarse_mass * grow) * m01r + (grow * grow) * m11)
        ar = (coarse_mass * m00 + grow * m01r) * bottom
        ai = (-grow * m01i) * bottom
        for i, (cr, ci) in enumerate(coef):
            answer[i] = (answer[i][0] + (ar * cr - ai * ci), answer[i][1] + (ar * ci + ai * cr))
        kr, ki = 1.0 - coarse_mass * ar, -coarse_mass * ai
        dr, di = -grow * ar, -grow * ai
        kk, dd = kr * kr + ki * ki, dr * dr + di * di
        wr, wi = kr * dr + ki * di, kr * di - ki * dr
        fresh = [[None] * size for _ in range(size)]
        for m in range(size - 1 - step):
            for n in range(m, size - 1 - step):
                hr, hi = moments[m][n]
                nr, ni = moments[m][n + 1]
                fr, fi = moments[m + 1][n + 1]
                if m == n:
                    fresh[m][n] = ((kk * hr + dd * fr) + 2.0 * (wr * nr - wi * ni), none)
                else:
                    lr, li = moments[m + 1][n]
                    fresh[m][n] = ((kk * hr + dd * fr) + (wr * nr - wi * ni) + (wr * lr + wi * li),
                                   (kk * hi + dd * fi) + (wr * ni + wi * nr) + (wr * li - wi * lr))
        moments = fresh
        grown = [(kr * cr - ki * ci, kr * ci + ki * cr) for cr, ci in coef] + [(none, none)]
        for i, (cr, ci) in enumerate(coef):
            gr, gi = grown[i + 1]
            grown[i + 1] = (gr + (dr * cr - di * ci), gi + (dr * ci + di * cr))
        coef = grown

    alpha, beta = PAIRS[0]
    for t in range(2):
        for s in range(4):
            parts = [[fields[4, ri, s, :, t], fields[9, ri, s, :, t], u[ri, s, :, t]] for ri in range(2)]
            for i in range(CITERS):
                cr, ci = answer[i][0][None], answer[i][1][None]
                for part, at in ((0, 5 + i), (1, 10 + i), (2, i)):
                    fr, fi = fields[at, 0, s, :, t], fields[at, 1, s, :, t]
                    re, im = cr * fr - ci * fi, cr * fi + ci * fr
                    parts[0][part] = plus(parts[0][part], re, 1.0 if part == 2 else -1.0)
                    parts[1][part] = plus(parts[1][part], im, 1.0 if part == 2 else -1.0)
            for ri in range(2):
                left, through, result = parts[ri]
                step = START * left
                left = left - START * through
                after = alpha * step + beta * left
                r[ri, s, :, t] = left
                p[ri, s, :, t] = after
                u[ri, s, :, t] = result + step + after

    found = none
    for i in range(CITERS):
        found = found + (answer[i][0] * vectors[i] - answer[i][1] * turned[i])
    for ri in range(2):
        part = found if ri == 0 else pltpu.roll(found, 96, 1)
        for c in range(4):
            for y in range(2):
                at = 8 * ri + 2 * c + y
                e_out[at:at + 1, :] = part[4 * y + c:4 * y + c + 1, 0:24]

    lax.fori_loop(DEG + 2, 2 * DEG, second_half, 0)
    for t in range(2):
        for x in range(4):
            u_out[:, 4 * x + 2 * t:4 * x + 2 * t + 2, :] = u[:, :, :, t, 2 * x:2 * x + 2, :].reshape(24, 2, 128)


def body(sizes, source_field, gauge_links, null_vectors, coarse_links):
    hbm = pl.BlockSpec(memory_space=pl.ANY)
    vmem = pl.BlockSpec(memory_space=pltpu.VMEM)
    keys, far = reach(sizes)
    most_rows = 64 * (len(keys) + len(keys) % 2)
    half = (10, 2, 2, 3, 2, 8, 128)
    full = (2, 4, 3, 2, 8, 128)
    most = max(sizes["ta"], sizes["grp"] * sizes["gz"]) - 1
    arguments = [(24, 16, 128), (72, 16, 8), (24, 4, 2, 2, 192), (480, 24)]
    shapes = arguments + [full, full, (14,) + full, (10,) + full, (4, 2, 3, 3, 2, 8, 128), (72, 2, 8, 8),
                          half, half, half, half, (10, 2, 2, 3, 8, 128), (10, 2, 2, 3, 8, 128),
                          (10, 2, 6, 8, 128), (10, 2, 2, 2, 3, 8, 128), (10, 2, 2, 2, 3, 8, 128),
                          (11, 2, 6, 8, 128), (11, 2, 2, 2, 3, 8, 128), (11, 2, 2, 2, 3, 8, 128),
                          (24, 2, 8, 192), (2, 384, 192), (2, 384, 192), (3, 96, 24), (128, 384), (256, 128), (512, 128), (8, 24, 128), (6, 8, 24, 128),
                          (most_rows, 128), (CITERS + 1, 8, 128), (2, len(far), 8, 128), (2, 8, 128), (2, most, 8, 128)]
    sems = [(4,), (10, 6), (11, 6), (3,), (3,), (6, 2), (6, 2), (2, len(far)), (2, len(far)), (2, most), (2, most)]
    out, found = pl.pallas_call(
        functools.partial(kernel, sizes),
        out_shape=(jax.ShapeDtypeStruct((24, 16, 128), F32), jax.ShapeDtypeStruct((16, 24), F32)),
        in_specs=[hbm] * 4,
        out_specs=(vmem, vmem),
        scratch_shapes=[pltpu.VMEM(shape, jnp.bfloat16 if shape == (2, 384, 192) else F32) for shape in shapes]
        + [pltpu.SemaphoreType.DMA(shape) for shape in sems],
        compiler_params=pltpu.CompilerParams(
            collective_id=0, has_side_effects=True, vmem_limit_bytes=56 * 1024 * 1024),
    )(
        source_field.reshape(arguments[0]),
        gauge_links.reshape(arguments[1]),
        null_vectors.reshape(arguments[2]),
        coarse_links.transpose(0, 1, 2, 4, 5, 6, 7, 3).reshape(arguments[3]),
    )
    found = found.reshape(2, 4, 2, 24).transpose(0, 3, 1, 2)
    return out.reshape(source_field.shape), found.reshape(2, 24, 4, 1, 1, 1, 2)


def solution(mesh):
    sizes = {axis: mesh.shape[axis] for axis in ("grp", "ta", "gz")}
    placed = (
        P(None, None, None, "grp", "ta", "gz", None),
        P(None, None, None, None, "grp", "ta", "gz", None),
        P(None, None, None, "grp", "ta", "gz", None),
        P(None, None, None, None, "grp", "ta", "gz", None),
    )
    return jax.shard_map(
        functools.partial(body, sizes),
        mesh=mesh,
        in_specs=placed,
        out_specs=(
            P(None, None, None, "grp", "ta", "gz", None),
            P(None, None, None, "grp", "ta", "gz", None),
        ),
        check_vma=False,
    )
```

```python
import functools

import jax
import jax.numpy as jnp
from jax import lax
from jax.experimental import pallas as pl
from jax.experimental.pallas import tpu as pltpu
from jax.sharding import PartitionSpec as P

MESH = pl.DeviceIdType.MESH
F32 = jnp.float32

site_mass = 2.0
hop_kappa = 0.1
fifth_hop = 0.4
wall_mass = 0.1
cheb_lower = 0.6
cheb_upper = 3.4
coarse_mass = 3.0
coarse_fifth = 0.3
basis_scale = 0.125
DEG = 4
CITERS = 4
gamma_table = (
    ((3, 0.0, 1.0), (2, 0.0, 1.0)),
    ((3, -1.0, 0.0), (2, 1.0, 0.0)),
    ((2, 0.0, 1.0), (3, 0.0, -1.0)),
    ((2, 1.0, 0.0), (3, 1.0, 0.0)),
)
AXES = ((0, "grp"), (2, "gz"), (3, "ta"))
COARSE_DIRS = (1, 3, 4)


def cheb_coefficients():
    centre = 0.5 * (cheb_upper + cheb_lower)
    half_width = 0.5 * (cheb_upper - cheb_lower)
    spread_ratio = centre / half_width
    ratio_now = 1.0 / spread_ratio
    pairs = []
    for _ in range(DEG - 1):
        ratio_next = 1.0 / (2.0 * spread_ratio - ratio_now)
        pairs.append((ratio_next * ratio_now, 2.0 * ratio_next / half_width))
        ratio_now = ratio_next
    return 1.0 / centre, pairs


START, PAIRS = cheb_coefficients()
ALPHA = [pair[0] for pair in PAIRS] + [0.0, 0.0] + [pair[0] for pair in PAIRS]
BETA = [pair[1] for pair in PAIRS] + [0.0, START] + [pair[1] for pair in PAIRS]


def plus(a, b, sign):
    return a + b if sign > 0 else a - b


def project(v, mu, f):
    real, imag = [], []
    for a in range(2):
        b, gr, gi = gamma_table[mu][a]
        if gr != 0.0:
            real.append(plus(v[0][a], v[0][b], f * gr))
            imag.append(plus(v[1][a], v[1][b], f * gr))
        else:
            real.append(plus(v[0][a], v[1][b], -f * gi))
            imag.append(plus(v[1][a], v[0][b], f * gi))
    return [real, imag]


def rebuild(acc, h, mu, f):
    for a in range(2):
        b, gr, gi = gamma_table[mu][a]
        acc[0][a] = acc[0][a] + h[0][a]
        acc[1][a] = acc[1][a] + h[1][a]
        if gr != 0.0:
            acc[0][b] = plus(acc[0][b], h[0][a], f * gr)
            acc[1][b] = plus(acc[1][b], h[1][a], f * gr)
        else:
            acc[0][b] = plus(acc[0][b], h[1][a], f * gi)
            acc[1][b] = plus(acc[1][b], h[0][a], -f * gi)


def link_mul(links, mu, t, h, dagger):
    out = [[None, None], [None, None]]
    for col in range(3):
        if dagger:
            lr, li = links[mu, 0, col, :, t], links[mu, 1, col, :, t]
        else:
            lr, li = links[mu, 0, :, col, t], links[mu, 1, :, col, t]
        for a in range(2):
            hr, hi = h[0][a][col][None], h[1][a][col][None]
            if dagger:
                re, im = lr * hr + li * hi, lr * hi - li * hr
            else:
                re, im = lr * hr - li * hi, lr * hi + li * hr
            out[0][a] = re if col == 0 else out[0][a] + re
            out[1][a] = im if col == 0 else out[1][a] + im
    return out


def each(fn, h):
    return [[fn(h[ri][a]) for a in range(2)] for ri in range(2)]


def dot(a, b, dims=((1,), (0,))):
    return lax.dot_general(
        a, b, (dims, ((), ())), precision=lax.Precision.HIGHEST, preferred_element_type=F32
    )


def halves(a):
    high = a.astype(jnp.bfloat16)
    return high, (a - high.astype(F32)).astype(jnp.bfloat16)


def dot_halves(a, b):
    return sum(jnp.dot(a[i], b[j], preferred_element_type=F32) for i, j in ((1, 0), (0, 1), (0, 0)))


def pick(ones, b):
    ones = ones.astype(jnp.bfloat16)
    high, low = halves(b)
    return jnp.dot(ones, low, preferred_element_type=F32) + jnp.dot(ones, high, preferred_element_type=F32)


def rows_times(a, weights):
    high = a.astype(jnp.bfloat16).astype(F32)
    both = jnp.concatenate([high, a - high], axis=0).astype(jnp.bfloat16)
    out = jnp.dot(both, weights[1], preferred_element_type=F32) + jnp.dot(both, weights[0], preferred_element_type=F32)
    return out[0:8] + out[8:16]


def iota(shape, dim):
    return lax.broadcasted_iota(jnp.int32, shape, dim)


def wrap(sizes, disp):
    return tuple(by % sizes[axis] for by, (_, axis) in zip(disp, AXES))


STENCIL = (((0, 0, 0), 0), ((0, 0, 0), 1), ((1, 0, 0), 0), ((-1, 0, 0), 0),
           ((0, 1, 0), 0), ((0, -1, 0), 0), ((0, 0, 1), 0), ((0, 0, -1), 0))
CHUNKS = ((0, 4), (4, 8))


def reach(sizes):
    keys = []
    for first, flip in STENCIL:
        for second, again in STENCIL:
            key = (wrap(sizes, [i + j for i, j in zip(first, second)]), flip ^ again)
            if key not in keys:
                keys.append(key)
    far = []
    for disp, _ in keys:
        if any(disp) and disp not in far:
            far.append(disp)
    return keys, far


def kernel(sizes, src_in, gauge_in, null_in, coarse_in, u_out, e_out, src, gauge, null, coarse, p, u, fields, acc, links, g8,
           hx, qx, hz, qz, ht, qt, sendx, sendz, sendt, recvx, recvz, recvt, nv, nvs, nvt, low, ff, fb, wide, rows24, wrecv,
           twice, wides, twices, basis, crecv, ar_send, ar_recv, isem, fsend, frecv, lsend, lrecv, wsend, wrsem, csend, crsem, asend, arsem):
    keys, far = reach(sizes)
    me = {axis: lax.axis_index(axis) for axis in ("grp", "ta", "gz")}
    plane = sizes["grp"] * sizes["gz"]
    spot = me["grp"] * sizes["gz"] + me["gz"]

    def moved(axis, by):
        return lax.rem(me[axis] + (by + sizes[axis]), sizes[axis])

    def in_plane(by):
        other = lax.rem(spot + by, plane)
        return {"grp": lax.div(other, sizes["gz"]), "gz": lax.rem(other, sizes["gz"])}

    groups = ([in_plane(by) for by in range(1, plane)], [{"ta": moved("ta", by)} for by in range(1, sizes["ta"])])

    def at(disp):
        return {axis: moved(axis, by) for by, (_, axis) in zip(disp, AXES)}

    def back(disp):
        return at(wrap(sizes, [-by for by in disp]))

    barrier = pltpu.get_barrier_semaphore()
    partners = [at(disp) for disp, _ in STENCIL if any(disp)]
    for partner in partners:
        pl.semaphore_signal(barrier, inc=1, device_id=partner, device_id_type=MESH)

    loads = [pltpu.make_async_copy(a, b, isem.at[i]) for i, (a, b) in enumerate(
        ((gauge_in, gauge), (src_in, src), (coarse_in, coarse), (null_in, null)))]
    for load in loads:
        load.start()

    r = fields.at[4]

    loads[0].wait()
    for t in range(2):
        for x in range(4):
            g8[:, t, 2 * x:2 * x + 2, :] = gauge[:, 4 * x + 2 * t:4 * x + 2 * t + 2, :]
    spread_y = jnp.where((iota((8, 128), 1) & 7) == iota((8, 128), 0), 1.0, 0.0).astype(F32)
    tiled = dot(g8[...].reshape(72 * 16, 8), spread_y) * (-hop_kappa)
    links[...] = tiled.reshape(4, 2, 3, 3, 2, 8, 128)
    loads[1].wait()
    for t in range(2):
        for x in range(4):
            rows = src[:, 4 * x + 2 * t:4 * x + 2 * t + 2, :].reshape(2, 4, 3, 2, 128)
            r[:, :, :, t, 2 * x:2 * x + 2, :] = rows
            p[:, :, :, t, 2 * x:2 * x + 2, :] = rows * START
            u[:, :, :, t, 2 * x:2 * x + 2, :] = rows * START
    loads[2].wait()

    pl.semaphore_wait(barrier, len(partners))

    def low_copy(d):
        return pltpu.make_async_remote_copy(
            src_ref=coarse.at[pl.ds(COARSE_DIRS[d] * 96, 96)], dst_ref=low.at[d], send_sem=lsend.at[d],
            recv_sem=lrecv.at[d], device_id={AXES[d][1]: moved(AXES[d][1], 1)}, device_id_type=MESH)

    row8 = iota((8, 128), 0)
    lane8 = iota((8, 128), 1)

    def face_copy(d, side, ls, rs):
        out, into = ((sendx, recvx), (sendz, recvz), (sendt, recvt))[d]
        axis = AXES[d][1]
        return pltpu.make_async_remote_copy(
            src_ref=out.at[ls, side], dst_ref=into.at[rs, side], send_sem=fsend.at[ls, 2 * d + side],
            recv_sem=frecv.at[rs, 2 * d + side], device_id={axis: moved(axis, 2 * side - 1)},
            device_id_type=MESH)

    def field(ref, t):
        return [[ref[ri, s, :, t] for s in range(4)] for ri in range(2)]

    def keep(ref, t, total):
        for ri in range(2):
            for s in range(4):
                ref[ri, s, :, t] = total[ri][s]

    def build_null():
        loads[3].wait()
        for t in range(2):
            for x in range(4):
                nv[:, t, 2 * x:2 * x + 2, :] = null[:, x, t]

    def build_null_transposed():
        for ri in range(2):
            half = nv[12 * ri:12 * ri + 12].reshape(192, 192)
            for part, value in enumerate(halves(half)):
                nvs[part, 192 * ri:192 * ri + 192, :] = value
            for part, value in enumerate(halves(half.T)):
                nvt[part, 192 * ri:192 * ri + 192, :] = value

    def build_coarse():
        for d in range(3):
            low_copy(d).wait()
        ff[...] = jnp.zeros_like(ff)
        fb[...] = jnp.zeros_like(fb)
        zero = jnp.zeros((24, 104), F32)

        def piece(ref, base, y):
            return jnp.concatenate([ref[pl.ds(base + y, 24, stride=2), :] * basis_scale, zero], axis=1)

        def placed(value, at):
            return value if at == 0 else pltpu.roll(value, at, 1)

        for y in range(2):
            blocks = []
            for direction in (0, 1, 3, 4, 2):
                blocks.append([piece(coarse, direction * 96 + ri * 48, y) for ri in range(2)])
            for ro in range(2):
                for tile in range(3):
                    total = None
                    for j in range(2):
                        if 2 * tile + j > 4:
                            continue
                        mr, mi = blocks[2 * tile + j]
                        first, second = (mr, -mi) if ro == 0 else (mi, mr)
                        part = placed(first, 64 * j) + placed(second, 64 * j + 32)
                        total = part if total is None else total + part
                    ff[64 * y + 32 * ro:64 * y + 32 * ro + 24, 128 * tile:128 * tile + 128] = total
        for block in range(4):
            parts = []
            for y in range(2):
                if block == 0:
                    parts.append([piece(coarse, 2 * 96 + ri * 48, 1 - y) for ri in range(2)])
                else:
                    parts.append([piece(low.at[block - 1], ri * 48, y) for ri in range(2)])
            for ri in range(2):
                total = None
                for y in range(2):
                    mr, mi = parts[y]
                    first, second = (mr, -mi) if ri == 0 else (mi, mr)
                    part = placed(first, 64 * y) + placed(second, 64 * y + 32)
                    total = part if total is None else total + part
                fb[64 * block + 32 * ri:64 * block + 32 * ri + 24, :] = total
        flat = ff[...].T
        order = (flat[0:64], flat[256:320] + fb[0:64], flat[64:128], fb[64:128], flat[128:192], fb[128:192],
                 flat[192:256], fb[192:256])
        for block, rows in enumerate(order):
            wide[64 * block:64 * block + 64, :] = rows
            rows24[block] = rows[0:24]
            for part, value in enumerate(halves(rows)):
                wides[part, 64 * block:64 * block + 64, :] = value

    def row_copy(block, chunk):
        first, last = CHUNKS[chunk]
        return pltpu.make_async_remote_copy(
            src_ref=rows24.at[first:last], dst_ref=wrecv.at[block - 2, first:last], send_sem=wsend.at[block - 2, chunk],
            recv_sem=wrsem.at[block - 2, chunk], device_id=back(STENCIL[block][0]), device_id_type=MESH)

    def send_rows(chunk):
        def send():
            for block in range(2, 8):
                row_copy(block, chunk).start()

        return send

    def build_null_and_send():
        send_rows(0)()
        build_null_transposed()

    def build_twice():
        twice[...] = jnp.zeros_like(twice)
        for block, (disp, flip) in enumerate(STENCIL):
            if block >= 2:
                for chunk in range(len(CHUNKS)):
                    row_copy(block, chunk).wait()
            mine = wide[64 * block:64 * block + 64, :]
            left = iota((64, 128), 1) < 64
            upper, lower = jnp.where(left, mine, 0.0), jnp.where(left, 0.0, mine)
            weights = jnp.concatenate([lower, upper] if flip else [upper, lower], axis=0)
            theirs = rows24[...] if block < 2 else wrecv[block - 2]
            product = dot(theirs.reshape(8 * 24, 128), weights)
            real_lane = (iota((8 * 24, 128), 1) & 32) == 0
            turned = jnp.where(real_lane, -pltpu.roll(product, 96, 1), pltpu.roll(product, 32, 1))
            for other, (further, again) in enumerate(STENCIL):
                key = (wrap(sizes, [i + j for i, j in zip(disp, further)]), flip ^ again)
                base = 64 * keys.index(key)
                for ri, part in ((0, product), (1, turned)):
                    twice[base + 32 * ri:base + 32 * ri + 24, :] += part[24 * other:24 * other + 24]
        for part, value in enumerate(halves(twice[...])):
            twices[part] = value

    even = (iota((3, 8, 128), 1) & 1) == 0

    def start(f, ls, rs):
        v = field(f, 0)
        down = project(v, 3, -1.0)
        own_up = link_mul(links, 3, 0, project(v, 3, 1.0), True)
        v = field(f, 1)
        own_down = project(v, 3, -1.0)
        up = link_mul(links, 3, 1, project(v, 3, 1.0), True)
        for ri in range(2):
            for a in range(2):
                sendt[ls, 0, ri, a] = down[ri][a]
                sendt[ls, 1, ri, a] = up[ri][a]
                ht[ls, ri, a] = own_down[ri][a]
                qt[ls, ri, a] = own_up[ri][a]
        face_copy(2, 0, ls, rs).start()
        face_copy(2, 1, ls, rs).start()
        for t in range(2):
            v = field(f, t)
            down = project(v, 0, -1.0)
            up = link_mul(links, 0, t, project(v, 0, 1.0), True)
            for ri in range(2):
                for a in range(2):
                    j = 2 * (2 * a + t)
                    sendx[ls, 0, 3 * ri:3 * ri + 3, j:j + 2, :] = down[ri][a][:, 0:2]
                    sendx[ls, 1, 3 * ri:3 * ri + 3, j:j + 2, :] = up[ri][a][:, 6:8]
                    hx[ls, ri, a, :, t] = pltpu.roll(down[ri][a], 6, 1)
                    qx[ls, ri, a, :, t] = pltpu.roll(up[ri][a], 2, 1)
        face_copy(0, 0, ls, rs).start()
        face_copy(0, 1, ls, rs).start()
        downs, ups = [], []
        for t in range(2):
            v = field(f, t)
            downs.append(project(v, 2, -1.0))
            ups.append(link_mul(links, 2, t, project(v, 2, 1.0), True))
        for ri in range(2):
            for a in range(2):
                for t in range(2):
                    hz[ls, ri, a, :, t] = pltpu.roll(downs[t][ri][a], 7, 1)
                    qz[ls, ri, a, :, t] = pltpu.roll(ups[t][ri][a], 1, 1)
                sendz[ls, 0, ri, a] = jnp.where(even, downs[0][ri][a], pltpu.roll(downs[1][ri][a], 1, 1))
                sendz[ls, 1, ri, a] = jnp.where(even, pltpu.roll(ups[0][ri][a], 7, 1), ups[1][ri][a])
        face_copy(1, 0, ls, rs).start()
        face_copy(1, 1, ls, rs).start()

        lane = iota((3, 8, 128), 2)
        ypos = lane & 7
        below = jnp.where(lane < 8, fifth_hop * wall_mass, -fifth_hop).astype(F32)
        above = jnp.where(lane >= 120, fifth_hop * wall_mass, -fifth_hop).astype(F32)
        for t in range(2):
            v = field(f, t)
            total = [[None] * 4, [None] * 4]
            for ri in range(2):
                for s in range(4):
                    if s < 2:
                        side = below * pltpu.roll(v[ri][s], 8, 2)
                    else:
                        side = above * pltpu.roll(v[ri][s], 120, 2)
                    total[ri][s] = site_mass * v[ri][s] + side
            h = each(lambda w: jnp.where(ypos == 7, pltpu.roll(w, 7, 2), pltpu.roll(w, 127, 2)), project(v, 1, -1.0))
            rebuild(total, link_mul(links, 1, t, h, False), 1, -1.0)
            h = link_mul(links, 1, t, project(v, 1, 1.0), True)
            h = each(lambda w: jnp.where(ypos == 0, pltpu.roll(w, 121, 2), pltpu.roll(w, 1, 2)), h)
            rebuild(total, h, 1, 1.0)
            if t == 0:
                h = [[ht[ls, ri, a] for a in range(2)] for ri in range(2)]
                rebuild(total, link_mul(links, 3, 0, h, False), 3, -1.0)
            else:
                rebuild(total, [[qt[ls, ri, a] for a in range(2)] for ri in range(2)], 3, 1.0)
            keep(acc.at[ls], t, total)

    def finish(ls, rs, emit):
        face_copy(1, 0, ls, rs).wait()
        face_copy(1, 1, ls, rs).wait()
        for t in range(2):
            total = field(acc.at[ls], t)
            h = [[None, None], [None, None]]
            q = [[None, None], [None, None]]
            for ri in range(2):
                for a in range(2):
                    came, back = recvz[rs, 0, ri, a], recvz[rs, 1, ri, a]
                    if t == 0:
                        came = pltpu.roll(came, 1, 1)
                    else:
                        back = pltpu.roll(back, 7, 1)
                    h[ri][a] = jnp.where(even, hz[ls, ri, a, :, t], came)
                    q[ri][a] = jnp.where(even, back, qz[ls, ri, a, :, t])
            rebuild(total, link_mul(links, 2, t, h, False), 2, -1.0)
            rebuild(total, q, 2, 1.0)
            keep(acc.at[ls], t, total)
        face_copy(0, 0, ls, rs).wait()
        face_copy(0, 1, ls, rs).wait()
        for ri in range(2):
            for a in range(2):
                for t in range(2):
                    j = 2 * (2 * a + t)
                    hx[ls, ri, a, :, t, 6:8, :] = recvx[rs, 0, 3 * ri:3 * ri + 3, j:j + 2, :]
                    qx[ls, ri, a, :, t, 0:2, :] = recvx[rs, 1, 3 * ri:3 * ri + 3, j:j + 2, :]
        for t in range(2):
            total = field(acc.at[ls], t)
            h = [[hx[ls, ri, a, :, t] for a in range(2)] for ri in range(2)]
            rebuild(total, link_mul(links, 0, t, h, False), 0, -1.0)
            rebuild(total, [[qx[ls, ri, a, :, t] for a in range(2)] for ri in range(2)], 0, 1.0)
            keep(acc.at[ls], t, total)
        face_copy(2, 0, ls, rs).wait()
        face_copy(2, 1, ls, rs).wait()
        for t in range(2):
            total = field(acc.at[ls], t)
            if t == 0:
                rebuild(total, [[recvt[rs, 1, ri, a] for a in range(2)] for ri in range(2)], 3, 1.0)
            else:
                h = [[recvt[rs, 0, ri, a] for a in range(2)] for ri in range(2)]
                rebuild(total, link_mul(links, 3, 1, h, False), 3, -1.0)
            emit(t, total)

    def advance(k):
        alpha = jnp.float32(ALPHA[0])
        beta = jnp.float32(BETA[0])
        for at in range(1, 2 * DEG):
            alpha = jnp.where(k == at, jnp.float32(ALPHA[at]), alpha)
            beta = jnp.where(k == at, jnp.float32(BETA[at]), beta)

        def emit(t, total):
            for ri in range(2):
                for s in range(4):
                    left = r[ri, s, :, t] - total[ri][s]
                    step = alpha * p[ri, s, :, t] + beta * left
                    r[ri, s, :, t] = left
                    p[ri, s, :, t] = step
                    u[ri, s, :, t] = u[ri, s, :, t] + step

        return emit

    def round_of(k, hooks):
        slot = lax.rem(k, 2)
        start(p, 0, slot)
        for at, hook in hooks:
            pl.when(k == at)(hook)
        finish(0, slot, advance(k))

    def first_half(k, carry):
        round_of(k, ((0, build_null), (1, build_coarse), (2, build_null_and_send), (3, send_rows(1))))
        return carry

    def second_half(k, carry):
        round_of(k, ())
        return carry

    for d in range(3):
        low_copy(d).start()
    lax.fori_loop(0, DEG, first_half, 0)

    diagonal = (iota((192, 256), 0) & 7) == (iota((192, 256), 1) & 7)
    selector = jnp.where(
        ((lane8 >> 5) == (row8 & 3)) & (((lane8 & 7) >> 2) == (row8 >> 2)), 1.0, 0.0).astype(F32)
    fold = jnp.where((iota((32, 192), 1) >> 3) == iota((32, 192), 0), 1.0, 0.0).astype(F32)
    unfold = jnp.where((iota((192, 32), 0) >> 3) == iota((192, 32), 1), 1.0, 0.0).astype(F32)
    both = jnp.concatenate([r[0].reshape(192, 128), r[1].reshape(192, 128)], axis=1)
    prod = dot_halves((nvt[0], nvt[1]), halves(both))
    real = prod[0:192, 0:128] + prod[192:384, 128:256]
    imag = prod[0:192, 128:256] - prod[192:384, 0:128]
    kept = jnp.where(diagonal, jnp.concatenate([real, imag], axis=1), 0.0)
    summed = pick(fold, kept)
    stacked = jnp.concatenate([summed[:, 0:128], summed[:, 128:256]] * 2, axis=0)
    basis[0] = dot(selector, stacked, ((1,), (1,)))

    def coarse_copies(step):
        return [pltpu.make_async_remote_copy(
            src_ref=basis.at[2 * step], dst_ref=crecv.at[step, i], send_sem=csend.at[step, i],
            recv_sem=crsem.at[step, i], device_id=back(disp), device_id_type=MESH)
            for i, disp in enumerate(far)]

    low_half = lane8 < 64

    def prolong(step):
        spread = dot(basis[step], selector, ((0,), (0,)))
        paired = jnp.concatenate([spread[0:32], spread[32:64]], axis=1)
        weights = jnp.where(diagonal, pick(unfold, paired), 0.0)
        prod = dot_halves((nvs[0], nvs[1]), halves(weights))
        fields[step, 0] = (prod[0:192, 0:128] - prod[192:384, 128:256]).reshape(4, 3, 2, 8, 128)
        fields[step, 1] = (prod[0:192, 128:256] + prod[192:384, 0:128]).reshape(4, 3, 2, 8, 128)

    def begin(f):
        start(fields.at[f], 1 + f, 2 + f)

    def end(f):
        finish(1 + f, 2 + f, lambda t, total: keep(fields.at[5 + f], t, total))

    def across(own):
        layer = row8 & 3
        from_below = jnp.where(layer == 0, -wall_mass * pltpu.roll(own, 5, 0), pltpu.roll(own, 1, 0))
        from_above = jnp.where(layer == 3, -wall_mass * pltpu.roll(own, 3, 0), pltpu.roll(own, 7, 0))
        return (-coarse_fifth * basis_scale) * (from_below + from_above)

    def gathered(step, wanted):
        own = basis[2 * step]
        parts = []
        for disp, flip in wanted:
            disp = wrap(sizes, disp)
            part = crecv[step, far.index(disp)] if any(disp) else own
            parts.append(pltpu.roll(part, 4, 0) if flip else part)
        if len(parts) % 2:
            parts.append(own)
        return jnp.concatenate(
            [jnp.where(low_half, parts[i], parts[i + 1]) for i in range(0, len(parts), 2)], axis=1)

    def own_y(out):
        return jnp.where((row8 < 4) == low_half, out, pltpu.roll(out, 64, 1))

    def send_basis(step):
        for copy in coarse_copies(step):
            copy.start()

    def take_basis(step):
        for copy in coarse_copies(step):
            copy.wait()
        once = own_y(rows_times(gathered(step, STENCIL), (wides[0], wides[1])))
        shifted = across(basis[2 * step])
        basis[2 * step + 1] = once + shifted
        return 2.0 * once + shifted

    def take_second(step, first):
        again = own_y(rows_times(gathered(step, keys), (twices[0], twices[1])))
        basis[2 * step + 2] = again + across(first)

    send_basis(0)
    prolong(0)
    begin(0)
    begin(4)
    build_twice()
    take_second(0, take_basis(0))
    send_basis(1)

    def lift(f, carry):
        prolong(f)
        begin(f)
        return carry

    lax.fori_loop(1, 3, lift, 0)
    end(0)
    begin(5)
    end(4)
    take_second(1, take_basis(1))

    size = CITERS + 1
    vectors = [basis[i] for i in range(size)]
    sign = jnp.where((lane8 & 32) == 0, 1.0, -1.0).astype(F32)
    turned = [sign * pltpu.roll(v, 32, 1) for v in vectors]
    entries = [(i, j, 0) for i in range(size) for j in range(i, size)]
    entries += [(i, j, 1) for i in range(size) for j in range(i + 1, size)]
    none = jnp.zeros((8, 128), F32)
    products = [vectors[i] * (vectors[j] if part == 0 else turned[j]) for i, j, part in entries]
    products = jnp.stack(products + [none] * (32 - len(products)))
    rows = jnp.sum(jnp.where(low_half[None], products, 0.0), axis=1)
    padded = jnp.concatenate([rows, jnp.zeros((96, 128), F32)], axis=0)
    sums = dot(jnp.ones((8, 128), F32), padded, ((1,), (1,)))

    def sum_copies(phase):
        return [pltpu.make_async_remote_copy(
            src_ref=ar_send.at[phase], dst_ref=ar_recv.at[phase, by], send_sem=asend.at[phase, by],
            recv_sem=arsem.at[phase, by], device_id=partner, device_id_type=MESH)
            for by, partner in enumerate(groups[phase])]

    def send_sums(phase, value):
        ar_send[phase] = value
        for copy in sum_copies(phase):
            copy.start()

    def take_sums(phase):
        parts = [ar_send[phase]]
        for by, copy in enumerate(sum_copies(phase)):
            copy.wait()
            parts.append(ar_recv[phase, by])
        while len(parts) > 1:
            parts = [parts[i] + parts[i + 1] if i + 1 < len(parts) else parts[i] for i in range(0, len(parts), 2)]
        return parts[0]

    def turn(f, carry):
        end(f)
        begin(5 + f)
        return carry

    def settle(f, carry):
        end(f)
        return carry

    send_sums(0, sums)
    prolong(3)
    begin(3)
    lax.fori_loop(1, 3, turn, 0)
    send_sums(1, take_sums(0))
    end(3)
    begin(8)
    end(5)
    lax.fori_loop(6, 9, settle, 0)
    sums = take_sums(1)

    moments = [[None] * size for _ in range(size)]
    for number, (i, j, part) in enumerate(entries):
        value = jnp.broadcast_to(sums[:, number:number + 1], (8, 128))
        moments[i][j] = (value, none) if part == 0 else (moments[i][j][0], value)
    one = jnp.ones((8, 128), F32)
    coef = [(one, none)]
    answer = [(none, none)] * CITERS
    grow = 1.0 / basis_scale
    for step in range(CITERS):
        m00, m11 = moments[0][0][0], moments[1][1][0]
        m01r, m01i = moments[0][1]
        bottom = 1.0 / ((coarse_mass * coarse_mass) * m00 + (2.0 * coarse_mass * grow) * m01r + (grow * grow) * m11)
        ar = (coarse_mass * m00 + grow * m01r) * bottom
        ai = (-grow * m01i) * bottom
        for i, (cr, ci) in enumerate(coef):
            answer[i] = (answer[i][0] + (ar * cr - ai * ci), answer[i][1] + (ar * ci + ai * cr))
        kr, ki = 1.0 - coarse_mass * ar, -coarse_mass * ai
        dr, di = -grow * ar, -grow * ai
        kk, dd = kr * kr + ki * ki, dr * dr + di * di
        wr, wi = kr * dr + ki * di, kr * di - ki * dr
        fresh = [[None] * size for _ in range(size)]
        for m in range(size - 1 - step):
            for n in range(m, size - 1 - step):
                hr, hi = moments[m][n]
                nr, ni = moments[m][n + 1]
                fr, fi = moments[m + 1][n + 1]
                if m == n:
                    fresh[m][n] = ((kk * hr + dd * fr) + 2.0 * (wr * nr - wi * ni), none)
                else:
                    lr, li = moments[m + 1][n]
                    fresh[m][n] = ((kk * hr + dd * fr) + (wr * nr - wi * ni) + (wr * lr + wi * li),
                                   (kk * hi + dd * fi) + (wr * ni + wi * nr) + (wr * li - wi * lr))
        moments = fresh
        grown = [(kr * cr - ki * ci, kr * ci + ki * cr) for cr, ci in coef] + [(none, none)]
        for i, (cr, ci) in enumerate(coef):
            gr, gi = grown[i + 1]
            grown[i + 1] = (gr + (dr * cr - di * ci), gi + (dr * ci + di * cr))
        coef = grown

    alpha, beta = PAIRS[0]
    for t in range(2):
        for s in range(4):
            parts = [[fields[4, ri, s, :, t], fields[9, ri, s, :, t], u[ri, s, :, t]] for ri in range(2)]
            for i in range(CITERS):
                cr, ci = answer[i][0][None], answer[i][1][None]
                for part, at in ((0, 5 + i), (1, 10 + i), (2, i)):
                    fr, fi = fields[at, 0, s, :, t], fields[at, 1, s, :, t]
                    re, im = cr * fr - ci * fi, cr * fi + ci * fr
                    parts[0][part] = plus(parts[0][part], re, 1.0 if part == 2 else -1.0)
                    parts[1][part] = plus(parts[1][part], im, 1.0 if part == 2 else -1.0)
            for ri in range(2):
                left, through, result = parts[ri]
                step = START * left
                left = left - START * through
                after = alpha * step + beta * left
                r[ri, s, :, t] = left
                p[ri, s, :, t] = after
                u[ri, s, :, t] = result + step + after

    found = none
    for i in range(CITERS):
        found = found + (answer[i][0] * vectors[i] - answer[i][1] * turned[i])
    for ri in range(2):
        part = found if ri == 0 else pltpu.roll(found, 96, 1)
        for c in range(4):
            for y in range(2):
                at = 8 * ri + 2 * c + y
                e_out[at:at + 1, :] = part[4 * y + c:4 * y + c + 1, 0:24]

    lax.fori_loop(DEG + 2, 2 * DEG, second_half, 0)
    for t in range(2):
        for x in range(4):
            u_out[:, 4 * x + 2 * t:4 * x + 2 * t + 2, :] = u[:, :, :, t, 2 * x:2 * x + 2, :].reshape(24, 2, 128)


def pinned(x):
    return pltpu.with_memory_space_constraint(x, pltpu.HBM)


def body(sizes, source_field, gauge_links, null_vectors, coarse_links):
    hbm = pl.BlockSpec(memory_space=pltpu.HBM)
    vmem = pl.BlockSpec(memory_space=pltpu.VMEM)
    keys, far = reach(sizes)
    most_rows = 64 * (len(keys) + len(keys) % 2)
    half = (10, 2, 2, 3, 2, 8, 128)
    full = (2, 4, 3, 2, 8, 128)
    most = max(sizes["ta"], sizes["grp"] * sizes["gz"]) - 1
    arguments = [(24, 16, 128), (72, 16, 8), (24, 4, 2, 2, 192), (480, 24)]
    shapes = arguments + [full, full, (14,) + full, (10,) + full, (4, 2, 3, 3, 2, 8, 128), (72, 2, 8, 8),
                          half, half, half, half, (10, 2, 2, 3, 8, 128), (10, 2, 2, 3, 8, 128),
                          (10, 2, 6, 8, 128), (10, 2, 2, 2, 3, 8, 128), (10, 2, 2, 2, 3, 8, 128),
                          (11, 2, 6, 8, 128), (11, 2, 2, 2, 3, 8, 128), (11, 2, 2, 2, 3, 8, 128),
                          (24, 2, 8, 192), (2, 384, 192), (2, 384, 192), (3, 96, 24), (128, 384), (256, 128), (512, 128), (8, 24, 128), (6, 8, 24, 128),
                          (most_rows, 128), (2, 512, 128), (2, most_rows, 128), (CITERS + 1, 8, 128), (2, len(far), 8, 128), (2, 8, 128), (2, most, 8, 128)]
    split = ((2, 384, 192), (2, 512, 128), (2, most_rows, 128))
    sems = [(4,), (10, 6), (11, 6), (3,), (3,), (6, 2), (6, 2), (2, len(far)), (2, len(far)), (2, most), (2, most)]
    out, found = pl.pallas_call(
        functools.partial(kernel, sizes),
        out_shape=(jax.ShapeDtypeStruct((24, 16, 128), F32), jax.ShapeDtypeStruct((16, 24), F32)),
        in_specs=[hbm] * 4,
        out_specs=(vmem, vmem),
        scratch_shapes=[pltpu.VMEM(shape, jnp.bfloat16 if shape in split else F32) for shape in shapes]
        + [pltpu.SemaphoreType.DMA(shape) for shape in sems],
        compiler_params=pltpu.CompilerParams(
            collective_id=0, has_side_effects=True, vmem_limit_bytes=32 * 1024 * 1024),
    )(
        pinned(source_field.reshape(arguments[0])),
        pinned(gauge_links.reshape(arguments[1])),
        pinned(null_vectors.reshape(arguments[2])),
        pinned(coarse_links.transpose(0, 1, 2, 4, 5, 6, 7, 3).reshape(arguments[3])),
    )
    found = found.reshape(2, 4, 2, 24).transpose(0, 3, 1, 2)
    return out.reshape(source_field.shape), found.reshape(2, 24, 4, 1, 1, 1, 2)


def solution(mesh):
    sizes = {axis: mesh.shape[axis] for axis in ("grp", "ta", "gz")}
    placed = (
        P(None, None, None, "grp", "ta", "gz", None),
        P(None, None, None, None, "grp", "ta", "gz", None),
        P(None, None, None, "grp", "ta", "gz", None),
        P(None, None, None, None, "grp", "ta", "gz", None),
    )
    return jax.shard_map(
        functools.partial(body, sizes),
        mesh=mesh,
        in_specs=placed,
        out_specs=(
            P(None, None, None, "grp", "ta", "gz", None),
            P(None, None, None, "grp", "ta", "gz", None),
        ),
        check_vma=False,
    )
```

```python
import functools

import jax
import jax.numpy as jnp
from jax import lax
from jax.experimental import pallas as pl
from jax.experimental.pallas import tpu as pltpu
from jax.sharding import PartitionSpec as P

MESH = pl.DeviceIdType.MESH
F32 = jnp.float32

site_mass = 2.0
hop_kappa = 0.1
fifth_hop = 0.4
wall_mass = 0.1
cheb_lower = 0.6
cheb_upper = 3.4
coarse_mass = 3.0
coarse_fifth = 0.3
basis_scale = 0.125
DEG = 4
CITERS = 4
gamma_table = (
    ((3, 0.0, 1.0), (2, 0.0, 1.0)),
    ((3, -1.0, 0.0), (2, 1.0, 0.0)),
    ((2, 0.0, 1.0), (3, 0.0, -1.0)),
    ((2, 1.0, 0.0), (3, 1.0, 0.0)),
)
AXES = ((0, "grp"), (2, "gz"), (3, "ta"))
COARSE_DIRS = (1, 3, 4)


def cheb_coefficients():
    centre = 0.5 * (cheb_upper + cheb_lower)
    half_width = 0.5 * (cheb_upper - cheb_lower)
    spread_ratio = centre / half_width
    ratio_now = 1.0 / spread_ratio
    pairs = []
    for _ in range(DEG - 1):
        ratio_next = 1.0 / (2.0 * spread_ratio - ratio_now)
        pairs.append((ratio_next * ratio_now, 2.0 * ratio_next / half_width))
        ratio_now = ratio_next
    return 1.0 / centre, pairs


START, PAIRS = cheb_coefficients()
ALPHA = [pair[0] for pair in PAIRS] + [0.0, 0.0] + [pair[0] for pair in PAIRS]
BETA = [pair[1] for pair in PAIRS] + [0.0, START] + [pair[1] for pair in PAIRS]


def plus(a, b, sign):
    return a + b if sign > 0 else a - b


def project(v, mu, f):
    real, imag = [], []
    for a in range(2):
        b, gr, gi = gamma_table[mu][a]
        if gr != 0.0:
            real.append(plus(v[0][a], v[0][b], f * gr))
            imag.append(plus(v[1][a], v[1][b], f * gr))
        else:
            real.append(plus(v[0][a], v[1][b], -f * gi))
            imag.append(plus(v[1][a], v[0][b], f * gi))
    return [real, imag]


def rebuild(acc, h, mu, f):
    for a in range(2):
        b, gr, gi = gamma_table[mu][a]
        acc[0][a] = acc[0][a] + h[0][a]
        acc[1][a] = acc[1][a] + h[1][a]
        if gr != 0.0:
            acc[0][b] = plus(acc[0][b], h[0][a], f * gr)
            acc[1][b] = plus(acc[1][b], h[1][a], f * gr)
        else:
            acc[0][b] = plus(acc[0][b], h[1][a], f * gi)
            acc[1][b] = plus(acc[1][b], h[0][a], -f * gi)


def link_mul(links, mu, t, h, dagger):
    out = [[None, None], [None, None]]
    for col in range(3):
        if dagger:
            lr, li = links[mu, 0, col, :, t], links[mu, 1, col, :, t]
        else:
            lr, li = links[mu, 0, :, col, t], links[mu, 1, :, col, t]
        for a in range(2):
            hr, hi = h[0][a][col][None], h[1][a][col][None]
            if dagger:
                re, im = lr * hr + li * hi, lr * hi - li * hr
            else:
                re, im = lr * hr - li * hi, lr * hi + li * hr
            out[0][a] = re if col == 0 else out[0][a] + re
            out[1][a] = im if col == 0 else out[1][a] + im
    return out


def each(fn, h):
    return [[fn(h[ri][a]) for a in range(2)] for ri in range(2)]


def dot(a, b, dims=((1,), (0,))):
    return lax.dot_general(
        a, b, (dims, ((), ())), precision=lax.Precision.HIGHEST, preferred_element_type=F32
    )


def halves(a):
    high = a.astype(jnp.bfloat16)
    return high, (a - high.astype(F32)).astype(jnp.bfloat16)


def dot_halves(a, b):
    return sum(jnp.dot(a[i], b[j], preferred_element_type=F32) for i, j in ((1, 0), (0, 1), (0, 0)))


def pick(ones, b):
    ones = ones.astype(jnp.bfloat16)
    high, low = halves(b)
    return jnp.dot(ones, low, preferred_element_type=F32) + jnp.dot(ones, high, preferred_element_type=F32)


def rows_times(a, weights):
    high = a.astype(jnp.bfloat16).astype(F32)
    both = jnp.concatenate([high, a - high], axis=0).astype(jnp.bfloat16)
    out = jnp.dot(both, weights[1], preferred_element_type=F32) + jnp.dot(both, weights[0], preferred_element_type=F32)
    return out[0:8] + out[8:16]


def iota(shape, dim):
    return lax.broadcasted_iota(jnp.int32, shape, dim)


def wrap(sizes, disp):
    return tuple(by % sizes[axis] for by, (_, axis) in zip(disp, AXES))


STENCIL = (((0, 0, 0), 0), ((0, 0, 0), 1), ((1, 0, 0), 0), ((-1, 0, 0), 0),
           ((0, 1, 0), 0), ((0, -1, 0), 0), ((0, 0, 1), 0), ((0, 0, -1), 0))
CHUNKS = ((0, 4), (4, 8))


def reach(sizes):
    keys = []
    for first, flip in STENCIL:
        for second, again in STENCIL:
            key = (wrap(sizes, [i + j for i, j in zip(first, second)]), flip ^ again)
            if key not in keys:
                keys.append(key)
    far = []
    for disp, _ in keys:
        if any(disp) and disp not in far:
            far.append(disp)
    return keys, far


def kernel(sizes, src_in, gauge_in, null_in, coarse_in, u_out, e_out, src, gauge, null, coarse, p, u, fields, acc, links, g8,
           hx, qx, hz, qz, ht, qt, sendx, sendz, sendt, recvx, recvz, recvt, nv, nvs, nvt, low, ff, fb, wide, rows24, wrecv,
           twice, wides, twices, basis, crecv, ar_send, ar_recv, isem, fsend, frecv, lsend, lrecv, wsend, wrsem, csend, crsem, asend, arsem):
    keys, far = reach(sizes)
    me = {axis: lax.axis_index(axis) for axis in ("grp", "ta", "gz")}
    plane = sizes["grp"] * sizes["gz"]
    spot = me["grp"] * sizes["gz"] + me["gz"]

    def moved(axis, by):
        return lax.rem(me[axis] + (by + sizes[axis]), sizes[axis])

    def in_plane(by):
        other = lax.rem(spot + by, plane)
        return {"grp": lax.div(other, sizes["gz"]), "gz": lax.rem(other, sizes["gz"])}

    groups = ([in_plane(by) for by in range(1, plane)], [{"ta": moved("ta", by)} for by in range(1, sizes["ta"])])

    def at(disp):
        return {axis: moved(axis, by) for by, (_, axis) in zip(disp, AXES)}

    def back(disp):
        return at(wrap(sizes, [-by for by in disp]))

    barrier = pltpu.get_barrier_semaphore()
    partners = [at(disp) for disp, _ in STENCIL if any(disp)]
    for partner in partners:
        pl.semaphore_signal(barrier, inc=1, device_id=partner, device_id_type=MESH)

    loads = [pltpu.make_async_copy(a, b, isem.at[i]) for i, (a, b) in enumerate(
        ((gauge_in, gauge), (src_in, src), (coarse_in, coarse), (null_in, null)))]
    for load in loads:
        load.start()

    r = fields.at[4]

    loads[0].wait()
    for t in range(2):
        for x in range(4):
            g8[:, t, 2 * x:2 * x + 2, :] = gauge[:, 4 * x + 2 * t:4 * x + 2 * t + 2, :]
    spread_y = jnp.where((iota((8, 128), 1) & 7) == iota((8, 128), 0), 1.0, 0.0).astype(F32)
    tiled = dot(g8[...].reshape(72 * 16, 8), spread_y) * (-hop_kappa)
    links[...] = tiled.reshape(4, 2, 3, 3, 2, 8, 128)
    loads[1].wait()
    for t in range(2):
        for x in range(4):
            rows = src[:, 4 * x + 2 * t:4 * x + 2 * t + 2, :].reshape(2, 4, 3, 2, 128)
            r[:, :, :, t, 2 * x:2 * x + 2, :] = rows
            p[:, :, :, t, 2 * x:2 * x + 2, :] = rows * START
            u[:, :, :, t, 2 * x:2 * x + 2, :] = rows * START
    loads[2].wait()

    pl.semaphore_wait(barrier, len(partners))

    def low_copy(d):
        return pltpu.make_async_remote_copy(
            src_ref=coarse.at[pl.ds(COARSE_DIRS[d] * 96, 96)], dst_ref=low.at[d], send_sem=lsend.at[d],
            recv_sem=lrecv.at[d], device_id={AXES[d][1]: moved(AXES[d][1], 1)}, device_id_type=MESH)

    row8 = iota((8, 128), 0)
    lane8 = iota((8, 128), 1)

    def face_copy(d, side, ls, rs):
        out, into = ((sendx, recvx), (sendz, recvz), (sendt, recvt))[d]
        axis = AXES[d][1]
        return pltpu.make_async_remote_copy(
            src_ref=out.at[ls, side], dst_ref=into.at[rs, side], send_sem=fsend.at[ls, 2 * d + side],
            recv_sem=frecv.at[rs, 2 * d + side], device_id={axis: moved(axis, 2 * side - 1)},
            device_id_type=MESH)

    def field(ref, t):
        return [[ref[ri, s, :, t] for s in range(4)] for ri in range(2)]

    def keep(ref, t, total):
        for ri in range(2):
            for s in range(4):
                ref[ri, s, :, t] = total[ri][s]

    def build_null():
        for d in range(3):
            low_copy(d).start()
        loads[3].wait()
        for t in range(2):
            for x in range(4):
                nv[:, t, 2 * x:2 * x + 2, :] = null[:, x, t]

    def build_null_transposed():
        for ri in range(2):
            half = nv[12 * ri:12 * ri + 12].reshape(192, 192)
            for part, value in enumerate(halves(half)):
                nvs[part, 192 * ri:192 * ri + 192, :] = value
            for part, value in enumerate(halves(half.T)):
                nvt[part, 192 * ri:192 * ri + 192, :] = value

    def build_coarse():
        for d in range(3):
            low_copy(d).wait()
        ff[...] = jnp.zeros_like(ff)
        fb[...] = jnp.zeros_like(fb)
        zero = jnp.zeros((24, 104), F32)

        def piece(ref, base, y):
            return jnp.concatenate([ref[pl.ds(base + y, 24, stride=2), :] * basis_scale, zero], axis=1)

        def placed(value, at):
            return value if at == 0 else pltpu.roll(value, at, 1)

        for y in range(2):
            blocks = []
            for direction in (0, 1, 3, 4, 2):
                blocks.append([piece(coarse, direction * 96 + ri * 48, y) for ri in range(2)])
            for ro in range(2):
                for tile in range(3):
                    total = None
                    for j in range(2):
                        if 2 * tile + j > 4:
                            continue
                        mr, mi = blocks[2 * tile + j]
                        first, second = (mr, -mi) if ro == 0 else (mi, mr)
                        part = placed(first, 64 * j) + placed(second, 64 * j + 32)
                        total = part if total is None else total + part
                    ff[64 * y + 32 * ro:64 * y + 32 * ro + 24, 128 * tile:128 * tile + 128] = total
        for block in range(4):
            parts = []
            for y in range(2):
                if block == 0:
                    parts.append([piece(coarse, 2 * 96 + ri * 48, 1 - y) for ri in range(2)])
                else:
                    parts.append([piece(low.at[block - 1], ri * 48, y) for ri in range(2)])
            for ri in range(2):
                total = None
                for y in range(2):
                    mr, mi = parts[y]
                    first, second = (mr, -mi) if ri == 0 else (mi, mr)
                    part = placed(first, 64 * y) + placed(second, 64 * y + 32)
                    total = part if total is None else total + part
                fb[64 * block + 32 * ri:64 * block + 32 * ri + 24, :] = total
        flat = ff[...].T
        order = (flat[0:64], flat[256:320] + fb[0:64], flat[64:128], fb[64:128], flat[128:192], fb[128:192],
                 flat[192:256], fb[192:256])
        for block, rows in enumerate(order):
            wide[64 * block:64 * block + 64, :] = rows
            rows24[block] = rows[0:24]
            for part, value in enumerate(halves(rows)):
                wides[part, 64 * block:64 * block + 64, :] = value

    def row_copy(block, chunk):
        first, last = CHUNKS[chunk]
        return pltpu.make_async_remote_copy(
            src_ref=rows24.at[first:last], dst_ref=wrecv.at[block - 2, first:last], send_sem=wsend.at[block - 2, chunk],
            recv_sem=wrsem.at[block - 2, chunk], device_id=back(STENCIL[block][0]), device_id_type=MESH)

    def send_rows(chunk):
        def send():
            for block in range(2, 8):
                row_copy(block, chunk).start()

        return send

    def build_coarse_and_send():
        build_coarse()
        send_rows(0)()

    def build_null_and_send():
        build_null_transposed()

    def build_twice():
        twice[...] = jnp.zeros_like(twice)
        for block, (disp, flip) in enumerate(STENCIL):
            if block >= 2:
                for chunk in range(len(CHUNKS)):
                    row_copy(block, chunk).wait()
            mine = wide[64 * block:64 * block + 64, :]
            left = iota((64, 128), 1) < 64
            upper, lower = jnp.where(left, mine, 0.0), jnp.where(left, 0.0, mine)
            weights = jnp.concatenate([lower, upper] if flip else [upper, lower], axis=0)
            theirs = rows24[...] if block < 2 else wrecv[block - 2]
            product = dot_halves(halves(theirs.reshape(8 * 24, 128)), halves(weights))
            real_lane = (iota((8 * 24, 128), 1) & 32) == 0
            turned = jnp.where(real_lane, -pltpu.roll(product, 96, 1), pltpu.roll(product, 32, 1))
            for other, (further, again) in enumerate(STENCIL):
                key = (wrap(sizes, [i + j for i, j in zip(disp, further)]), flip ^ again)
                base = 64 * keys.index(key)
                for ri, part in ((0, product), (1, turned)):
                    twice[base + 32 * ri:base + 32 * ri + 24, :] += part[24 * other:24 * other + 24]
        for part, value in enumerate(halves(twice[...])):
            twices[part] = value

    even = (iota((3, 8, 128), 1) & 1) == 0

    def start(f, ls, rs):
        v = field(f, 0)
        down = project(v, 3, -1.0)
        own_up = link_mul(links, 3, 0, project(v, 3, 1.0), True)
        v = field(f, 1)
        own_down = project(v, 3, -1.0)
        up = link_mul(links, 3, 1, project(v, 3, 1.0), True)
        for ri in range(2):
            for a in range(2):
                sendt[ls, 0, ri, a] = down[ri][a]
                sendt[ls, 1, ri, a] = up[ri][a]
                ht[ls, ri, a] = own_down[ri][a]
                qt[ls, ri, a] = own_up[ri][a]
        face_copy(2, 0, ls, rs).start()
        face_copy(2, 1, ls, rs).start()
        for t in range(2):
            v = field(f, t)
            down = project(v, 0, -1.0)
            up = link_mul(links, 0, t, project(v, 0, 1.0), True)
            for ri in range(2):
                for a in range(2):
                    j = 2 * (2 * a + t)
                    sendx[ls, 0, 3 * ri:3 * ri + 3, j:j + 2, :] = down[ri][a][:, 0:2]
                    sendx[ls, 1, 3 * ri:3 * ri + 3, j:j + 2, :] = up[ri][a][:, 6:8]
                    hx[ls, ri, a, :, t] = pltpu.roll(down[ri][a], 6, 1)
                    qx[ls, ri, a, :, t] = pltpu.roll(up[ri][a], 2, 1)
        face_copy(0, 0, ls, rs).start()
        face_copy(0, 1, ls, rs).start()
        downs, ups = [], []
        for t in range(2):
            v = field(f, t)
            downs.append(project(v, 2, -1.0))
            ups.append(link_mul(links, 2, t, project(v, 2, 1.0), True))
        for ri in range(2):
            for a in range(2):
                for t in range(2):
                    hz[ls, ri, a, :, t] = pltpu.roll(downs[t][ri][a], 7, 1)
                    qz[ls, ri, a, :, t] = pltpu.roll(ups[t][ri][a], 1, 1)
                sendz[ls, 0, ri, a] = jnp.where(even, downs[0][ri][a], pltpu.roll(downs[1][ri][a], 1, 1))
                sendz[ls, 1, ri, a] = jnp.where(even, pltpu.roll(ups[0][ri][a], 7, 1), ups[1][ri][a])
        face_copy(1, 0, ls, rs).start()
        face_copy(1, 1, ls, rs).start()

        lane = iota((3, 8, 128), 2)
        ypos = lane & 7
        below = jnp.where(lane < 8, fifth_hop * wall_mass, -fifth_hop).astype(F32)
        above = jnp.where(lane >= 120, fifth_hop * wall_mass, -fifth_hop).astype(F32)
        for t in range(2):
            v = field(f, t)
            total = [[None] * 4, [None] * 4]
            for ri in range(2):
                for s in range(4):
                    if s < 2:
                        side = below * pltpu.roll(v[ri][s], 8, 2)
                    else:
                        side = above * pltpu.roll(v[ri][s], 120, 2)
                    total[ri][s] = site_mass * v[ri][s] + side
            h = each(lambda w: jnp.where(ypos == 7, pltpu.roll(w, 7, 2), pltpu.roll(w, 127, 2)), project(v, 1, -1.0))
            rebuild(total, link_mul(links, 1, t, h, False), 1, -1.0)
            h = link_mul(links, 1, t, project(v, 1, 1.0), True)
            h = each(lambda w: jnp.where(ypos == 0, pltpu.roll(w, 121, 2), pltpu.roll(w, 1, 2)), h)
            rebuild(total, h, 1, 1.0)
            if t == 0:
                h = [[ht[ls, ri, a] for a in range(2)] for ri in range(2)]
                rebuild(total, link_mul(links, 3, 0, h, False), 3, -1.0)
            else:
                rebuild(total, [[qt[ls, ri, a] for a in range(2)] for ri in range(2)], 3, 1.0)
            keep(acc.at[ls], t, total)

    def finish(ls, rs, emit):
        face_copy(1, 0, ls, rs).wait()
        face_copy(1, 1, ls, rs).wait()
        for t in range(2):
            total = field(acc.at[ls], t)
            h = [[None, None], [None, None]]
            q = [[None, None], [None, None]]
            for ri in range(2):
                for a in range(2):
                    came, back = recvz[rs, 0, ri, a], recvz[rs, 1, ri, a]
                    if t == 0:
                        came = pltpu.roll(came, 1, 1)
                    else:
                        back = pltpu.roll(back, 7, 1)
                    h[ri][a] = jnp.where(even, hz[ls, ri, a, :, t], came)
                    q[ri][a] = jnp.where(even, back, qz[ls, ri, a, :, t])
            rebuild(total, link_mul(links, 2, t, h, False), 2, -1.0)
            rebuild(total, q, 2, 1.0)
            keep(acc.at[ls], t, total)
        face_copy(0, 0, ls, rs).wait()
        face_copy(0, 1, ls, rs).wait()
        for ri in range(2):
            for a in range(2):
                for t in range(2):
                    j = 2 * (2 * a + t)
                    hx[ls, ri, a, :, t, 6:8, :] = recvx[rs, 0, 3 * ri:3 * ri + 3, j:j + 2, :]
                    qx[ls, ri, a, :, t, 0:2, :] = recvx[rs, 1, 3 * ri:3 * ri + 3, j:j + 2, :]
        for t in range(2):
            total = field(acc.at[ls], t)
            h = [[hx[ls, ri, a, :, t] for a in range(2)] for ri in range(2)]
            rebuild(total, link_mul(links, 0, t, h, False), 0, -1.0)
            rebuild(total, [[qx[ls, ri, a, :, t] for a in range(2)] for ri in range(2)], 0, 1.0)
            keep(acc.at[ls], t, total)
        face_copy(2, 0, ls, rs).wait()
        face_copy(2, 1, ls, rs).wait()
        for t in range(2):
            total = field(acc.at[ls], t)
            if t == 0:
                rebuild(total, [[recvt[rs, 1, ri, a] for a in range(2)] for ri in range(2)], 3, 1.0)
            else:
                h = [[recvt[rs, 0, ri, a] for a in range(2)] for ri in range(2)]
                rebuild(total, link_mul(links, 3, 1, h, False), 3, -1.0)
            emit(t, total)

    def advance(k):
        alpha = jnp.float32(ALPHA[0])
        beta = jnp.float32(BETA[0])
        for at in range(1, 2 * DEG):
            alpha = jnp.where(k == at, jnp.float32(ALPHA[at]), alpha)
            beta = jnp.where(k == at, jnp.float32(BETA[at]), beta)

        def emit(t, total):
            for ri in range(2):
                for s in range(4):
                    left = r[ri, s, :, t] - total[ri][s]
                    step = alpha * p[ri, s, :, t] + beta * left
                    r[ri, s, :, t] = left
                    p[ri, s, :, t] = step
                    u[ri, s, :, t] = u[ri, s, :, t] + step

        return emit

    def round_of(k, hooks):
        slot = lax.rem(k, 2)
        start(p, 0, slot)
        for at, hook in hooks:
            pl.when(k == at)(hook)
        finish(0, slot, advance(k))

    def first_half(k, carry):
        round_of(k, ((0, build_null), (1, build_null_and_send), (2, build_coarse_and_send), (3, send_rows(1))))
        return carry

    def second_half(k, carry):
        round_of(k, ())
        return carry

    lax.fori_loop(0, DEG, first_half, 0)

    diagonal = (iota((192, 256), 0) & 7) == (iota((192, 256), 1) & 7)
    selector = jnp.where(
        ((lane8 >> 5) == (row8 & 3)) & (((lane8 & 7) >> 2) == (row8 >> 2)), 1.0, 0.0).astype(F32)
    fold = jnp.where((iota((32, 192), 1) >> 3) == iota((32, 192), 0), 1.0, 0.0).astype(F32)
    unfold = jnp.where((iota((192, 32), 0) >> 3) == iota((192, 32), 1), 1.0, 0.0).astype(F32)
    both = jnp.concatenate([r[0].reshape(192, 128), r[1].reshape(192, 128)], axis=1)
    prod = dot_halves((nvt[0], nvt[1]), halves(both))
    real = prod[0:192, 0:128] + prod[192:384, 128:256]
    imag = prod[0:192, 128:256] - prod[192:384, 0:128]
    kept = jnp.where(diagonal, jnp.concatenate([real, imag], axis=1), 0.0)
    summed = pick(fold, kept)
    stacked = jnp.concatenate([summed[:, 0:128], summed[:, 128:256]] * 2, axis=0)
    basis[0] = dot(selector, stacked, ((1,), (1,)))

    def coarse_copies(step):
        return [pltpu.make_async_remote_copy(
            src_ref=basis.at[2 * step], dst_ref=crecv.at[step, i], send_sem=csend.at[step, i],
            recv_sem=crsem.at[step, i], device_id=back(disp), device_id_type=MESH)
            for i, disp in enumerate(far)]

    low_half = lane8 < 64

    def prolong(step):
        spread = dot(basis[step], selector, ((0,), (0,)))
        paired = jnp.concatenate([spread[0:32], spread[32:64]], axis=1)
        weights = jnp.where(diagonal, pick(unfold, paired), 0.0)
        prod = dot_halves((nvs[0], nvs[1]), halves(weights))
        fields[step, 0] = (prod[0:192, 0:128] - prod[192:384, 128:256]).reshape(4, 3, 2, 8, 128)
        fields[step, 1] = (prod[0:192, 128:256] + prod[192:384, 0:128]).reshape(4, 3, 2, 8, 128)

    def begin(f):
        start(fields.at[f], 1 + f, 2 + f)

    def end(f):
        finish(1 + f, 2 + f, lambda t, total: keep(fields.at[5 + f], t, total))

    def across(own):
        layer = row8 & 3
        from_below = jnp.where(layer == 0, -wall_mass * pltpu.roll(own, 5, 0), pltpu.roll(own, 1, 0))
        from_above = jnp.where(layer == 3, -wall_mass * pltpu.roll(own, 3, 0), pltpu.roll(own, 7, 0))
        return (-coarse_fifth * basis_scale) * (from_below + from_above)

    def gathered(step, wanted):
        own = basis[2 * step]
        parts = []
        for disp, flip in wanted:
            disp = wrap(sizes, disp)
            part = crecv[step, far.index(disp)] if any(disp) else own
            parts.append(pltpu.roll(part, 4, 0) if flip else part)
        if len(parts) % 2:
            parts.append(own)
        return jnp.concatenate(
            [jnp.where(low_half, parts[i], parts[i + 1]) for i in range(0, len(parts), 2)], axis=1)

    def own_y(out):
        return jnp.where((row8 < 4) == low_half, out, pltpu.roll(out, 64, 1))

    def send_basis(step):
        for copy in coarse_copies(step):
            copy.start()

    def take_basis(step):
        for copy in coarse_copies(step):
            copy.wait()
        once = own_y(rows_times(gathered(step, STENCIL), (wides[0], wides[1])))
        shifted = across(basis[2 * step])
        basis[2 * step + 1] = once + shifted
        return 2.0 * once + shifted

    def take_second(step, first):
        again = own_y(rows_times(gathered(step, keys), (twices[0], twices[1])))
        basis[2 * step + 2] = again + across(first)

    send_basis(0)
    prolong(0)
    begin(0)
    begin(4)
    build_twice()
    take_second(0, take_basis(0))
    send_basis(1)

    def lift(f, carry):
        prolong(f)
        begin(f)
        return carry

    lax.fori_loop(1, 3, lift, 0)
    end(0)
    begin(5)
    take_second(1, take_basis(1))

    size = CITERS + 1
    vectors = [basis[i] for i in range(size)]
    sign = jnp.where((lane8 & 32) == 0, 1.0, -1.0).astype(F32)
    turned = [sign * pltpu.roll(v, 32, 1) for v in vectors]
    entries = [(i, j, 0) for i in range(size) for j in range(i, size)]
    entries += [(i, j, 1) for i in range(size) for j in range(i + 1, size)]
    none = jnp.zeros((8, 128), F32)
    products = [vectors[i] * (vectors[j] if part == 0 else turned[j]) for i, j, part in entries]
    products = jnp.stack(products + [none] * (32 - len(products)))
    rows = jnp.sum(jnp.where(low_half[None], products, 0.0), axis=1)
    padded = jnp.concatenate([rows, jnp.zeros((96, 128), F32)], axis=0)
    sums = dot(jnp.ones((8, 128), F32), padded, ((1,), (1,)))[0:1]

    def sum_copies(phase):
        return [pltpu.make_async_remote_copy(
            src_ref=ar_send.at[phase], dst_ref=ar_recv.at[phase, by], send_sem=asend.at[phase, by],
            recv_sem=arsem.at[phase, by], device_id=partner, device_id_type=MESH)
            for by, partner in enumerate(groups[phase])]

    def send_sums(phase, value):
        ar_send[phase] = value
        for copy in sum_copies(phase):
            copy.start()

    def take_sums(phase):
        parts = [ar_send[phase]]
        for by, copy in enumerate(sum_copies(phase)):
            copy.wait()
            parts.append(ar_recv[phase, by])
        while len(parts) > 1:
            parts = [parts[i] + parts[i + 1] if i + 1 < len(parts) else parts[i] for i in range(0, len(parts), 2)]
        return parts[0]

    def turn(f, carry):
        end(f)
        begin(5 + f)
        return carry

    def settle(f, carry):
        end(f)
        return carry

    send_sums(0, sums)
    prolong(3)
    begin(3)
    lax.fori_loop(1, 3, turn, 0)
    send_sums(1, take_sums(0))
    end(3)
    begin(8)
    end(4)
    end(5)
    lax.fori_loop(6, 9, settle, 0)
    sums = take_sums(1)

    moments = [[None] * size for _ in range(size)]
    for number, (i, j, part) in enumerate(entries):
        value = jnp.broadcast_to(sums[:, number:number + 1], (8, 128))
        moments[i][j] = (value, none) if part == 0 else (moments[i][j][0], value)
    one = jnp.ones((8, 128), F32)
    coef = [(one, none)]
    answer = [(none, none)] * CITERS
    grow = 1.0 / basis_scale
    for step in range(CITERS):
        m00, m11 = moments[0][0][0], moments[1][1][0]
        m01r, m01i = moments[0][1]
        bottom = 1.0 / ((coarse_mass * coarse_mass) * m00 + (2.0 * coarse_mass * grow) * m01r + (grow * grow) * m11)
        ar = (coarse_mass * m00 + grow * m01r) * bottom
        ai = (-grow * m01i) * bottom
        for i, (cr, ci) in enumerate(coef):
            answer[i] = (answer[i][0] + (ar * cr - ai * ci), answer[i][1] + (ar * ci + ai * cr))
        kr, ki = 1.0 - coarse_mass * ar, -coarse_mass * ai
        dr, di = -grow * ar, -grow * ai
        kk, dd = kr * kr + ki * ki, dr * dr + di * di
        wr, wi = kr * dr + ki * di, kr * di - ki * dr
        fresh = [[None] * size for _ in range(size)]
        for m in range(size - 1 - step):
            for n in range(m, size - 1 - step):
                hr, hi = moments[m][n]
                nr, ni = moments[m][n + 1]
                fr, fi = moments[m + 1][n + 1]
                if m == n:
                    fresh[m][n] = ((kk * hr + dd * fr) + 2.0 * (wr * nr - wi * ni), none)
                else:
                    lr, li = moments[m + 1][n]
                    fresh[m][n] = ((kk * hr + dd * fr) + (wr * nr - wi * ni) + (wr * lr + wi * li),
                                   (kk * hi + dd * fi) + (wr * ni + wi * nr) + (wr * li - wi * lr))
        moments = fresh
        grown = [(kr * cr - ki * ci, kr * ci + ki * cr) for cr, ci in coef] + [(none, none)]
        for i, (cr, ci) in enumerate(coef):
            gr, gi = grown[i + 1]
            grown[i + 1] = (gr + (dr * cr - di * ci), gi + (dr * ci + di * cr))
        coef = grown

    alpha, beta = PAIRS[0]
    for t in range(2):
        for s in range(4):
            parts = [[fields[4, ri, s, :, t], fields[9, ri, s, :, t], u[ri, s, :, t]] for ri in range(2)]
            for i in range(CITERS):
                cr, ci = answer[i][0][None], answer[i][1][None]
                for part, at in ((0, 5 + i), (1, 10 + i), (2, i)):
                    fr, fi = fields[at, 0, s, :, t], fields[at, 1, s, :, t]
                    re, im = cr * fr - ci * fi, cr * fi + ci * fr
                    parts[0][part] = plus(parts[0][part], re, 1.0 if part == 2 else -1.0)
                    parts[1][part] = plus(parts[1][part], im, 1.0 if part == 2 else -1.0)
            for ri in range(2):
                left, through, result = parts[ri]
                step = START * left
                left = left - START * through
                after = alpha * step + beta * left
                r[ri, s, :, t] = left
                p[ri, s, :, t] = after
                u[ri, s, :, t] = result + step + after

    found = none
    for i in range(CITERS):
        found = found + (answer[i][0] * vectors[i] - answer[i][1] * turned[i])
    for ri in range(2):
        part = found if ri == 0 else pltpu.roll(found, 96, 1)
        for c in range(4):
            for y in range(2):
                at = 8 * ri + 2 * c + y
                e_out[at:at + 1, :] = part[4 * y + c:4 * y + c + 1, 0:24]

    lax.fori_loop(DEG + 2, 2 * DEG, second_half, 0)
    for t in range(2):
        for x in range(4):
            u_out[:, 4 * x + 2 * t:4 * x + 2 * t + 2, :] = u[:, :, :, t, 2 * x:2 * x + 2, :].reshape(24, 2, 128)


def pinned(x):
    return pltpu.with_memory_space_constraint(x, pltpu.HBM)


def body(sizes, source_field, gauge_links, null_vectors, coarse_links):
    hbm = pl.BlockSpec(memory_space=pltpu.HBM)
    vmem = pl.BlockSpec(memory_space=pltpu.VMEM)
    keys, far = reach(sizes)
    most_rows = 64 * (len(keys) + len(keys) % 2)
    half = (10, 2, 2, 3, 2, 8, 128)
    full = (2, 4, 3, 2, 8, 128)
    most = max(sizes["ta"], sizes["grp"] * sizes["gz"]) - 1
    arguments = [(24, 16, 128), (72, 16, 8), (24, 4, 2, 2, 192), (480, 24)]
    shapes = arguments + [full, full, (14,) + full, (10,) + full, (4, 2, 3, 3, 2, 8, 128), (72, 2, 8, 8),
                          half, half, half, half, (10, 2, 2, 3, 8, 128), (10, 2, 2, 3, 8, 128),
                          (10, 2, 6, 8, 128), (10, 2, 2, 2, 3, 8, 128), (10, 2, 2, 2, 3, 8, 128),
                          (11, 2, 6, 8, 128), (11, 2, 2, 2, 3, 8, 128), (11, 2, 2, 2, 3, 8, 128),
                          (24, 2, 8, 192), (2, 384, 192), (2, 384, 192), (3, 96, 24), (128, 384), (256, 128), (512, 128), (8, 24, 128), (6, 8, 24, 128),
                          (most_rows, 128), (2, 512, 128), (2, most_rows, 128), (CITERS + 1, 8, 128), (2, len(far), 8, 128), (2, 1, 128), (2, most, 1, 128)]
    split = ((2, 384, 192), (2, 512, 128), (2, most_rows, 128))
    sems = [(4,), (10, 6), (11, 6), (3,), (3,), (6, 2), (6, 2), (2, len(far)), (2, len(far)), (2, most), (2, most)]
    out, found = pl.pallas_call(
        functools.partial(kernel, sizes),
        out_shape=(jax.ShapeDtypeStruct((24, 16, 128), F32), jax.ShapeDtypeStruct((16, 24), F32)),
        in_specs=[hbm] * 4,
        out_specs=(vmem, vmem),
        scratch_shapes=[pltpu.VMEM(shape, jnp.bfloat16 if shape in split else F32) for shape in shapes]
        + [pltpu.SemaphoreType.DMA(shape) for shape in sems],
        compiler_params=pltpu.CompilerParams(
            collective_id=0, has_side_effects=True, vmem_limit_bytes=32 * 1024 * 1024),
    )(
        pinned(source_field.reshape(arguments[0])),
        pinned(gauge_links.reshape(arguments[1])),
        pinned(null_vectors.reshape(arguments[2])),
        pinned(coarse_links.transpose(0, 1, 2, 4, 5, 6, 7, 3).reshape(arguments[3])),
    )
    found = found.reshape(2, 4, 2, 24).transpose(0, 3, 1, 2)
    return out.reshape(source_field.shape), found.reshape(2, 24, 4, 1, 1, 1, 2)


def solution(mesh):
    sizes = {axis: mesh.shape[axis] for axis in ("grp", "ta", "gz")}
    placed = (
        P(None, None, None, "grp", "ta", "gz", None),
        P(None, None, None, None, "grp", "ta", "gz", None),
        P(None, None, None, "grp", "ta", "gz", None),
        P(None, None, None, None, "grp", "ta", "gz", None),
    )
    return jax.shard_map(
        functools.partial(body, sizes),
        mesh=mesh,
        in_specs=placed,
        out_specs=(
            P(None, None, None, "grp", "ta", "gz", None),
            P(None, None, None, "grp", "ta", "gz", None),
        ),
        check_vma=False,
    )
```

```python
import functools

import jax
import jax.numpy as jnp
from jax import lax
from jax.experimental import pallas as pl
from jax.experimental.pallas import tpu as pltpu
from jax.sharding import PartitionSpec as P

MESH = pl.DeviceIdType.MESH
F32 = jnp.float32

site_mass = 2.0
hop_kappa = 0.1
fifth_hop = 0.4
wall_mass = 0.1
cheb_lower = 0.6
cheb_upper = 3.4
coarse_mass = 3.0
coarse_fifth = 0.3
basis_scale = 0.125
DEG = 4
CITERS = 4
gamma_table = (
    ((3, 0.0, 1.0), (2, 0.0, 1.0)),
    ((3, -1.0, 0.0), (2, 1.0, 0.0)),
    ((2, 0.0, 1.0), (3, 0.0, -1.0)),
    ((2, 1.0, 0.0), (3, 1.0, 0.0)),
)
AXES = ((0, "grp"), (2, "gz"), (3, "ta"))
COARSE_DIRS = (1, 3, 4)


def cheb_coefficients():
    centre = 0.5 * (cheb_upper + cheb_lower)
    half_width = 0.5 * (cheb_upper - cheb_lower)
    spread_ratio = centre / half_width
    ratio_now = 1.0 / spread_ratio
    pairs = []
    for _ in range(DEG - 1):
        ratio_next = 1.0 / (2.0 * spread_ratio - ratio_now)
        pairs.append((ratio_next * ratio_now, 2.0 * ratio_next / half_width))
        ratio_now = ratio_next
    return 1.0 / centre, pairs


START, PAIRS = cheb_coefficients()
ALPHA = [pair[0] for pair in PAIRS] + [0.0, 0.0] + [pair[0] for pair in PAIRS]
BETA = [pair[1] for pair in PAIRS] + [0.0, START] + [pair[1] for pair in PAIRS]


def plus(a, b, sign):
    return a + b if sign > 0 else a - b


def project(v, mu, f):
    real, imag = [], []
    for a in range(2):
        b, gr, gi = gamma_table[mu][a]
        if gr != 0.0:
            real.append(plus(v[0][a], v[0][b], f * gr))
            imag.append(plus(v[1][a], v[1][b], f * gr))
        else:
            real.append(plus(v[0][a], v[1][b], -f * gi))
            imag.append(plus(v[1][a], v[0][b], f * gi))
    return [real, imag]


def rebuild(acc, h, mu, f):
    for a in range(2):
        b, gr, gi = gamma_table[mu][a]
        acc[0][a] = acc[0][a] + h[0][a]
        acc[1][a] = acc[1][a] + h[1][a]
        if gr != 0.0:
            acc[0][b] = plus(acc[0][b], h[0][a], f * gr)
            acc[1][b] = plus(acc[1][b], h[1][a], f * gr)
        else:
            acc[0][b] = plus(acc[0][b], h[1][a], f * gi)
            acc[1][b] = plus(acc[1][b], h[0][a], -f * gi)


def link_mul(links, mu, t, h, dagger):
    out = [[None, None], [None, None]]
    for col in range(3):
        if dagger:
            lr, li = links[mu, 0, col, :, t], links[mu, 1, col, :, t]
        else:
            lr, li = links[mu, 0, :, col, t], links[mu, 1, :, col, t]
        for a in range(2):
            hr, hi = h[0][a][col][None], h[1][a][col][None]
            if dagger:
                re, im = lr * hr + li * hi, lr * hi - li * hr
            else:
                re, im = lr * hr - li * hi, lr * hi + li * hr
            out[0][a] = re if col == 0 else out[0][a] + re
            out[1][a] = im if col == 0 else out[1][a] + im
    return out


def each(fn, h):
    return [[fn(h[ri][a]) for a in range(2)] for ri in range(2)]


def dot(a, b, dims=((1,), (0,))):
    return lax.dot_general(
        a, b, (dims, ((), ())), precision=lax.Precision.HIGHEST, preferred_element_type=F32
    )


def halves(a):
    high = a.astype(jnp.bfloat16)
    return high, (a - high.astype(F32)).astype(jnp.bfloat16)


def dot_halves(a, b):
    return sum(jnp.dot(a[i], b[j], preferred_element_type=F32) for i, j in ((1, 0), (0, 1), (0, 0)))


def pick(ones, b):
    ones = ones.astype(jnp.bfloat16)
    high, low = halves(b)
    return jnp.dot(ones, low, preferred_element_type=F32) + jnp.dot(ones, high, preferred_element_type=F32)


def rows_times(a, weights):
    high = a.astype(jnp.bfloat16).astype(F32)
    both = jnp.concatenate([high, a - high], axis=0).astype(jnp.bfloat16)
    out = jnp.dot(both, weights[1], preferred_element_type=F32) + jnp.dot(both, weights[0], preferred_element_type=F32)
    return out[0:8] + out[8:16]


def iota(shape, dim):
    return lax.broadcasted_iota(jnp.int32, shape, dim)


def wrap(sizes, disp):
    return tuple(by % sizes[axis] for by, (_, axis) in zip(disp, AXES))


STENCIL = (((0, 0, 0), 0), ((0, 0, 0), 1), ((1, 0, 0), 0), ((-1, 0, 0), 0),
           ((0, 1, 0), 0), ((0, -1, 0), 0), ((0, 0, 1), 0), ((0, 0, -1), 0))
CHUNKS = ((0, 4), (4, 8))


def reach(sizes):
    keys = []
    for first, flip in STENCIL:
        for second, again in STENCIL:
            key = (wrap(sizes, [i + j for i, j in zip(first, second)]), flip ^ again)
            if key not in keys:
                keys.append(key)
    far = []
    for disp, _ in keys:
        if any(disp) and disp not in far:
            far.append(disp)
    return keys, far


def kernel(sizes, src_in, gauge_in, null_in, coarse_in, u_out, e_out, src, gauge, null, coarse, p, u, fields, acc, links, g8,
           hx, qx, hz, qz, ht, qt, sendx, sendz, sendt, recvx, recvz, recvt, nv, nvs, nvt, low, ff, fb, wide, rows24, wrecv,
           twice, wides, twices, basis, crecv, ar_send, ar_recv, isem, fsend, frecv, lsend, lrecv, wsend, wrsem, csend, crsem, asend, arsem):
    keys, far = reach(sizes)
    me = {axis: lax.axis_index(axis) for axis in ("grp", "ta", "gz")}
    plane = sizes["grp"] * sizes["gz"]
    spot = me["grp"] * sizes["gz"] + me["gz"]

    def moved(axis, by):
        return lax.rem(me[axis] + (by + sizes[axis]), sizes[axis])

    def in_plane(by):
        other = lax.rem(spot + by, plane)
        return {"grp": lax.div(other, sizes["gz"]), "gz": lax.rem(other, sizes["gz"])}

    groups = ([in_plane(by) for by in range(1, plane)], [{"ta": moved("ta", by)} for by in range(1, sizes["ta"])])

    def at(disp):
        return {axis: moved(axis, by) for by, (_, axis) in zip(disp, AXES)}

    def back(disp):
        return at(wrap(sizes, [-by for by in disp]))

    barrier = pltpu.get_barrier_semaphore()
    partners = [at(disp) for disp, _ in STENCIL if any(disp)]
    for partner in partners:
        pl.semaphore_signal(barrier, inc=1, device_id=partner, device_id_type=MESH)

    loads = [pltpu.make_async_copy(a, b, isem.at[i]) for i, (a, b) in enumerate(
        ((gauge_in, gauge), (src_in, src), (coarse_in, coarse), (null_in, null)))]
    for load in loads:
        load.start()

    r = fields.at[4]

    loads[0].wait()
    for t in range(2):
        for x in range(4):
            g8[:, t, 2 * x:2 * x + 2, :] = gauge[:, 4 * x + 2 * t:4 * x + 2 * t + 2, :]
    spread_y = jnp.where((iota((8, 128), 1) & 7) == iota((8, 128), 0), 1.0, 0.0).astype(F32)
    tiled = dot(g8[...].reshape(72 * 16, 8), spread_y) * (-hop_kappa)
    links[...] = tiled.reshape(4, 2, 3, 3, 2, 8, 128)
    loads[1].wait()
    for t in range(2):
        for x in range(4):
            rows = src[:, 4 * x + 2 * t:4 * x + 2 * t + 2, :].reshape(2, 4, 3, 2, 128)
            r[:, :, :, t, 2 * x:2 * x + 2, :] = rows
            p[:, :, :, t, 2 * x:2 * x + 2, :] = rows * START
            u[:, :, :, t, 2 * x:2 * x + 2, :] = rows * START
    loads[2].wait()

    pl.semaphore_wait(barrier, len(partners))

    def low_copy(d):
        return pltpu.make_async_remote_copy(
            src_ref=coarse.at[pl.ds(COARSE_DIRS[d] * 96, 96)], dst_ref=low.at[d], send_sem=lsend.at[d],
            recv_sem=lrecv.at[d], device_id={AXES[d][1]: moved(AXES[d][1], 1)}, device_id_type=MESH)

    row8 = iota((8, 128), 0)
    lane8 = iota((8, 128), 1)

    def face_copy(d, side, ls, rs):
        out, into = ((sendx, recvx), (sendz, recvz), (sendt, recvt))[d]
        axis = AXES[d][1]
        return pltpu.make_async_remote_copy(
            src_ref=out.at[ls, side], dst_ref=into.at[rs, side], send_sem=fsend.at[ls, 2 * d + side],
            recv_sem=frecv.at[rs, 2 * d + side], device_id={axis: moved(axis, 2 * side - 1)},
            device_id_type=MESH)

    def field(ref, t):
        return [[ref[ri, s, :, t] for s in range(4)] for ri in range(2)]

    def keep(ref, t, total):
        for ri in range(2):
            for s in range(4):
                ref[ri, s, :, t] = total[ri][s]

    def build_null():
        for d in range(3):
            low_copy(d).start()
        loads[3].wait()
        for t in range(2):
            for x in range(4):
                nv[:, t, 2 * x:2 * x + 2, :] = null[:, x, t]

    def build_null_transposed():
        for ri in range(2):
            half = nv[12 * ri:12 * ri + 12].reshape(192, 192)
            for part, value in enumerate(halves(half)):
                nvs[part, 192 * ri:192 * ri + 192, :] = value
            for part, value in enumerate(halves(half.T)):
                nvt[part, 192 * ri:192 * ri + 192, :] = value

    def build_coarse():
        for d in range(3):
            low_copy(d).wait()
        ff[...] = jnp.zeros_like(ff)
        fb[...] = jnp.zeros_like(fb)
        zero = jnp.zeros((24, 104), F32)

        def piece(ref, base, y):
            return jnp.concatenate([ref[pl.ds(base + y, 24, stride=2), :] * basis_scale, zero], axis=1)

        def placed(value, at):
            return value if at == 0 else pltpu.roll(value, at, 1)

        for y in range(2):
            blocks = []
            for direction in (0, 1, 3, 4, 2):
                blocks.append([piece(coarse, direction * 96 + ri * 48, y) for ri in range(2)])
            for ro in range(2):
                for tile in range(3):
                    total = None
                    for j in range(2):
                        if 2 * tile + j > 4:
                            continue
                        mr, mi = blocks[2 * tile + j]
                        first, second = (mr, -mi) if ro == 0 else (mi, mr)
                        part = placed(first, 64 * j) + placed(second, 64 * j + 32)
                        total = part if total is None else total + part
                    ff[64 * y + 32 * ro:64 * y + 32 * ro + 24, 128 * tile:128 * tile + 128] = total
        for block in range(4):
            parts = []
            for y in range(2):
                if block == 0:
                    parts.append([piece(coarse, 2 * 96 + ri * 48, 1 - y) for ri in range(2)])
                else:
                    parts.append([piece(low.at[block - 1], ri * 48, y) for ri in range(2)])
            for ri in range(2):
                total = None
                for y in range(2):
                    mr, mi = parts[y]
                    first, second = (mr, -mi) if ri == 0 else (mi, mr)
                    part = placed(first, 64 * y) + placed(second, 64 * y + 32)
                    total = part if total is None else total + part
                fb[64 * block + 32 * ri:64 * block + 32 * ri + 24, :] = total
        flat = ff[...].T
        order = (flat[0:64], flat[256:320] + fb[0:64], flat[64:128], fb[64:128], flat[128:192], fb[128:192],
                 flat[192:256], fb[192:256])
        for block, rows in enumerate(order):
            wide[64 * block:64 * block + 64, :] = rows
            rows24[block] = rows[0:24]
            for part, value in enumerate(halves(rows)):
                wides[part, 64 * block:64 * block + 64, :] = value

    def row_copy(block, chunk):
        first, last = CHUNKS[chunk]
        return pltpu.make_async_remote_copy(
            src_ref=rows24.at[first:last], dst_ref=wrecv.at[block - 2, first:last], send_sem=wsend.at[block - 2, chunk],
            recv_sem=wrsem.at[block - 2, chunk], device_id=back(STENCIL[block][0]), device_id_type=MESH)

    def send_rows(chunk):
        def send():
            for block in range(2, 8):
                row_copy(block, chunk).start()

        return send

    def build_coarse_and_send():
        build_coarse()
        send_rows(0)()

    def build_null_and_send():
        build_null_transposed()

    def build_twice():
        twice[...] = jnp.zeros_like(twice)
        for block, (disp, flip) in enumerate(STENCIL):
            if block >= 2:
                for chunk in range(len(CHUNKS)):
                    row_copy(block, chunk).wait()
            mine = wide[64 * block:64 * block + 64, :]
            left = iota((64, 128), 1) < 64
            upper, lower = jnp.where(left, mine, 0.0), jnp.where(left, 0.0, mine)
            weights = jnp.concatenate([lower, upper] if flip else [upper, lower], axis=0)
            theirs = rows24[...] if block < 2 else wrecv[block - 2]
            product = dot_halves(halves(theirs.reshape(8 * 24, 128)), halves(weights))
            real_lane = (iota((8 * 24, 128), 1) & 32) == 0
            turned = jnp.where(real_lane, -pltpu.roll(product, 96, 1), pltpu.roll(product, 32, 1))
            for other, (further, again) in enumerate(STENCIL):
                key = (wrap(sizes, [i + j for i, j in zip(disp, further)]), flip ^ again)
                base = 64 * keys.index(key)
                for ri, part in ((0, product), (1, turned)):
                    twice[base + 32 * ri:base + 32 * ri + 24, :] += part[24 * other:24 * other + 24]
        for part, value in enumerate(halves(twice[...])):
            twices[part] = value

    even = (iota((3, 8, 128), 1) & 1) == 0

    def start(f, ls, rs):
        v = field(f, 0)
        down = project(v, 3, -1.0)
        own_up = link_mul(links, 3, 0, project(v, 3, 1.0), True)
        v = field(f, 1)
        own_down = project(v, 3, -1.0)
        up = link_mul(links, 3, 1, project(v, 3, 1.0), True)
        for ri in range(2):
            for a in range(2):
                sendt[ls, 0, ri, a] = down[ri][a]
                sendt[ls, 1, ri, a] = up[ri][a]
                ht[ls, ri, a] = own_down[ri][a]
                qt[ls, ri, a] = own_up[ri][a]
        face_copy(2, 0, ls, rs).start()
        face_copy(2, 1, ls, rs).start()
        for t in range(2):
            v = field(f, t)
            down = project(v, 0, -1.0)
            up = link_mul(links, 0, t, project(v, 0, 1.0), True)
            for ri in range(2):
                for a in range(2):
                    j = 2 * (2 * a + t)
                    sendx[ls, 0, 3 * ri:3 * ri + 3, j:j + 2, :] = down[ri][a][:, 0:2]
                    sendx[ls, 1, 3 * ri:3 * ri + 3, j:j + 2, :] = up[ri][a][:, 6:8]
                    hx[ls, ri, a, :, t] = pltpu.roll(down[ri][a], 6, 1)
                    qx[ls, ri, a, :, t] = pltpu.roll(up[ri][a], 2, 1)
        face_copy(0, 0, ls, rs).start()
        face_copy(0, 1, ls, rs).start()
        downs, ups = [], []
        for t in range(2):
            v = field(f, t)
            downs.append(project(v, 2, -1.0))
            ups.append(link_mul(links, 2, t, project(v, 2, 1.0), True))
        for ri in range(2):
            for a in range(2):
                for t in range(2):
                    hz[ls, ri, a, :, t] = pltpu.roll(downs[t][ri][a], 7, 1)
                    qz[ls, ri, a, :, t] = pltpu.roll(ups[t][ri][a], 1, 1)
                sendz[ls, 0, ri, a] = jnp.where(even, downs[0][ri][a], pltpu.roll(downs[1][ri][a], 1, 1))
                sendz[ls, 1, ri, a] = jnp.where(even, pltpu.roll(ups[0][ri][a], 7, 1), ups[1][ri][a])
        face_copy(1, 0, ls, rs).start()
        face_copy(1, 1, ls, rs).start()

        lane = iota((3, 8, 128), 2)
        ypos = lane & 7
        below = jnp.where(lane < 8, fifth_hop * wall_mass, -fifth_hop).astype(F32)
        above = jnp.where(lane >= 120, fifth_hop * wall_mass, -fifth_hop).astype(F32)
        for t in range(2):
            v = field(f, t)
            total = [[None] * 4, [None] * 4]
            for ri in range(2):
                for s in range(4):
                    if s < 2:
                        side = below * pltpu.roll(v[ri][s], 8, 2)
                    else:
                        side = above * pltpu.roll(v[ri][s], 120, 2)
                    total[ri][s] = site_mass * v[ri][s] + side
            h = each(lambda w: jnp.where(ypos == 7, pltpu.roll(w, 7, 2), pltpu.roll(w, 127, 2)), project(v, 1, -1.0))
            rebuild(total, link_mul(links, 1, t, h, False), 1, -1.0)
            h = link_mul(links, 1, t, project(v, 1, 1.0), True)
            h = each(lambda w: jnp.where(ypos == 0, pltpu.roll(w, 121, 2), pltpu.roll(w, 1, 2)), h)
            rebuild(total, h, 1, 1.0)
            if t == 0:
                h = [[ht[ls, ri, a] for a in range(2)] for ri in range(2)]
                rebuild(total, link_mul(links, 3, 0, h, False), 3, -1.0)
            else:
                rebuild(total, [[qt[ls, ri, a] for a in range(2)] for ri in range(2)], 3, 1.0)
            keep(acc.at[ls], t, total)

    def finish(ls, rs, emit):
        face_copy(1, 0, ls, rs).wait()
        face_copy(1, 1, ls, rs).wait()
        for t in range(2):
            total = field(acc.at[ls], t)
            h = [[None, None], [None, None]]
            q = [[None, None], [None, None]]
            for ri in range(2):
                for a in range(2):
                    came, back = recvz[rs, 0, ri, a], recvz[rs, 1, ri, a]
                    if t == 0:
                        came = pltpu.roll(came, 1, 1)
                    else:
                        back = pltpu.roll(back, 7, 1)
                    h[ri][a] = jnp.where(even, hz[ls, ri, a, :, t], came)
                    q[ri][a] = jnp.where(even, back, qz[ls, ri, a, :, t])
            rebuild(total, link_mul(links, 2, t, h, False), 2, -1.0)
            rebuild(total, q, 2, 1.0)
            keep(acc.at[ls], t, total)
        face_copy(0, 0, ls, rs).wait()
        face_copy(0, 1, ls, rs).wait()
        for ri in range(2):
            for a in range(2):
                for t in range(2):
                    j = 2 * (2 * a + t)
                    hx[ls, ri, a, :, t, 6:8, :] = recvx[rs, 0, 3 * ri:3 * ri + 3, j:j + 2, :]
                    qx[ls, ri, a, :, t, 0:2, :] = recvx[rs, 1, 3 * ri:3 * ri + 3, j:j + 2, :]
        for t in range(2):
            total = field(acc.at[ls], t)
            h = [[hx[ls, ri, a, :, t] for a in range(2)] for ri in range(2)]
            rebuild(total, link_mul(links, 0, t, h, False), 0, -1.0)
            rebuild(total, [[qx[ls, ri, a, :, t] for a in range(2)] for ri in range(2)], 0, 1.0)
            keep(acc.at[ls], t, total)
        face_copy(2, 0, ls, rs).wait()
        face_copy(2, 1, ls, rs).wait()
        for t in range(2):
            total = field(acc.at[ls], t)
            if t == 0:
                rebuild(total, [[recvt[rs, 1, ri, a] for a in range(2)] for ri in range(2)], 3, 1.0)
            else:
                h = [[recvt[rs, 0, ri, a] for a in range(2)] for ri in range(2)]
                rebuild(total, link_mul(links, 3, 1, h, False), 3, -1.0)
            emit(t, total)

    def advance(k):
        alpha = jnp.float32(ALPHA[0])
        beta = jnp.float32(BETA[0])
        for at in range(1, 2 * DEG):
            alpha = jnp.where(k == at, jnp.float32(ALPHA[at]), alpha)
            beta = jnp.where(k == at, jnp.float32(BETA[at]), beta)

        def emit(t, total):
            for ri in range(2):
                for s in range(4):
                    left = r[ri, s, :, t] - total[ri][s]
                    step = alpha * p[ri, s, :, t] + beta * left
                    r[ri, s, :, t] = left
                    p[ri, s, :, t] = step
                    u[ri, s, :, t] = u[ri, s, :, t] + step

        return emit

    def round_of(k, hooks):
        slot = lax.rem(k, 2)
        start(p, 0, slot)
        for at, hook in hooks:
            pl.when(k == at)(hook)
        finish(0, slot, advance(k))

    def first_half(k, carry):
        round_of(k, ((0, build_null), (1, build_null_and_send), (2, build_coarse_and_send), (3, send_rows(1))))
        return carry

    lax.fori_loop(0, DEG, first_half, 0)

    diagonal = (iota((192, 256), 0) & 7) == (iota((192, 256), 1) & 7)
    selector = jnp.where(
        ((lane8 >> 5) == (row8 & 3)) & (((lane8 & 7) >> 2) == (row8 >> 2)), 1.0, 0.0).astype(F32)
    fold = jnp.where((iota((32, 192), 1) >> 3) == iota((32, 192), 0), 1.0, 0.0).astype(F32)
    unfold = jnp.where((iota((192, 32), 0) >> 3) == iota((192, 32), 1), 1.0, 0.0).astype(F32)
    both = jnp.concatenate([r[0].reshape(192, 128), r[1].reshape(192, 128)], axis=1)
    prod = dot_halves((nvt[0], nvt[1]), halves(both))
    real = prod[0:192, 0:128] + prod[192:384, 128:256]
    imag = prod[0:192, 128:256] - prod[192:384, 0:128]
    kept = jnp.where(diagonal, jnp.concatenate([real, imag], axis=1), 0.0)
    summed = pick(fold, kept)
    stacked = jnp.concatenate([summed[:, 0:128], summed[:, 128:256]] * 2, axis=0)
    basis[0] = dot(selector, stacked, ((1,), (1,)))

    def coarse_copies(step):
        return [pltpu.make_async_remote_copy(
            src_ref=basis.at[2 * step], dst_ref=crecv.at[step, i], send_sem=csend.at[step, i],
            recv_sem=crsem.at[step, i], device_id=back(disp), device_id_type=MESH)
            for i, disp in enumerate(far)]

    low_half = lane8 < 64

    def prolong(step):
        spread = dot(basis[step], selector, ((0,), (0,)))
        paired = jnp.concatenate([spread[0:32], spread[32:64]], axis=1)
        weights = jnp.where(diagonal, pick(unfold, paired), 0.0)
        prod = dot_halves((nvs[0], nvs[1]), halves(weights))
        fields[step, 0] = (prod[0:192, 0:128] - prod[192:384, 128:256]).reshape(4, 3, 2, 8, 128)
        fields[step, 1] = (prod[0:192, 128:256] + prod[192:384, 0:128]).reshape(4, 3, 2, 8, 128)

    def begin(f):
        start(fields.at[f], 1 + f, 2 + f)

    def end(f):
        finish(1 + f, 2 + f, lambda t, total: keep(fields.at[5 + f], t, total))

    def across(own):
        layer = row8 & 3
        from_below = jnp.where(layer == 0, -wall_mass * pltpu.roll(own, 5, 0), pltpu.roll(own, 1, 0))
        from_above = jnp.where(layer == 3, -wall_mass * pltpu.roll(own, 3, 0), pltpu.roll(own, 7, 0))
        return (-coarse_fifth * basis_scale) * (from_below + from_above)

    def gathered(step, wanted):
        own = basis[2 * step]
        parts = []
        for disp, flip in wanted:
            disp = wrap(sizes, disp)
            part = crecv[step, far.index(disp)] if any(disp) else own
            parts.append(pltpu.roll(part, 4, 0) if flip else part)
        if len(parts) % 2:
            parts.append(own)
        return jnp.concatenate(
            [jnp.where(low_half, parts[i], parts[i + 1]) for i in range(0, len(parts), 2)], axis=1)

    def own_y(out):
        return jnp.where((row8 < 4) == low_half, out, pltpu.roll(out, 64, 1))

    def send_basis(step):
        for copy in coarse_copies(step):
            copy.start()

    def take_basis(step):
        for copy in coarse_copies(step):
            copy.wait()
        once = own_y(rows_times(gathered(step, STENCIL), (wides[0], wides[1])))
        shifted = across(basis[2 * step])
        basis[2 * step + 1] = once + shifted
        return 2.0 * once + shifted

    def take_second(step, first):
        again = own_y(rows_times(gathered(step, keys), (twices[0], twices[1])))
        basis[2 * step + 2] = again + across(first)

    send_basis(0)
    prolong(0)
    begin(0)
    begin(4)
    build_twice()
    take_second(0, take_basis(0))
    send_basis(1)

    def lift(f, carry):
        prolong(f)
        begin(f)
        return carry

    lax.fori_loop(1, 3, lift, 0)
    end(0)
    begin(5)
    take_second(1, take_basis(1))

    size = CITERS + 1
    vectors = [basis[i] for i in range(size)]
    sign = jnp.where((lane8 & 32) == 0, 1.0, -1.0).astype(F32)
    turned = [sign * pltpu.roll(v, 32, 1) for v in vectors]
    entries = [(i, j, 0) for i in range(size) for j in range(i, size)]
    entries += [(i, j, 1) for i in range(size) for j in range(i + 1, size)]
    none = jnp.zeros((8, 128), F32)
    products = [vectors[i] * (vectors[j] if part == 0 else turned[j]) for i, j, part in entries]
    products = jnp.stack(products + [none] * (32 - len(products)))
    rows = jnp.sum(jnp.where(low_half[None], products, 0.0), axis=1)
    padded = jnp.concatenate([rows, jnp.zeros((96, 128), F32)], axis=0)
    sums = dot(jnp.ones((8, 128), F32), padded, ((1,), (1,)))[0:1]

    def sum_copies(phase):
        return [pltpu.make_async_remote_copy(
            src_ref=ar_send.at[phase], dst_ref=ar_recv.at[phase, by], send_sem=asend.at[phase, by],
            recv_sem=arsem.at[phase, by], device_id=partner, device_id_type=MESH)
            for by, partner in enumerate(groups[phase])]

    def send_sums(phase, value):
        ar_send[phase] = value
        for copy in sum_copies(phase):
            copy.start()

    def take_sums(phase):
        parts = [ar_send[phase]]
        for by, copy in enumerate(sum_copies(phase)):
            copy.wait()
            parts.append(ar_recv[phase, by])
        while len(parts) > 1:
            parts = [parts[i] + parts[i + 1] if i + 1 < len(parts) else parts[i] for i in range(0, len(parts), 2)]
        return parts[0]

    def turn(f, carry):
        end(f)
        begin(5 + f)
        return carry

    def settle(f, carry):
        end(f)
        return carry

    send_sums(0, sums)
    prolong(3)
    begin(3)
    lax.fori_loop(1, 3, turn, 0)
    send_sums(1, take_sums(0))
    end(3)
    begin(8)
    end(4)
    end(5)
    lax.fori_loop(6, 9, settle, 0)
    sums = take_sums(1)

    moments = [[None] * size for _ in range(size)]
    for number, (i, j, part) in enumerate(entries):
        value = jnp.broadcast_to(sums[:, number:number + 1], (8, 128))
        moments[i][j] = (value, none) if part == 0 else (moments[i][j][0], value)
    one = jnp.ones((8, 128), F32)
    coef = [(one, none)]
    answer = [(none, none)] * CITERS
    grow = 1.0 / basis_scale
    for step in range(CITERS):
        m00, m11 = moments[0][0][0], moments[1][1][0]
        m01r, m01i = moments[0][1]
        bottom = 1.0 / ((coarse_mass * coarse_mass) * m00 + (2.0 * coarse_mass * grow) * m01r + (grow * grow) * m11)
        ar = (coarse_mass * m00 + grow * m01r) * bottom
        ai = (-grow * m01i) * bottom
        for i, (cr, ci) in enumerate(coef):
            answer[i] = (answer[i][0] + (ar * cr - ai * ci), answer[i][1] + (ar * ci + ai * cr))
        kr, ki = 1.0 - coarse_mass * ar, -coarse_mass * ai
        dr, di = -grow * ar, -grow * ai
        kk, dd = kr * kr + ki * ki, dr * dr + di * di
        wr, wi = kr * dr + ki * di, kr * di - ki * dr
        fresh = [[None] * size for _ in range(size)]
        for m in range(size - 1 - step):
            for n in range(m, size - 1 - step):
                hr, hi = moments[m][n]
                nr, ni = moments[m][n + 1]
                fr, fi = moments[m + 1][n + 1]
                if m == n:
                    fresh[m][n] = ((kk * hr + dd * fr) + 2.0 * (wr * nr - wi * ni), none)
                else:
                    lr, li = moments[m + 1][n]
                    fresh[m][n] = ((kk * hr + dd * fr) + (wr * nr - wi * ni) + (wr * lr + wi * li),
                                   (kk * hi + dd * fi) + (wr * ni + wi * nr) + (wr * li - wi * lr))
        moments = fresh
        grown = [(kr * cr - ki * ci, kr * ci + ki * cr) for cr, ci in coef] + [(none, none)]
        for i, (cr, ci) in enumerate(coef):
            gr, gi = grown[i + 1]
            grown[i + 1] = (gr + (dr * cr - di * ci), gi + (dr * ci + di * cr))
        coef = grown

    alpha, beta = PAIRS[0]
    for t in range(2):
        for s in range(4):
            parts = [[fields[4, ri, s, :, t], fields[9, ri, s, :, t], u[ri, s, :, t]] for ri in range(2)]
            for i in range(CITERS):
                cr, ci = answer[i][0][None], answer[i][1][None]
                for part, at in ((0, 5 + i), (1, 10 + i), (2, i)):
                    fr, fi = fields[at, 0, s, :, t], fields[at, 1, s, :, t]
                    re, im = cr * fr - ci * fi, cr * fi + ci * fr
                    parts[0][part] = plus(parts[0][part], re, 1.0 if part == 2 else -1.0)
                    parts[1][part] = plus(parts[1][part], im, 1.0 if part == 2 else -1.0)
            for ri in range(2):
                left, through, result = parts[ri]
                step = START * left
                left = left - START * through
                after = alpha * step + beta * left
                r[ri, s, :, t] = left
                p[ri, s, :, t] = after
                u[ri, s, :, t] = result + step + after

    def write_found():
        found = none
        for i in range(CITERS):
            found = found + (answer[i][0] * vectors[i] - answer[i][1] * turned[i])
        for ri in range(2):
            part = found if ri == 0 else pltpu.roll(found, 96, 1)
            for c in range(4):
                for y in range(2):
                    row = 8 * ri + 2 * c + y
                    e_out[row:row + 1, :] = part[4 * y + c:4 * y + c + 1, 0:24]

    def last(t, total):
        for ri in range(2):
            for s in range(4):
                step = ALPHA[-1] * p[ri, s, :, t] + BETA[-1] * (r[ri, s, :, t] - total[ri][s])
                value = u[ri, s, :, t] + step
                at = 12 * ri + 3 * s
                for x in range(4):
                    u_out[at:at + 3, 4 * x + 2 * t:4 * x + 2 * t + 2, :] = value[:, 2 * x:2 * x + 2]

    start(p, 0, 0)
    write_found()
    finish(0, 0, advance(2 * DEG - 2))
    start(p, 0, 1)
    finish(0, 1, last)


def pinned(x):
    return pltpu.with_memory_space_constraint(x, pltpu.HBM)


def body(sizes, source_field, gauge_links, null_vectors, coarse_links):
    hbm = pl.BlockSpec(memory_space=pltpu.HBM)
    vmem = pl.BlockSpec(memory_space=pltpu.VMEM)
    keys, far = reach(sizes)
    most_rows = 64 * (len(keys) + len(keys) % 2)
    half = (10, 2, 2, 3, 2, 8, 128)
    full = (2, 4, 3, 2, 8, 128)
    most = max(sizes["ta"], sizes["grp"] * sizes["gz"]) - 1
    arguments = [(24, 16, 128), (72, 16, 8), (24, 4, 2, 2, 192), (480, 24)]
    shapes = arguments + [full, full, (14,) + full, (10,) + full, (4, 2, 3, 3, 2, 8, 128), (72, 2, 8, 8),
                          half, half, half, half, (10, 2, 2, 3, 8, 128), (10, 2, 2, 3, 8, 128),
                          (10, 2, 6, 8, 128), (10, 2, 2, 2, 3, 8, 128), (10, 2, 2, 2, 3, 8, 128),
                          (11, 2, 6, 8, 128), (11, 2, 2, 2, 3, 8, 128), (11, 2, 2, 2, 3, 8, 128),
                          (24, 2, 8, 192), (2, 384, 192), (2, 384, 192), (3, 96, 24), (128, 384), (256, 128), (512, 128), (8, 24, 128), (6, 8, 24, 128),
                          (most_rows, 128), (2, 512, 128), (2, most_rows, 128), (CITERS + 1, 8, 128), (2, len(far), 8, 128), (2, 1, 128), (2, most, 1, 128)]
    split = ((2, 384, 192), (2, 512, 128), (2, most_rows, 128))
    sems = [(4,), (10, 6), (11, 6), (3,), (3,), (6, 2), (6, 2), (2, len(far)), (2, len(far)), (2, most), (2, most)]
    out, found = pl.pallas_call(
        functools.partial(kernel, sizes),
        out_shape=(jax.ShapeDtypeStruct((24, 16, 128), F32), jax.ShapeDtypeStruct((16, 24), F32)),
        in_specs=[hbm] * 4,
        out_specs=(vmem, vmem),
        scratch_shapes=[pltpu.VMEM(shape, jnp.bfloat16 if shape in split else F32) for shape in shapes]
        + [pltpu.SemaphoreType.DMA(shape) for shape in sems],
        compiler_params=pltpu.CompilerParams(
            collective_id=0, has_side_effects=True, vmem_limit_bytes=32 * 1024 * 1024),
    )(
        pinned(source_field.reshape(arguments[0])),
        pinned(gauge_links.reshape(arguments[1])),
        pinned(null_vectors.reshape(arguments[2])),
        pinned(coarse_links.transpose(0, 1, 2, 4, 5, 6, 7, 3).reshape(arguments[3])),
    )
    found = found.reshape(2, 4, 2, 24).transpose(0, 3, 1, 2)
    return out.reshape(source_field.shape), found.reshape(2, 24, 4, 1, 1, 1, 2)


def solution(mesh):
    sizes = {axis: mesh.shape[axis] for axis in ("grp", "ta", "gz")}
    placed = (
        P(None, None, None, "grp", "ta", "gz", None),
        P(None, None, None, None, "grp", "ta", "gz", None),
        P(None, None, None, "grp", "ta", "gz", None),
        P(None, None, None, None, "grp", "ta", "gz", None),
    )
    return jax.shard_map(
        functools.partial(body, sizes),
        mesh=mesh,
        in_specs=placed,
        out_specs=(
            P(None, None, None, "grp", "ta", "gz", None),
            P(None, None, None, "grp", "ta", "gz", None),
        ),
        check_vma=False,
    )
```
